512 devices in a mesh: grp: 16 (over y, z_lo), dev: 32 (over z_hi, x, core).
Axes of the slice: x: 4, y: 4, z: 16 (z_hi: 4, z_lo: 4; z = z_hi * 4 + z_lo), core: 2. Of those that a mesh axis runs over, the one named last changes fastest.
Arguments:
- lhs_table: bfloat16 [65536, 400], P(('grp', 'dev')), may hold values from -0.29882812 to 0.29882812
- lhs_state: float32 [65536], P(('grp', 'dev')), may hold values from 0.01 to 1
- rhs_table: bfloat16 [65536, 400], P(('grp', 'dev')), may hold values from -0.29882812 to 0.29882812
- rhs_state: float32 [65536], P(('grp', 'dev')), may hold values from 0.01 to 1
- relations: float32 [2080, 400], P('dev'), may hold values from -1.8 to 1.8
- rel_state: float32 [2080], P('dev'), may hold values from 1e-05 to 0.1
- src_index: int32 [512, 2, 512], P(('grp', 'dev')), may hold values from 0 to 127
- dst_index: int32 [512, 2, 512], P(('grp', 'dev')), may hold values from 0 to 127
- rel_index: int32 [512, 2, 512], P(('grp', 'dev')), may hold values from 0 to 2079
- neg_index: int32 [512, 2, 512], P(('grp', 'dev')), may hold values from 0 to 127
- edge_count: int32 [512, 2], P(('grp', 'dev')), may hold values from 128 to 512, as said below
Outputs:
- lhs_out: bfloat16 [65536, 400], P(('grp', 'dev'))
- lhs_state_out: float32 [65536], P(('grp', 'dev'))
- rhs_out: bfloat16 [65536, 400], P(('grp', 'dev'))
- rhs_state_out: float32 [65536], P(('grp', 'dev'))
- relations_out: float32 [2080, 400], P('dev')
- rel_state_out: float32 [2080], P('dev')
The draws below stay inside these ranges and needn't reach their ends.
Inputs may be any that keep to these rules, and one draw needn't show every extreme that they name: Edges of a bucket are live in its first edge_count slots; at least a quarter of the slots are live and some bucket is full.
All inputs are finite; a program needn't handle non-finite values.
Results may differ from the reference program's by a relative error of at most 0.001.
The reference program's roundings to bfloat16 on the way count: a program that leaves them out, or rounds other values in their place, can miss the bound.
Values may be sent and summed in bfloat16 or wider, within the bound.
A program may use at most 64 MiB of HBM per device.

```python
import math
import jax
import jax.numpy as jnp
from jax import lax

D = 400
NR = 2080
E_P = 128
BLOCK = 512
NEG = 512
ROUNDS = 2
BUCKETS = 512
ENTITIES = 65536
N_GRP = 16
N_DEV = 32


def draw_edge_count(key, part):
    key = jax.random.fold_in(key, 11)
    counts = jax.random.randint(key, (N_GRP * N_DEV, ROUNDS), BLOCK // 4, BLOCK + 1)
    return counts.at[0, 0].set(BLOCK).astype(jnp.int32)


def touch_ends(entries, stream_key, least, largest):
    extent = entries.shape
    place = [jax.random.randint(jax.random.fold_in(stream_key, axis), (), 0, extent[axis]) for axis in range(len(extent))]
    entries = entries.at[tuple(place)].set(least)
    longest = extent.index(max(extent))
    place[longest] = (place[longest] + 1) % extent[longest]
    return entries.at[tuple(place)].set(largest)


def shard_levels(own_key, extent, cuts, low, high):
    loudness = 1.0
    for axis_at, blocks in cuts:
        draws = jax.random.uniform(jax.random.fold_in(jax.random.fold_in(own_key, 6), axis_at), (blocks,), jnp.float32, low / len(cuts), high / len(cuts))
        loudness = loudness * jnp.repeat(jnp.exp(draws), extent[axis_at] // blocks).reshape((-1,) + (1,) * (len(extent) - 1 - axis_at))
    return loudness


def setup_inputs(seed: int = 0) -> dict:
    streams_of = jax.random.split(jax.random.key(seed), 12)
    lhs_table = jnp.clip(jax.random.uniform(streams_of[0], (ENTITIES, D), jnp.float32, -0.29882812, 0.29882812) * shard_levels(streams_of[0], (ENTITIES, D), ((0, 512),), -0.4, 0.0), -0.29882812, 0.29882812).astype(jnp.bfloat16)
    lhs_state = jnp.clip(jnp.exp(math.log(1.0) - 4.6051702 * jax.random.uniform(streams_of[1], (ENTITIES,), jnp.float32) ** shard_levels(streams_of[1], (ENTITIES,), ((0, 512),), -0.2, 0.2)), 0.01, 1.0)
    rhs_table = jnp.clip(jax.random.uniform(streams_of[2], (ENTITIES, D), jnp.float32, -0.29882812, 0.29882812) * shard_levels(streams_of[2], (ENTITIES, D), ((0, 512),), -0.4, 0.0), -0.29882812, 0.29882812).astype(jnp.bfloat16)
    rhs_state = jnp.clip(jnp.exp(math.log(1.0) - 4.6051702 * jax.random.uniform(streams_of[3], (ENTITIES,), jnp.float32) ** shard_levels(streams_of[3], (ENTITIES,), ((0, 512),), -0.2, 0.2)), 0.01, 1.0)
    relations = jnp.clip(jax.random.uniform(streams_of[4], (NR, D), jnp.float32, -1.8, 1.8) * shard_levels(streams_of[4], (NR, D), ((0, 32),), -0.4, 0.0), -1.8, 1.8)
    rel_state = jnp.clip(jnp.exp(math.log(0.1) - 9.2103404 * jax.random.uniform(streams_of[5], (NR,), jnp.float32) ** shard_levels(streams_of[5], (NR,), ((0, 32),), -0.2, 0.2)), 9.999999747378752e-06, 0.1)
    src_index = touch_ends(jax.random.randint(streams_of[6], (BUCKETS, ROUNDS, BLOCK), 0, E_P), jax.random.fold_in(streams_of[6], 1), 0, E_P - 1).astype(jnp.int32)
    dst_index = touch_ends(jax.random.randint(streams_of[7], (BUCKETS, ROUNDS, BLOCK), 0, E_P), jax.random.fold_in(streams_of[7], 1), 0, E_P - 1).astype(jnp.int32)
    rel_index = touch_ends(jax.random.randint(streams_of[8], (BUCKETS, ROUNDS, BLOCK), 0, NR), jax.random.fold_in(streams_of[8], 1), 0, NR - 1).astype(jnp.int32)
    neg_index = touch_ends(jax.random.randint(streams_of[9], (BUCKETS, ROUNDS, NEG), 0, E_P), jax.random.fold_in(streams_of[9], 1), 0, E_P - 1).astype(jnp.int32)
    edge_count = draw_edge_count(jax.random.fold_in(streams_of[11], 71), 0)
    return {"lhs_table": lhs_table, "lhs_state": lhs_state, "rhs_table": rhs_table, "rhs_state": rhs_state, "relations": relations, "rel_state": rel_state, "src_index": src_index, "dst_index": dst_index, "rel_index": rel_index, "neg_index": neg_index, "edge_count": edge_count}


LEARN = 0.1
EPSILON = 1e-06

def row_adagrad(rows, state, grad):
    new_state = state + lax.optimization_barrier(jnp.mean(grad * grad, axis=-1))
    moved = rows.astype(jnp.float32) - LEARN * grad / (jnp.sqrt(new_state) + EPSILON)[:, None]
    return (moved.astype(jnp.bfloat16), new_state)

def train_round(lhs, lhs_st, rhs, rhs_st, table, source, target, kinds, negatives, count):
    parts_rows = lhs.shape[0]
    width = lhs.shape[1]
    half = width // 2
    slots = source.shape[0]
    live = (jnp.arange(slots, dtype=jnp.int32) < count).astype(jnp.float32)
    left = lhs[source].astype(jnp.float32)
    right = rhs[target]
    noise = rhs[negatives]
    oper = table[kinds].astype(jnp.float32)
    a_re, a_im = (left[:, :half], left[:, half:])
    r_re, r_im = (oper[:, :half], oper[:, half:])
    query = jnp.concatenate([a_re * r_re - a_im * r_im, a_re * r_im + a_im * r_re], axis=1)
    q_bf = query.astype(jnp.bfloat16)
    q_wide = q_bf.astype(jnp.float32)
    right_wide = right.astype(jnp.float32)
    pos = lax.optimization_barrier(jnp.sum(q_wide * right_wide, axis=1))
    neg = jnp.dot(q_bf, noise.T, preferred_element_type=jnp.float32)
    pos_exp = jnp.exp(pos)
    neg_exp = jnp.exp(neg)
    total = pos_exp + lax.optimization_barrier(jnp.sum(neg_exp, axis=1))
    w_pos = live * (pos_exp / total - 1.0)
    w_neg = (live[:, None] * neg_exp / total[:, None]).astype(jnp.bfloat16)
    dq = w_pos[:, None] * right_wide + jnp.dot(w_neg, noise, preferred_element_type=jnp.float32)
    grad_y = w_pos[:, None] * q_wide
    grad_n = lax.dot_general(w_neg, q_bf, (((0,), (0,)), ((), ())), preferred_element_type=jnp.float32)
    dq_re, dq_im = (dq[:, :half], dq[:, half:])
    grad_a = jnp.concatenate([dq_re * r_re + dq_im * r_im, dq_im * r_re - dq_re * r_im], axis=1)
    grad_r = jnp.concatenate([dq_re * a_re + dq_im * a_im, dq_im * a_re - dq_re * a_im], axis=1)
    lhs_grad = jax.ops.segment_sum(grad_a, source, parts_rows)
    rhs_grad = jax.ops.segment_sum(grad_y, target, parts_rows) + jax.ops.segment_sum(grad_n, negatives, parts_rows)
    rel_grad = jax.ops.segment_sum(grad_r, kinds, table.shape[0])
    lhs_new, lhs_st_new = row_adagrad(lhs, lhs_st, lhs_grad)
    rhs_new, rhs_st_new = row_adagrad(rhs, rhs_st, rhs_grad)
    return (lhs_new, lhs_st_new, rhs_new, rhs_st_new, rel_grad)

def all_buckets(lhs, lhs_st, rhs, rhs_st, table, source, target, kinds, negatives, count, accum):

    def step(carry, item):
        out = train_round(*item[:4], table, *item[4:])
        return (carry + out[4], out[:4])
    accum, outs = lax.scan(step, accum, (lhs, lhs_st, rhs, rhs_st, source, target, kinds, negatives, count))
    return (outs, accum)

def reference(lhs_table, lhs_state, rhs_table, rhs_state, relations, rel_state, src_index, dst_index, rel_index, neg_index, edge_count):
    parts = N_GRP * N_DEV
    table = relations.astype(jnp.bfloat16)
    lhs = lhs_table.reshape(parts, E_P, D)
    rhs = rhs_table.reshape(parts, E_P, D)
    lhs_st = lhs_state.reshape(parts, E_P)
    rhs_st = rhs_state.reshape(parts, E_P)
    accum = jnp.zeros((NR, D), jnp.float32)
    for turn in range(ROUNDS):
        if turn > 0:
            rhs = jnp.roll(rhs.reshape(N_GRP, N_DEV, E_P, D), 1, axis=1).reshape(parts, E_P, D)
            rhs_st = jnp.roll(rhs_st.reshape(N_GRP, N_DEV, E_P), 1, axis=1).reshape(parts, E_P)
        outs, accum = all_buckets(lhs, lhs_st, rhs, rhs_st, table, src_index[:, turn], dst_index[:, turn], rel_index[:, turn], neg_index[:, turn], edge_count[:, turn], accum)
        lhs, lhs_st, rhs, rhs_st = outs
    new_rel_state = rel_state + lax.optimization_barrier(jnp.mean(accum * accum, axis=1))
    new_relations = relations - LEARN * accum / (jnp.sqrt(new_rel_state) + EPSILON)[:, None]
    return (lhs.reshape(parts * E_P, D), lhs_st.reshape(parts * E_P), rhs.reshape(parts * E_P, D), rhs_st.reshape(parts * E_P), new_relations, new_rel_state)
```

```python
import functools

import jax
import jax.numpy as jnp
from jax import lax
from jax.experimental import pallas as pl
from jax.experimental.pallas import tpu as pltpu
from jax.sharding import PartitionSpec as P

LEARN = 0.1
EPSILON = 1e-06
MESH = pl.DeviceIdType.MESH
F32, BF16, I32 = jnp.float32, jnp.bfloat16, jnp.int32

D = 400
HALF = 200
WIDE = 512
OWN = 65
ROWS = 80
EP = 128
SLOTS = 512
LANE = 128


def flip(value, k):
    if k == 1:
        return value + 1 - 2 * (value % 2)
    if k == 3:
        return 3 - value
    return (value + 2) % 4


def dot(a, b, ca, cb):
    return lax.dot_general(a, b, (((ca,), (cb,)), ((), ())), preferred_element_type=F32)


def hot(index, first, count):
    rows = lax.broadcasted_iota(I32, (count, index.shape[1]), 0) + first
    return jnp.where(rows == index, 1.0, 0.0).astype(BF16)


def split(value):
    high = value.astype(BF16)
    return high, (value - high.astype(F32)).astype(BF16)


def adagrad(rows, state, grad):
    new_state = state + jnp.sum(grad * grad, axis=0, keepdims=True) / D
    moved = rows.astype(F32) - LEARN * grad / (jnp.sqrt(new_state) + EPSILON)
    return moved.astype(BF16), new_state


def kernel(
    lhs_ref, lst_ref, rhs_ref, rst_ref, rel_ref, relst_ref, src_ref, dst_ref, kind_ref, neg_ref, count_ref,
    lhs_out, lst_out, rhs_out, rst_out, rel_out, relst_out,
    table, hot_all, hot_mine, kinds, a_buf, rr_buf, q_buf, m_hi, m_lo, edges,
    rhs_send, rst_send, rhs_in, rst_in, part, x_in, y_in, x2_in, y2_in, z_out, z_in, low, full, stage2x, stage2y,
    send_sem, recv_sem,
):
    grp, dev = lax.axis_index("grp"), lax.axis_index("dev")
    y, zl = grp // 4, grp % 4
    zh, x, c = dev // 8, (dev // 2) % 4, dev % 2

    def place(x_=None, y_=None, zh_=None, zl_=None, c_=None):
        x_ = x if x_ is None else x_
        y_ = y if y_ is None else y_
        zh_ = zh if zh_ is None else zh_
        zl_ = zl if zl_ is None else zl_
        c_ = c if c_ is None else c_
        return (y_ * 4 + zl_, zh_ * 8 + x_ * 2 + c_)

    sibling = place(c_=1 - c)
    after = (grp, (dev + 1) % 32)
    before = (grp, (dev + 31) % 32)
    ks = (1, 3, 2)
    xs = {k: place(x_=flip(x, k)) for k in ks}
    ys = {k: place(y_=flip(y, k)) for k in ks}
    zhs = {k: place(zh_=flip(zh, k)) for k in ks}
    zls = {k: place(zl_=flip(zl, k)) for k in ks}

    barrier = pltpu.get_barrier_semaphore()
    greet = [sibling, before, *xs.values(), *ys.values(), *zhs.values(), *zls.values()]
    for other in greet:
        pl.semaphore_signal(barrier, inc=1, device_id=other, device_id_type=MESH)

    started = []

    def send(src, dst, target):
        i = len(started)
        copy = pltpu.make_async_remote_copy(
            src_ref=src, dst_ref=dst, send_sem=send_sem.at[i], recv_sem=recv_sem.at[i],
            device_id=target, device_id_type=MESH,
        )
        copy.start()
        started.append(copy)
        return copy

    def arrived(copies):
        for copy in copies:
            copy.wait_recv()

    def lane(value):
        return pl.ds(pl.multiple_of(value * LANE, LANE), LANE)

    table[zh, x, c] = jnp.zeros((ROWS, WIDE), BF16)
    table[zh, x, c, 0:OWN, 0:D] = rel_ref[...].astype(BF16)
    kinds[c] = jnp.concatenate([kind_ref[0], jnp.zeros((6, SLOTS), I32)], axis=0)
    own_slots = pl.ds(pl.multiple_of(c * 2 * SLOTS, 2 * SLOTS), 2 * SLOTS)
    edges[D:WIDE, own_slots] = jnp.zeros((WIDE - D, 2 * SLOTS), BF16)

    pl.semaphore_wait(barrier, len(greet))

    mine = table.at[zh, x, c]
    quarter = table.at[zh, x, c, :, lane(y)]
    to_zh = {k: send(quarter, quarter, zhs[k]) for k in ks}
    own_x = [send(mine, mine, xs[k]) for k in ks]
    kinds_sib = send(kinds.at[c], kinds.at[c], sibling)

    both = jnp.concatenate([kind_ref[0, 0:1, :], kind_ref[0, 1:2, :]], axis=1)
    shard_of = (both * 64528) >> 22
    spot = both + (ROWS - OWN) * shard_of

    def fill(i, _):
        hot_all[i // 8, pl.ds(pl.multiple_of((i % 8) * ROWS, ROWS), ROWS), :] = hot(spot, i * ROWS, ROWS)
        return 0

    lax.fori_loop(0, 32, fill, 0)

    def spread_y_first(k, lo, hi):
        other = flip(zh, k)
        piece = table.at[other, x, c, lo:hi, lane(y)]
        return [send(piece, piece, ys[j]) for j in ks]

    def spread_y_second(k, lo, hi):
        other = flip(zh, k)
        piece = table.at[other, :, c, lo:hi, lane(y)]
        return [send(piece, piece, ys[j]) for j in ks]

    def spread_x_first(k, lo, hi):
        other = flip(zh, k)
        piece = table.at[other, x, c, lo:hi, lane(y)]
        return [send(piece, piece, xs[j]) for j in ks]

    def spread_x_second(k, lo, hi):
        other = flip(zh, k)
        piece = table.at[other, x, c, lo:hi, :]
        return [send(piece, piece, xs[j]) for j in ks]

    def to_sibling(where):
        piece = table.at[where, :, c]
        return send(piece, piece, sibling)

    def look_up(where, first):
        got = dot(table[where].reshape(8 * ROWS, WIDE)[:, 0:D], hot_all[where], 0, 0)
        if first:
            rr_buf[...] = got
        else:
            rr_buf[...] += got

    cut = 48
    arrived([to_zh[1]])
    one_a = spread_y_first(1, 0, ROWS)
    arrived([to_zh[3]])
    three_a = spread_x_first(3, 0, ROWS)
    arrived(own_x)
    sib_own = to_sibling(zh)
    arrived([to_zh[2]])
    two_x = spread_x_first(2, 0, cut)
    two_y = spread_y_first(2, cut, ROWS)
    arrived(one_a)
    one_b = spread_x_second(1, 0, ROWS)
    arrived(three_a)
    three_b = spread_y_second(3, 0, ROWS)
    arrived([sib_own])
    look_up(zh, True)
    arrived(two_x)
    two_xb = spread_y_second(2, 0, cut)
    arrived(two_y)
    two_yb = spread_x_second(2, cut, ROWS)
    arrived(one_b)
    sib_one = to_sibling(flip(zh, 1))
    arrived(three_b)
    sib_three = to_sibling(flip(zh, 3))
    arrived([sib_one])
    look_up(flip(zh, 1), False)
    arrived(two_xb)
    arrived(two_yb)
    sib_two = to_sibling(flip(zh, 2))
    arrived([sib_three])
    look_up(flip(zh, 3), False)
    arrived([sib_two])
    look_up(flip(zh, 2), False)

    def front(turn, lhs):
        src = hot(src_ref[0, turn : turn + 1, :], 0, EP)
        a_buf[...] = dot(lhs, src, 1, 0)
        cols = slice(turn * SLOTS, (turn + 1) * SLOTS)
        a_re, a_im = a_buf[0:HALF, :], a_buf[HALF:D, :]
        r_re, r_im = rr_buf[0:HALF, cols], rr_buf[HALF:D, cols]
        q_buf[...] = jnp.concatenate([a_re * r_re - a_im * r_im, a_re * r_im + a_im * r_re], axis=0).astype(BF16)

    def weights(turn, rhs):
        score = dot(rhs, q_buf[...], 0, 0)
        dst = dst_ref[0, turn : turn + 1, :]
        is_dst = lax.broadcasted_iota(I32, (EP, SLOTS), 0) == dst
        drawn = hot(neg_ref[0, turn : turn + 1, :], 0, EP)
        times = jnp.sum(drawn.astype(F32), axis=1, keepdims=True)
        pos = jnp.sum(jnp.where(is_dst, score, 0.0), axis=0, keepdims=True)
        live = jnp.where(
            lax.broadcasted_iota(I32, (1, SLOTS), 1) < count_ref[0, turn], 1.0, 0.0
        )
        neg_exp = jnp.exp(score)
        pos_exp = jnp.exp(pos)
        total = pos_exp + jnp.sum(jnp.where(times > 0.0, times * neg_exp, 0.0), axis=0, keepdims=True)
        w_pos = live * (pos_exp / total - 1.0)
        w_neg = (live * neg_exp / total).astype(BF16).astype(F32)
        weight = jnp.where(times > 0.0, times * w_neg, 0.0) + jnp.where(is_dst, w_pos, 0.0)
        high, rest = split(weight)
        m_hi[...] = high
        m_lo[...] = rest

    def rhs_grad():
        q = q_buf[...]
        return dot(q, m_hi[...], 1, 1) + dot(q, m_lo[...], 1, 1)

    def back(turn, rhs):
        dq = dot(rhs, m_hi[...], 1, 0) + dot(rhs, m_lo[...], 1, 0)
        cols = slice(turn * SLOTS, (turn + 1) * SLOTS)
        d_re, d_im = dq[0:HALF, :], dq[HALF:D, :]
        a_re, a_im = a_buf[0:HALF, :], a_buf[HALF:D, :]
        r_re, r_im = rr_buf[0:HALF, cols], rr_buf[HALF:D, cols]
        grad_r = jnp.concatenate([d_re * a_re + d_im * a_im, d_im * a_re - d_re * a_im], axis=0)
        a_buf[...] = jnp.concatenate([d_re * r_re + d_im * r_im, d_im * r_re - d_re * r_im], axis=0)
        spot_ = pl.ds(pl.multiple_of((c * 2 + turn) * SLOTS, SLOTS), SLOTS)
        edges[0:D, spot_] = grad_r.astype(BF16)
        return send(edges.at[:, spot_], edges.at[:, spot_], sibling)

    def lhs_grad(turn):
        src = hot(src_ref[0, turn : turn + 1, :], 0, EP)
        high, rest = split(a_buf[...])
        return dot(high, src, 1, 1) + dot(rest, src, 1, 1)

    front(0, lhs_ref[...])
    weights(0, rhs_ref[...])
    new_rhs, new_rst = adagrad(rhs_ref[...], rst_ref[...], rhs_grad())
    rhs_send[...] = new_rhs
    rst_send[...] = jnp.broadcast_to(new_rst, (8, EP))
    passed = [send(rhs_send, rhs_in, after), send(rst_send, rst_in, after)]
    edges_sib = [back(0, rhs_ref[...])]
    new_lhs, new_lst = adagrad(lhs_ref[...], lst_ref[...], lhs_grad(0))
    lhs_out[...] = new_lhs
    lst_out[...] = new_lst

    front(1, lhs_out[...])

    arrived([kinds_sib])
    for core in range(2):
        for turn in range(2):
            kind = kinds[core, turn : turn + 1, :]
            shard = (kind * 64528) >> 22
            half = shard >> 1
            local = jnp.where(shard - 2 * half == c, kind - OWN * shard + ROWS * half, -1)
            at = (core * 2 + turn) * SLOTS

            def fill_mine(i, _, local=local, at=at):
                hot_mine[i // 4, pl.ds(pl.multiple_of((i % 4) * ROWS, ROWS), ROWS), at : at + SLOTS] = hot(
                    local, i * ROWS, ROWS
                )
                return 0

            lax.fori_loop(0, 16, fill_mine, 0)

    arrived(passed)
    weights(1, rhs_in[...])
    edges_sib.append(back(1, rhs_in[...]))
    arrived(edges_sib)

    def chunk(i):
        got = dot(hot_mine[i], edges[...], 1, 1)
        part[i] = got.astype(BF16).reshape(4, ROWS, WIDE)

    chunk(0)
    chunk(1)
    xa = {k: send(part.at[0:2, flip(x, k)], x_in.at[k - 1], xs[k]) for k in ks}
    chunk(2)
    chunk(3)
    ya = {k: send(part.at[2:4, :, :, lane(flip(y, k))], y_in.at[k - 1], ys[k]) for k in ks}

    new_rhs, new_rst = adagrad(rhs_in[...], rst_in[0:1, :], rhs_grad())
    rhs_out[...] = new_rhs
    rst_out[...] = new_rst
    new_lhs, new_lst = adagrad(lhs_out[...], lst_out[...], lhs_grad(1))
    lhs_out[...] = new_lhs
    lst_out[...] = new_lst

    arrived(xa.values())
    sum_x = part[0:2, x].astype(F32)
    for k in ks:
        sum_x += x_in[k - 1].astype(F32)
    stage2y[...] = sum_x.astype(BF16)
    yb = {k: send(stage2y.at[:, :, lane(flip(y, k))], y2_in.at[k - 1], ys[k]) for k in ks}

    arrived(ya.values())
    sum_y = part[2:4, :, :, lane(y)].astype(F32)
    for k in ks:
        sum_y += y_in[k - 1].astype(F32)
    stage2x[...] = sum_y.astype(BF16)
    xb = {k: send(stage2x.at[:, flip(x, k)], x2_in.at[k - 1], xs[k]) for k in ks}

    arrived(yb.values())
    low_sum = stage2y[:, :, lane(y)].astype(F32)
    for k in ks:
        low_sum += y2_in[k - 1].astype(F32)
    z_out[0:2] = low_sum.astype(BF16)
    arrived(xb.values())
    high_sum = stage2x[:, x].astype(F32)
    for k in ks:
        high_sum += x2_in[k - 1].astype(F32)
    z_out[2:4] = high_sum.astype(BF16)

    za = {k: send(z_out.at[flip(zh, k)], z_in.at[k - 1], zhs[k]) for k in ks}
    arrived(za.values())
    over_zh = z_out[zh].astype(F32)
    for k in ks:
        over_zh += z_in[k - 1].astype(F32)
    low[zl] = over_zh.astype(BF16)
    zb = [send(low.at[zl], low.at[zl], zls[k]) for k in ks]
    arrived(zb)
    both_z = (low[0].astype(F32) + low[1].astype(F32)) + (low[2].astype(F32) + low[3].astype(F32))
    full[:, lane(y)] = both_z
    last = [send(full.at[:, lane(y)], full.at[:, lane(y)], ys[k]) for k in ks]
    arrived(last)

    total = full[0:OWN, 0:D]
    eye = lax.broadcasted_iota(I32, (OWN, OWN), 0) == lax.broadcasted_iota(I32, (OWN, OWN), 1)
    old = jnp.sum(jnp.where(eye, relst_ref[...], 0.0), axis=1, keepdims=True)
    new = old + jnp.sum(total * total, axis=1, keepdims=True) / D
    rel_out[...] = rel_ref[...] - LEARN * total / (jnp.sqrt(new) + EPSILON)
    relst_out[...] = jnp.sum(jnp.where(eye, new, 0.0), axis=0, keepdims=True)

    for copy in started:
        copy.wait_send()


N_COPIES = 80


def body(
    lhs_table, lhs_state, rhs_table, rhs_state, relations, rel_state,
    src_index, dst_index, rel_index, neg_index, edge_count,
):
    vmem = pl.BlockSpec(memory_space=pltpu.VMEM)
    smem = pl.BlockSpec(memory_space=pltpu.SMEM)
    shape = jax.ShapeDtypeStruct
    outs = pl.pallas_call(
        kernel,
        out_shape=(
            shape((D, EP), BF16), shape((1, EP), F32), shape((D, EP), BF16), shape((1, EP), F32),
            shape((OWN, D), F32), shape((1, OWN), F32),
        ),
        in_specs=[vmem] * 10 + [smem],
        out_specs=(vmem,) * 6,
        scratch_shapes=[
            pltpu.VMEM((4, 4, 2, ROWS, WIDE), BF16),
            pltpu.VMEM((4, 8 * ROWS, 2 * SLOTS), BF16),
            pltpu.VMEM((4, 4 * ROWS, 4 * SLOTS), BF16),
            pltpu.VMEM((2, 8, SLOTS), I32),
            pltpu.VMEM((D, SLOTS), F32),
            pltpu.VMEM((D, 2 * SLOTS), F32),
            pltpu.VMEM((D, SLOTS), BF16),
            pltpu.VMEM((EP, SLOTS), BF16),
            pltpu.VMEM((EP, SLOTS), BF16),
            pltpu.VMEM((WIDE, 4 * SLOTS), BF16),
            pltpu.VMEM((D, EP), BF16),
            pltpu.VMEM((8, EP), F32),
            pltpu.VMEM((D, EP), BF16),
            pltpu.VMEM((8, EP), F32),
            pltpu.VMEM((4, 4, ROWS, WIDE), BF16),
            pltpu.VMEM((3, 2, ROWS, WIDE), BF16),
            pltpu.VMEM((3, 2, 4, ROWS, LANE), BF16),
            pltpu.VMEM((3, 2, ROWS, LANE), BF16),
            pltpu.VMEM((3, 2, ROWS, LANE), BF16),
            pltpu.VMEM((4, ROWS, LANE), BF16),
            pltpu.VMEM((3, ROWS, LANE), BF16),
            pltpu.VMEM((4, ROWS, LANE), BF16),
            pltpu.VMEM((ROWS, WIDE), F32),
            pltpu.VMEM((2, 4, ROWS, LANE), BF16),
            pltpu.VMEM((2, ROWS, WIDE), BF16),
            pltpu.SemaphoreType.DMA((N_COPIES,)),
            pltpu.SemaphoreType.DMA((N_COPIES,)),
        ],
        compiler_params=pltpu.CompilerParams(
            collective_id=0, has_side_effects=True, vmem_limit_bytes=48 * 2**20
        ),
        name="train",
    )(
        lhs_table.T, lhs_state[None, :], rhs_table.T, rhs_state[None, :], relations, rel_state[None, :],
        src_index, dst_index, rel_index, neg_index, edge_count,
    )
    lhs, lhs_st, rhs, rhs_st, rel, rel_st = outs
    return (lhs.T, lhs_st[0], rhs.T, rhs_st[0], rel, rel_st[0])


def solution(mesh):
    return jax.shard_map(
        body,
        mesh=mesh,
        in_specs=(
            P(("grp", "dev"), None),
            P(("grp", "dev")),
            P(("grp", "dev"), None),
            P(("grp", "dev")),
            P("dev", None),
            P("dev"),
            P(("grp", "dev"), None, None),
            P(("grp", "dev"), None, None),
            P(("grp", "dev"), None, None),
            P(("grp", "dev"), None, None),
            P(("grp", "dev"), None),
        ),
        out_specs=(
            P(("grp", "dev"), None),
            P(("grp", "dev")),
            P(("grp", "dev"), None),
            P(("grp", "dev")),
            P("dev", None),
            P("dev"),
        ),
        check_vma=False,
    )
```

```python
import functools

import jax
import jax.numpy as jnp
from jax import lax
from jax.experimental import pallas as pl
from jax.experimental.pallas import tpu as pltpu
from jax.sharding import PartitionSpec as P

LEARN = 0.1
EPSILON = 1e-06
MESH = pl.DeviceIdType.MESH
F32, BF16, I32 = jnp.float32, jnp.bfloat16, jnp.int32

D = 400
HALF = 200
WIDE = 512
OWN = 65
ROWS = 80
EP = 128
SLOTS = 512
LANE = 128


def flip(value, k):
    if k == 1:
        return value + 1 - 2 * (value % 2)
    if k == 3:
        return 3 - value
    return (value + 2) % 4


def dot(a, b, ca, cb):
    return lax.dot_general(a, b, (((ca,), (cb,)), ((), ())), preferred_element_type=F32)


def hot(index, first, count):
    rows = lax.broadcasted_iota(I32, (count, index.shape[1]), 0) + first
    return jnp.where(rows == index, 1.0, 0.0).astype(BF16)


def split(value):
    high = value.astype(BF16)
    return high, (value - high.astype(F32)).astype(BF16)


def adagrad(rows, state, grad):
    new_state = state + jnp.sum(grad * grad, axis=0, keepdims=True) / D
    moved = rows.astype(F32) - LEARN * grad / (jnp.sqrt(new_state) + EPSILON)
    return moved.astype(BF16), new_state


def kernel(
    lhs_hbm, lst_hbm, rhs_hbm, rst_hbm, rel_hbm, relst_hbm, src_hbm, dst_hbm, kind_hbm, neg_hbm, count_ref,
    lhs_res, lst_res, rhs_res, rst_res, rel_res, relst_res,
    lhs_ref, lst_ref, rhs_ref, rst_ref, rel_ref, relst_ref, src_ref, dst_ref, kind_ref, neg_ref,
    lhs_out, lst_out, rhs_out, rst_out, rel_out, relst_out,
    table, hot_all, hot_mine, kinds, a_buf, rr_buf, q_buf, m_hi, m_lo, edges,
    rhs_send, rst_send, rhs_in, rst_in, part, x_in, y_in, x2_in, y2_in, z_out, z_in, low, full, stage2x, stage2y,
    send_sem, recv_sem, in_sem, out_sem,
):
    grp, dev = lax.axis_index("grp"), lax.axis_index("dev")
    y, zl = grp // 4, grp % 4
    zh, x, c = dev // 8, (dev // 2) % 4, dev % 2

    def place(x_=None, y_=None, zh_=None, zl_=None, c_=None):
        x_ = x if x_ is None else x_
        y_ = y if y_ is None else y_
        zh_ = zh if zh_ is None else zh_
        zl_ = zl if zl_ is None else zl_
        c_ = c if c_ is None else c_
        return (y_ * 4 + zl_, zh_ * 8 + x_ * 2 + c_)

    sibling = place(c_=1 - c)
    after = (grp, (dev + 1) % 32)
    before = (grp, (dev + 31) % 32)
    ks = (1, 3, 2)
    xs = {k: place(x_=flip(x, k)) for k in ks}
    ys = {k: place(y_=flip(y, k)) for k in ks}
    zhs = {k: place(zh_=flip(zh, k)) for k in ks}
    zls = {k: place(zl_=flip(zl, k)) for k in ks}

    barrier = pltpu.get_barrier_semaphore()
    greet = [sibling, before, *xs.values(), *ys.values(), *zhs.values(), *zls.values()]
    for other in greet:
        pl.semaphore_signal(barrier, inc=1, device_id=other, device_id_type=MESH)

    loads = [
        pltpu.make_async_copy(src, dst, in_sem.at[i])
        for i, (src, dst) in enumerate(
            (
                (rel_hbm, rel_ref), (kind_hbm, kind_ref), (lhs_hbm, lhs_ref), (src_hbm, src_ref), (rhs_hbm, rhs_ref),
                (dst_hbm, dst_ref), (neg_hbm, neg_ref), (lst_hbm, lst_ref), (rst_hbm, rst_ref), (relst_hbm, relst_ref),
            )
        )
    ]
    for copy in loads:
        copy.start()
    started, stores = [], []

    def give(src, dst):
        copy = pltpu.make_async_copy(src, dst, out_sem.at[len(stores)])
        copy.start()
        stores.append(copy)

    def send(src, dst, target):
        i = len(started)
        copy = pltpu.make_async_remote_copy(
            src_ref=src, dst_ref=dst, send_sem=send_sem.at[i], recv_sem=recv_sem.at[i],
            device_id=target, device_id_type=MESH,
        )
        copy.start()
        started.append(copy)
        return copy

    def arrived(copies):
        for copy in copies:
            copy.wait_recv()

    def lane(value):
        return pl.ds(pl.multiple_of(value * LANE, LANE), LANE)

    own_slots = pl.ds(pl.multiple_of(c * 2 * SLOTS, 2 * SLOTS), 2 * SLOTS)
    edges[D:WIDE, own_slots] = jnp.zeros((WIDE - D, 2 * SLOTS), BF16)
    table[zh, x, c] = jnp.zeros((ROWS, WIDE), BF16)
    for copy in loads[:2]:
        copy.wait()
    table[zh, x, c, 0:OWN, 0:D] = rel_ref[...].astype(BF16)
    kinds[c] = jnp.concatenate([kind_ref[0], jnp.zeros((6, SLOTS), I32)], axis=0)

    pl.semaphore_wait(barrier, len(greet))

    mine = table.at[zh, x, c]
    quarter = table.at[zh, x, c, :, lane(y)]
    to_zh = {k: send(quarter, quarter, zhs[k]) for k in ks}
    own_x = [send(mine, mine, xs[k]) for k in ks]
    kinds_sib = send(kinds.at[c], kinds.at[c], sibling)

    both = jnp.concatenate([kind_ref[0, 0:1, :], kind_ref[0, 1:2, :]], axis=1)
    shard_of = (both * 64528) >> 22
    spot = both + (ROWS - OWN) * shard_of

    def fill(i, _):
        hot_all[i // 8, pl.ds(pl.multiple_of((i % 8) * ROWS, ROWS), ROWS), :] = hot(spot, i * ROWS, ROWS)
        return 0

    lax.fori_loop(0, 32, fill, 0)
    for copy in loads[2:]:
        copy.wait()

    def spread_y_first(k, lo, hi):
        other = flip(zh, k)
        piece = table.at[other, x, c, lo:hi, lane(y)]
        return [send(piece, piece, ys[j]) for j in ks]

    def spread_y_second(k, lo, hi):
        other = flip(zh, k)
        piece = table.at[other, :, c, lo:hi, lane(y)]
        return [send(piece, piece, ys[j]) for j in ks]

    def spread_x_first(k, lo, hi):
        other = flip(zh, k)
        piece = table.at[other, x, c, lo:hi, lane(y)]
        return [send(piece, piece, xs[j]) for j in ks]

    def spread_x_second(k, lo, hi):
        other = flip(zh, k)
        piece = table.at[other, x, c, lo:hi, :]
        return [send(piece, piece, xs[j]) for j in ks]

    def to_sibling(where):
        piece = table.at[where, :, c]
        return send(piece, piece, sibling)

    def look_up(where, first):
        got = dot(table[where].reshape(8 * ROWS, WIDE)[:, 0:D], hot_all[where], 0, 0)
        if first:
            rr_buf[...] = got
        else:
            rr_buf[...] += got

    cut = 48
    arrived([to_zh[1]])
    one_a = spread_y_first(1, 0, ROWS)
    arrived([to_zh[3]])
    three_a = spread_x_first(3, 0, ROWS)
    arrived(own_x)
    sib_own = to_sibling(zh)
    arrived([to_zh[2]])
    two_x = spread_x_first(2, 0, cut)
    two_y = spread_y_first(2, cut, ROWS)
    arrived(one_a)
    one_b = spread_x_second(1, 0, ROWS)
    arrived(three_a)
    three_b = spread_y_second(3, 0, ROWS)
    arrived([sib_own])
    look_up(zh, True)
    arrived(two_x)
    two_xb = spread_y_second(2, 0, cut)
    arrived(two_y)
    two_yb = spread_x_second(2, cut, ROWS)
    arrived(one_b)
    sib_one = to_sibling(flip(zh, 1))
    arrived(three_b)
    sib_three = to_sibling(flip(zh, 3))
    arrived([sib_one])
    look_up(flip(zh, 1), False)
    arrived(two_xb)
    arrived(two_yb)
    sib_two = to_sibling(flip(zh, 2))
    arrived([sib_three])
    look_up(flip(zh, 3), False)
    arrived([sib_two])
    look_up(flip(zh, 2), False)

    def front(turn, lhs):
        src = hot(src_ref[0, turn : turn + 1, :], 0, EP)
        a_buf[...] = dot(lhs, src, 1, 0)
        cols = slice(turn * SLOTS, (turn + 1) * SLOTS)
        a_re, a_im = a_buf[0:HALF, :], a_buf[HALF:D, :]
        r_re, r_im = rr_buf[0:HALF, cols], rr_buf[HALF:D, cols]
        q_buf[...] = jnp.concatenate([a_re * r_re - a_im * r_im, a_re * r_im + a_im * r_re], axis=0).astype(BF16)

    def weights(turn, rhs):
        score = dot(rhs, q_buf[...], 0, 0)
        dst = dst_ref[0, turn : turn + 1, :]
        is_dst = lax.broadcasted_iota(I32, (EP, SLOTS), 0) == dst
        drawn = hot(neg_ref[0, turn : turn + 1, :], 0, EP)
        times = jnp.sum(drawn.astype(F32), axis=1, keepdims=True)
        pos = jnp.sum(jnp.where(is_dst, score, 0.0), axis=0, keepdims=True)
        live = jnp.where(
            lax.broadcasted_iota(I32, (1, SLOTS), 1) < count_ref[0, turn], 1.0, 0.0
        )
        neg_exp = jnp.exp(score)
        pos_exp = jnp.exp(pos)
        total = pos_exp + jnp.sum(jnp.where(times > 0.0, times * neg_exp, 0.0), axis=0, keepdims=True)
        w_pos = live * (pos_exp / total - 1.0)
        w_neg = (live * neg_exp / total).astype(BF16).astype(F32)
        weight = jnp.where(times > 0.0, times * w_neg, 0.0) + jnp.where(is_dst, w_pos, 0.0)
        high, rest = split(weight)
        m_hi[...] = high
        m_lo[...] = rest

    def rhs_grad():
        q = q_buf[...]
        return dot(q, m_hi[...], 1, 1) + dot(q, m_lo[...], 1, 1)

    def back(turn, rhs):
        dq = dot(rhs, m_hi[...], 1, 0) + dot(rhs, m_lo[...], 1, 0)
        cols = slice(turn * SLOTS, (turn + 1) * SLOTS)
        d_re, d_im = dq[0:HALF, :], dq[HALF:D, :]
        a_re, a_im = a_buf[0:HALF, :], a_buf[HALF:D, :]
        r_re, r_im = rr_buf[0:HALF, cols], rr_buf[HALF:D, cols]
        grad_r = jnp.concatenate([d_re * a_re + d_im * a_im, d_im * a_re - d_re * a_im], axis=0)
        a_buf[...] = jnp.concatenate([d_re * r_re + d_im * r_im, d_im * r_re - d_re * r_im], axis=0)
        spot_ = pl.ds(pl.multiple_of((c * 2 + turn) * SLOTS, SLOTS), SLOTS)
        edges[0:D, spot_] = grad_r.astype(BF16)
        return send(edges.at[:, spot_], edges.at[:, spot_], sibling)

    def lhs_grad(turn):
        src = hot(src_ref[0, turn : turn + 1, :], 0, EP)
        high, rest = split(a_buf[...])
        return dot(high, src, 1, 1) + dot(rest, src, 1, 1)

    front(0, lhs_ref[...])
    weights(0, rhs_ref[...])
    new_rhs, new_rst = adagrad(rhs_ref[...], rst_ref[...], rhs_grad())
    rhs_send[...] = new_rhs
    rst_send[...] = jnp.broadcast_to(new_rst, (8, EP))
    passed = [send(rhs_send, rhs_in, after), send(rst_send, rst_in, after)]
    edges_sib = [back(0, rhs_ref[...])]
    new_lhs, new_lst = adagrad(lhs_ref[...], lst_ref[...], lhs_grad(0))
    lhs_out[...] = new_lhs
    lst_out[...] = new_lst

    front(1, lhs_out[...])

    arrived([kinds_sib])
    for core in range(2):
        for turn in range(2):
            kind = kinds[core, turn : turn + 1, :]
            shard = (kind * 64528) >> 22
            half = shard >> 1
            local = jnp.where(shard - 2 * half == c, kind - OWN * shard + ROWS * half, -1)
            at = (core * 2 + turn) * SLOTS

            def fill_mine(i, _, local=local, at=at):
                hot_mine[i // 4, pl.ds(pl.multiple_of((i % 4) * ROWS, ROWS), ROWS), at : at + SLOTS] = hot(
                    local, i * ROWS, ROWS
                )
                return 0

            lax.fori_loop(0, 16, fill_mine, 0)

    arrived(passed)
    weights(1, rhs_in[...])
    edges_sib.append(back(1, rhs_in[...]))
    arrived(edges_sib)

    def chunk(i):
        got = dot(hot_mine[i], edges[...], 1, 1)
        part[i] = got.astype(BF16).reshape(4, ROWS, WIDE)

    def x_first(i):
        chunk(i)
        return {k: send(part.at[i, flip(x, k)], x_in.at[i, k - 1], xs[k]) for k in ks}

    def y_first(i):
        chunk(i)
        return {k: send(part.at[i, :, :, lane(flip(y, k))], y_in.at[i - 2, k - 1], ys[k]) for k in ks}

    first = {0: x_first(0), 2: y_first(2), 1: x_first(1), 3: y_first(3)}

    new_rhs, new_rst = adagrad(rhs_in[...], rst_in[0:1, :], rhs_grad())
    rhs_out[...] = new_rhs
    rst_out[...] = new_rst
    new_lhs, new_lst = adagrad(lhs_out[...], lst_out[...], lhs_grad(1))
    lhs_out[...] = new_lhs
    lst_out[...] = new_lst
    for src, dst in ((lhs_out, lhs_res), (lst_out, lst_res), (rhs_out, rhs_res), (rst_out, rst_res)):
        give(src, dst)

    def x_then_y(i):
        arrived(first[i].values())
        total = part[i, x].astype(F32)
        for k in ks:
            total += x_in[i, k - 1].astype(F32)
        stage2y[i] = total.astype(BF16)
        return {k: send(stage2y.at[i, :, lane(flip(y, k))], y2_in.at[i, k - 1], ys[k]) for k in ks}

    def y_then_x(i):
        arrived(first[i].values())
        total = part[i, :, :, lane(y)].astype(F32)
        for k in ks:
            total += y_in[i - 2, k - 1].astype(F32)
        stage2x[i - 2] = total.astype(BF16)
        return {k: send(stage2x.at[i - 2, flip(x, k)], x2_in.at[i - 2, k - 1], xs[k]) for k in ks}

    second = {0: x_then_y(0), 2: y_then_x(2), 1: x_then_y(1), 3: y_then_x(3)}

    for i in (0, 2, 1, 3):
        arrived(second[i].values())
        total = (stage2y[i, :, lane(y)] if i < 2 else stage2x[i - 2, x]).astype(F32)
        for k in ks:
            total += (y2_in[i, k - 1] if i < 2 else x2_in[i - 2, k - 1]).astype(F32)
        z_out[i] = total.astype(BF16)

    za = {k: send(z_out.at[flip(zh, k)], z_in.at[k - 1], zhs[k]) for k in ks}
    arrived(za.values())
    over_zh = z_out[zh].astype(F32)
    for k in ks:
        over_zh += z_in[k - 1].astype(F32)
    low[zl] = over_zh.astype(BF16)
    zb = [send(low.at[zl], low.at[zl], zls[k]) for k in ks]
    arrived(zb)
    both_z = (low[0].astype(F32) + low[1].astype(F32)) + (low[2].astype(F32) + low[3].astype(F32))
    full[:, lane(y)] = both_z
    last = [send(full.at[:, lane(y)], full.at[:, lane(y)], ys[k]) for k in ks]
    arrived(last)

    total = full[0:OWN, 0:D]
    eye = lax.broadcasted_iota(I32, (OWN, OWN), 0) == lax.broadcasted_iota(I32, (OWN, OWN), 1)
    old = jnp.sum(jnp.where(eye, relst_ref[...], 0.0), axis=1, keepdims=True)
    new = old + jnp.sum(total * total, axis=1, keepdims=True) / D
    rel_out[...] = rel_ref[...] - LEARN * total / (jnp.sqrt(new) + EPSILON)
    relst_out[...] = jnp.sum(jnp.where(eye, new, 0.0), axis=0, keepdims=True)

    give(rel_out, rel_res)
    give(relst_out, relst_res)
    for copy in started:
        copy.wait_send()
    for copy in stores:
        copy.wait()


def hand_on(*refs):
    held, sem = refs[12:18], refs[18]
    loads = [pltpu.make_async_copy(refs[i], held[i], sem.at[i]) for i in range(6)]
    stores = [pltpu.make_async_copy(held[i], refs[6 + i], sem.at[6 + i]) for i in range(6)]
    for copy in loads:
        copy.start()
    for load, store in zip(loads, stores):
        load.wait()
        store.start()
    for copy in stores:
        copy.wait()


N_COPIES = 96


def body(
    lhs_table, lhs_state, rhs_table, rhs_state, relations, rel_state,
    src_index, dst_index, rel_index, neg_index, edge_count,
):
    hbm = pl.BlockSpec(memory_space=pltpu.HBM)
    smem = pl.BlockSpec(memory_space=pltpu.SMEM)
    shape = jax.ShapeDtypeStruct
    out_shape = (
        shape((D, EP), BF16), shape((1, EP), F32), shape((D, EP), BF16), shape((1, EP), F32),
        shape((OWN, D), F32), shape((1, OWN), F32),
    )
    outs = pl.pallas_call(
        kernel,
        out_shape=out_shape,
        in_specs=[hbm] * 10 + [smem],
        out_specs=(hbm,) * 6,
        scratch_shapes=[
            pltpu.VMEM((D, EP), BF16), pltpu.VMEM((1, EP), F32), pltpu.VMEM((D, EP), BF16), pltpu.VMEM((1, EP), F32),
            pltpu.VMEM((OWN, D), F32), pltpu.VMEM((1, OWN), F32),
            *[pltpu.VMEM((1, 2, SLOTS), I32) for _ in range(4)],
            *[pltpu.VMEM(out.shape, out.dtype) for out in out_shape],
            pltpu.VMEM((4, 4, 2, ROWS, WIDE), BF16),
            pltpu.VMEM((4, 8 * ROWS, 2 * SLOTS), BF16),
            pltpu.VMEM((4, 4 * ROWS, 4 * SLOTS), BF16),
            pltpu.VMEM((2, 8, SLOTS), I32),
            pltpu.VMEM((D, SLOTS), F32),
            pltpu.VMEM((D, 2 * SLOTS), F32),
            pltpu.VMEM((D, SLOTS), BF16),
            pltpu.VMEM((EP, SLOTS), BF16),
            pltpu.VMEM((EP, SLOTS), BF16),
            pltpu.VMEM((WIDE, 4 * SLOTS), BF16),
            pltpu.VMEM((D, EP), BF16),
            pltpu.VMEM((8, EP), F32),
            pltpu.VMEM((D, EP), BF16),
            pltpu.VMEM((8, EP), F32),
            pltpu.VMEM((4, 4, ROWS, WIDE), BF16),
            pltpu.VMEM((2, 3, ROWS, WIDE), BF16),
            pltpu.VMEM((2, 3, 4, ROWS, LANE), BF16),
            pltpu.VMEM((2, 3, ROWS, LANE), BF16),
            pltpu.VMEM((2, 3, ROWS, LANE), BF16),
            pltpu.VMEM((4, ROWS, LANE), BF16),
            pltpu.VMEM((3, ROWS, LANE), BF16),
            pltpu.VMEM((4, ROWS, LANE), BF16),
            pltpu.VMEM((ROWS, WIDE), F32),
            pltpu.VMEM((2, 4, ROWS, LANE), BF16),
            pltpu.VMEM((2, ROWS, WIDE), BF16),
            pltpu.SemaphoreType.DMA((N_COPIES,)),
            pltpu.SemaphoreType.DMA((N_COPIES,)),
            pltpu.SemaphoreType.DMA((10,)),
            pltpu.SemaphoreType.DMA((6,)),
        ],
        compiler_params=pltpu.CompilerParams(
            collective_id=0, has_side_effects=True, vmem_limit_bytes=60 * 2**20
        ),
        name="train",
    )(
        lhs_table.T, lhs_state[None, :], rhs_table.T, rhs_state[None, :], relations, rel_state[None, :],
        src_index, dst_index, rel_index, neg_index, edge_count,
    )
    lhs, lhs_st, rhs, rhs_st, rel, rel_st = pl.pallas_call(
        hand_on,
        out_shape=out_shape,
        in_specs=[hbm] * 6,
        out_specs=(hbm,) * 6,
        scratch_shapes=[*[pltpu.VMEM(out.shape, out.dtype) for out in out_shape], pltpu.SemaphoreType.DMA((12,))],
        compiler_params=pltpu.CompilerParams(vmem_limit_bytes=60 * 2**20),
        name="hand_on",
    )(*outs)
    return (lhs.T, lhs_st[0], rhs.T, rhs_st[0], rel, rel_st[0])


def solution(mesh):
    return jax.shard_map(
        body,
        mesh=mesh,
        in_specs=(
            P(("grp", "dev"), None),
            P(("grp", "dev")),
            P(("grp", "dev"), None),
            P(("grp", "dev")),
            P("dev", None),
            P("dev"),
            P(("grp", "dev"), None, None),
            P(("grp", "dev"), None, None),
            P(("grp", "dev"), None, None),
            P(("grp", "dev"), None, None),
            P(("grp", "dev"), None),
        ),
        out_specs=(
            P(("grp", "dev"), None),
            P(("grp", "dev")),
            P(("grp", "dev"), None),
            P(("grp", "dev")),
            P("dev", None),
            P("dev"),
        ),
        check_vma=False,
    )
```

```python
import functools

import jax
import jax.numpy as jnp
from jax import lax
from jax.experimental import pallas as pl
from jax.experimental.pallas import tpu as pltpu
from jax.sharding import PartitionSpec as P

LEARN = 0.1
EPSILON = 1e-06
MESH = pl.DeviceIdType.MESH
F32, BF16, I32 = jnp.float32, jnp.bfloat16, jnp.int32

D = 400
HALF = 200
WIDE = 512
OWN = 65
ROWS = 80
EP = 128
SLOTS = 512
LANE = 128


def flip(value, k):
    if k == 1:
        return value + 1 - 2 * (value % 2)
    if k == 3:
        return 3 - value
    return (value + 2) % 4


def dot(a, b, ca, cb):
    return lax.dot_general(a, b, (((ca,), (cb,)), ((), ())), preferred_element_type=F32)


def hot(index, first, count):
    rows = lax.broadcasted_iota(I32, (count, index.shape[1]), 0) + first
    return jnp.where(rows == index, 1.0, 0.0).astype(BF16)


def split(value):
    high = value.astype(BF16)
    return high, (value - high.astype(F32)).astype(BF16)


def adagrad(rows, state, grad):
    new_state = state + jnp.sum(grad * grad, axis=0, keepdims=True) / D
    moved = rows.astype(F32) - LEARN * grad / (jnp.sqrt(new_state) + EPSILON)
    return moved.astype(BF16), new_state


def kernel(
    lhs_hbm, lst_hbm, rhs_hbm, rst_hbm, rel_hbm, relst_hbm, src_hbm, dst_hbm, kind_hbm, neg_hbm, count_ref,
    lhs_res, lst_res, rhs_res, rst_res, rel_res, relst_res,
    lhs_ref, lst_ref, rhs_ref, rst_ref, rel_ref, relst_ref, src_ref, dst_ref, kind_ref, neg_ref,
    lhs_out, lst_out, rhs_out, rst_out, rel_out, relst_out,
    table, hot_all, hot_mine, kinds, a_buf, rr_buf, q_buf, m_hi, m_lo, edges,
    rhs_send, rst_send, rhs_in, rst_in, part, x_in, y_in, x2_in, y2_in, z_out, z_in, low, full, stage2x, stage2y,
    send_sem, recv_sem, in_sem, out_sem,
):
    grp, dev = lax.axis_index("grp"), lax.axis_index("dev")
    y, zl = grp // 4, grp % 4
    zh, x, c = dev // 8, (dev // 2) % 4, dev % 2

    def place(x_=None, y_=None, zh_=None, zl_=None, c_=None):
        x_ = x if x_ is None else x_
        y_ = y if y_ is None else y_
        zh_ = zh if zh_ is None else zh_
        zl_ = zl if zl_ is None else zl_
        c_ = c if c_ is None else c_
        return (y_ * 4 + zl_, zh_ * 8 + x_ * 2 + c_)

    sibling = place(c_=1 - c)
    after = (grp, (dev + 1) % 32)
    ks = (1, 3, 2)
    xs = {k: place(x_=flip(x, k)) for k in ks}
    ys = {k: place(y_=flip(y, k)) for k in ks}
    zhs = {k: place(zh_=flip(zh, k)) for k in ks}
    zls = {k: place(zl_=flip(zl, k)) for k in ks}

    barrier = pltpu.get_barrier_semaphore()
    greet = [sibling, *xs.values(), *ys.values(), zhs[1], zhs[3], *zls.values()]
    for other in greet:
        pl.semaphore_signal(barrier, inc=1, device_id=other, device_id_type=MESH)

    loads = [
        pltpu.make_async_copy(src, dst, in_sem.at[i])
        for i, (src, dst) in enumerate(
            (
                (rel_hbm, rel_ref), (kind_hbm, kind_ref), (lhs_hbm, lhs_ref), (src_hbm, src_ref), (rhs_hbm, rhs_ref),
                (dst_hbm, dst_ref), (neg_hbm, neg_ref), (lst_hbm, lst_ref), (rst_hbm, rst_ref), (relst_hbm, relst_ref),
            )
        )
    ]
    for copy in loads:
        copy.start()
    started, stores = [], []

    def give(src, dst):
        copy = pltpu.make_async_copy(src, dst, out_sem.at[len(stores)])
        copy.start()
        stores.append(copy)

    def send(src, dst, target):
        i = len(started)
        copy = pltpu.make_async_remote_copy(
            src_ref=src, dst_ref=dst, send_sem=send_sem.at[i], recv_sem=recv_sem.at[i],
            device_id=target, device_id_type=MESH,
        )
        copy.start()
        started.append(copy)
        return copy

    def arrived(copies):
        for copy in copies:
            copy.wait_recv()

    def lane(value):
        return pl.ds(pl.multiple_of(value * LANE, LANE), LANE)

    own_slots = pl.ds(pl.multiple_of(c * 2 * SLOTS, 2 * SLOTS), 2 * SLOTS)
    edges[D:WIDE, own_slots] = jnp.zeros((WIDE - D, 2 * SLOTS), BF16)
    table[zh, x, c] = jnp.zeros((ROWS, WIDE), BF16)
    for copy in loads[:2]:
        copy.wait()
    table[zh, x, c, 0:OWN, 0:D] = rel_ref[...].astype(BF16)
    kinds[c] = jnp.concatenate([kind_ref[0], jnp.zeros((6, SLOTS), I32)], axis=0)

    pl.semaphore_wait(barrier, len(greet))

    mine = table.at[zh, x, c]
    quarter = table.at[zh, x, c, :, lane(y)]
    to_zh = {k: send(quarter, quarter, zhs[k]) for k in (1, 3)}
    own_x = [send(mine, mine, xs[k]) for k in ks]
    kinds_sib = send(kinds.at[c], kinds.at[c], sibling)

    both = jnp.concatenate([kind_ref[0, 0:1, :], kind_ref[0, 1:2, :]], axis=1)
    shard_of = (both * 64528) >> 22
    spot = both + (ROWS - OWN) * shard_of

    def fill(i, _):
        hot_all[i // 8, pl.ds(pl.multiple_of((i % 8) * ROWS, ROWS), ROWS), :] = hot(spot, i * ROWS, ROWS)
        return 0

    lax.fori_loop(0, 32, fill, 0)
    for copy in loads[2:]:
        copy.wait()

    def spread_y_first(k, lo, hi):
        other = flip(zh, k)
        piece = table.at[other, x, c, lo:hi, lane(y)]
        return [send(piece, piece, ys[j]) for j in ks]

    def spread_y_second(k, lo, hi):
        other = flip(zh, k)
        piece = table.at[other, :, c, lo:hi, lane(y)]
        return [send(piece, piece, ys[j]) for j in ks]

    def spread_x_first(k, lo, hi):
        other = flip(zh, k)
        piece = table.at[other, x, c, lo:hi, lane(y)]
        return [send(piece, piece, xs[j]) for j in ks]

    def spread_x_second(k, lo, hi):
        other = flip(zh, k)
        piece = table.at[other, x, c, lo:hi, :]
        return [send(piece, piece, xs[j]) for j in ks]

    def relay(source, target, lo, hi):
        piece = table.at[flip(zh, source), x, c, lo:hi, lane(y)]
        return send(piece, piece, zhs[target])

    def to_sibling(where):
        piece = table.at[where, :, c]
        return send(piece, piece, sibling)

    def look_up(where, first):
        got = dot(table[where].reshape(8 * ROWS, WIDE)[:, 0:D], hot_all[where], 0, 0)
        if first:
            rr_buf[...] = got
        else:
            rr_buf[...] += got

    cut = 48
    arrived([to_zh[1]])
    relay_x = relay(1, 3, 0, cut)
    one_a = spread_y_first(1, 0, ROWS)
    arrived([to_zh[3]])
    relay_y = relay(3, 1, cut, ROWS)
    three_a = spread_x_first(3, 0, ROWS)
    arrived(own_x)
    sib_own = to_sibling(zh)
    arrived([relay_x])
    two_x = spread_x_first(2, 0, cut)
    arrived([relay_y])
    two_y = spread_y_first(2, cut, ROWS)
    arrived(one_a)
    one_b = spread_x_second(1, 0, ROWS)
    arrived(three_a)
    three_b = spread_y_second(3, 0, ROWS)
    arrived([sib_own])
    look_up(zh, True)
    arrived(two_x)
    two_xb = spread_y_second(2, 0, cut)
    arrived(two_y)
    two_yb = spread_x_second(2, cut, ROWS)
    arrived(one_b)
    sib_one = to_sibling(flip(zh, 1))
    arrived(three_b)
    sib_three = to_sibling(flip(zh, 3))
    arrived([sib_one])
    look_up(flip(zh, 1), False)
    arrived(two_xb)
    arrived(two_yb)
    sib_two = to_sibling(flip(zh, 2))
    arrived([sib_three])
    look_up(flip(zh, 3), False)
    arrived([sib_two])
    look_up(flip(zh, 2), False)

    def front(turn, lhs):
        src = hot(src_ref[0, turn : turn + 1, :], 0, EP)
        a_buf[...] = dot(lhs, src, 1, 0)
        cols = slice(turn * SLOTS, (turn + 1) * SLOTS)
        a_re, a_im = a_buf[0:HALF, :], a_buf[HALF:D, :]
        r_re, r_im = rr_buf[0:HALF, cols], rr_buf[HALF:D, cols]
        q_buf[...] = jnp.concatenate([a_re * r_re - a_im * r_im, a_re * r_im + a_im * r_re], axis=0).astype(BF16)

    def weights(turn, rhs):
        score = dot(rhs, q_buf[...], 0, 0)
        dst = dst_ref[0, turn : turn + 1, :]
        is_dst = lax.broadcasted_iota(I32, (EP, SLOTS), 0) == dst
        drawn = hot(neg_ref[0, turn : turn + 1, :], 0, EP)
        times = jnp.sum(drawn.astype(F32), axis=1, keepdims=True)
        pos = jnp.sum(jnp.where(is_dst, score, 0.0), axis=0, keepdims=True)
        live = jnp.where(
            lax.broadcasted_iota(I32, (1, SLOTS), 1) < count_ref[0, turn], 1.0, 0.0
        )
        neg_exp = jnp.exp(score)
        pos_exp = jnp.exp(pos)
        total = pos_exp + jnp.sum(jnp.where(times > 0.0, times * neg_exp, 0.0), axis=0, keepdims=True)
        w_pos = live * (pos_exp / total - 1.0)
        w_neg = (live * neg_exp / total).astype(BF16).astype(F32)
        weight = jnp.where(times > 0.0, times * w_neg, 0.0) + jnp.where(is_dst, w_pos, 0.0)
        high, rest = split(weight)
        m_hi[...] = high
        m_lo[...] = rest

    def rhs_grad():
        q = q_buf[...]
        return dot(q, m_hi[...], 1, 1) + dot(q, m_lo[...], 1, 1)

    def back(turn, rhs):
        dq = dot(rhs, m_hi[...], 1, 0) + dot(rhs, m_lo[...], 1, 0)
        cols = slice(turn * SLOTS, (turn + 1) * SLOTS)
        d_re, d_im = dq[0:HALF, :], dq[HALF:D, :]
        a_re, a_im = a_buf[0:HALF, :], a_buf[HALF:D, :]
        r_re, r_im = rr_buf[0:HALF, cols], rr_buf[HALF:D, cols]
        grad_r = jnp.concatenate([d_re * a_re + d_im * a_im, d_im * a_re - d_re * a_im], axis=0)
        a_buf[...] = jnp.concatenate([d_re * r_re + d_im * r_im, d_im * r_re - d_re * r_im], axis=0)
        spot_ = pl.ds(pl.multiple_of((c * 2 + turn) * SLOTS, SLOTS), SLOTS)
        edges[0:D, spot_] = grad_r.astype(BF16)
        return send(edges.at[:, spot_], edges.at[:, spot_], sibling)

    def lhs_grad(turn):
        src = hot(src_ref[0, turn : turn + 1, :], 0, EP)
        high, rest = split(a_buf[...])
        return dot(high, src, 1, 1) + dot(rest, src, 1, 1)

    front(0, lhs_ref[...])
    weights(0, rhs_ref[...])
    new_rhs, new_rst = adagrad(rhs_ref[...], rst_ref[...], rhs_grad())
    rhs_send[...] = new_rhs
    rst_send[...] = jnp.broadcast_to(new_rst, (8, EP))
    passed = [send(rhs_send, rhs_in, after), send(rst_send, rst_in, after)]
    edges_sib = [back(0, rhs_ref[...])]
    new_lhs, new_lst = adagrad(lhs_ref[...], lst_ref[...], lhs_grad(0))
    lhs_out[...] = new_lhs
    lst_out[...] = new_lst

    front(1, lhs_out[...])

    arrived([kinds_sib])
    for core in range(2):
        for turn in range(2):
            kind = kinds[core, turn : turn + 1, :]
            shard = (kind * 64528) >> 22
            half = shard >> 1
            local = jnp.where(shard - 2 * half == c, kind - OWN * shard + ROWS * half, -1)
            at = (core * 2 + turn) * SLOTS

            def fill_mine(i, _, local=local, at=at):
                hot_mine[i // 4, pl.ds(pl.multiple_of((i % 4) * ROWS, ROWS), ROWS), at : at + SLOTS] = hot(
                    local, i * ROWS, ROWS
                )
                return 0

            lax.fori_loop(0, 16, fill_mine, 0)

    arrived(passed)
    weights(1, rhs_in[...])
    edges_sib.append(back(1, rhs_in[...]))
    arrived(edges_sib)

    def chunk(i):
        got = dot(hot_mine[i], edges[...], 1, 1)
        part[i] = got.astype(BF16).reshape(4, ROWS, WIDE)

    def x_first(i):
        chunk(i)
        return {k: send(part.at[i, flip(x, k)], x_in.at[i, k - 1], xs[k]) for k in ks}

    def y_first(i):
        chunk(i)
        return {k: send(part.at[i, :, :, lane(flip(y, k))], y_in.at[i - 2, k - 1], ys[k]) for k in ks}

    first = {0: x_first(0), 2: y_first(2), 1: x_first(1), 3: y_first(3)}

    new_rhs, new_rst = adagrad(rhs_in[...], rst_in[0:1, :], rhs_grad())
    rhs_out[...] = new_rhs
    rst_out[...] = new_rst
    new_lhs, new_lst = adagrad(lhs_out[...], lst_out[...], lhs_grad(1))
    lhs_out[...] = new_lhs
    lst_out[...] = new_lst
    for src, dst in ((lhs_out, lhs_res), (lst_out, lst_res), (rhs_out, rhs_res), (rst_out, rst_res)):
        give(src, dst)

    def x_then_y(i):
        arrived(first[i].values())
        total = part[i, x].astype(F32)
        for k in ks:
            total += x_in[i, k - 1].astype(F32)
        stage2y[i] = total.astype(BF16)
        return {k: send(stage2y.at[i, :, lane(flip(y, k))], y2_in.at[i, k - 1], ys[k]) for k in ks}

    def y_then_x(i):
        arrived(first[i].values())
        total = part[i, :, :, lane(y)].astype(F32)
        for k in ks:
            total += y_in[i - 2, k - 1].astype(F32)
        stage2x[i - 2] = total.astype(BF16)
        return {k: send(stage2x.at[i - 2, flip(x, k)], x2_in.at[i - 2, k - 1], xs[k]) for k in ks}

    second = {0: x_then_y(0), 2: y_then_x(2), 1: x_then_y(1), 3: y_then_x(3)}

    for i in (0, 2, 1, 3):
        arrived(second[i].values())
        total = (stage2y[i, :, lane(y)] if i < 2 else stage2x[i - 2, x]).astype(F32)
        for k in ks:
            total += (y2_in[i, k - 1] if i < 2 else x2_in[i - 2, k - 1]).astype(F32)
        z_out[i] = total.astype(BF16)

    za = {k: send(z_out.at[flip(zh, k)], z_in.at[k - 1], zhs[k]) for k in ks}
    arrived(za.values())
    over_zh = z_out[zh].astype(F32)
    for k in ks:
        over_zh += z_in[k - 1].astype(F32)
    low[zl] = over_zh.astype(BF16)
    zb = [send(low.at[zl], low.at[zl], zls[k]) for k in ks]
    arrived(zb)
    both_z = (low[0].astype(F32) + low[1].astype(F32)) + (low[2].astype(F32) + low[3].astype(F32))
    full[:, lane(y)] = both_z
    last = [send(full.at[:, lane(y)], full.at[:, lane(y)], ys[k]) for k in ks]
    arrived(last)

    total = full[0:OWN, 0:D]
    eye = lax.broadcasted_iota(I32, (OWN, OWN), 0) == lax.broadcasted_iota(I32, (OWN, OWN), 1)
    old = jnp.sum(jnp.where(eye, relst_ref[...], 0.0), axis=1, keepdims=True)
    new = old + jnp.sum(total * total, axis=1, keepdims=True) / D
    rel_out[...] = rel_ref[...] - LEARN * total / (jnp.sqrt(new) + EPSILON)
    relst_out[...] = jnp.sum(jnp.where(eye, new, 0.0), axis=0, keepdims=True)

    give(rel_out, rel_res)
    give(relst_out, relst_res)
    for copy in started:
        copy.wait_send()
    for copy in stores:
        copy.wait()


def hand_on(*refs):
    held, sem = refs[12:18], refs[18]
    loads = [pltpu.make_async_copy(refs[i], held[i], sem.at[i]) for i in range(6)]
    stores = [pltpu.make_async_copy(held[i], refs[6 + i], sem.at[6 + i]) for i in range(6)]
    for copy in loads:
        copy.start()
    for load, store in zip(loads, stores):
        load.wait()
        store.start()
    for copy in stores:
        copy.wait()


N_COPIES = 96


def body(
    lhs_table, lhs_state, rhs_table, rhs_state, relations, rel_state,
    src_index, dst_index, rel_index, neg_index, edge_count,
):
    hbm = pl.BlockSpec(memory_space=pltpu.HBM)
    smem = pl.BlockSpec(memory_space=pltpu.SMEM)
    shape = jax.ShapeDtypeStruct
    out_shape = (
        shape((D, EP), BF16), shape((1, EP), F32), shape((D, EP), BF16), shape((1, EP), F32),
        shape((OWN, D), F32), shape((1, OWN), F32),
    )
    outs = pl.pallas_call(
        kernel,
        out_shape=out_shape,
        in_specs=[hbm] * 10 + [smem],
        out_specs=(hbm,) * 6,
        scratch_shapes=[
            pltpu.VMEM((D, EP), BF16), pltpu.VMEM((1, EP), F32), pltpu.VMEM((D, EP), BF16), pltpu.VMEM((1, EP), F32),
            pltpu.VMEM((OWN, D), F32), pltpu.VMEM((1, OWN), F32),
            *[pltpu.VMEM((1, 2, SLOTS), I32) for _ in range(4)],
            *[pltpu.VMEM(out.shape, out.dtype) for out in out_shape],
            pltpu.VMEM((4, 4, 2, ROWS, WIDE), BF16),
            pltpu.VMEM((4, 8 * ROWS, 2 * SLOTS), BF16),
            pltpu.VMEM((4, 4 * ROWS, 4 * SLOTS), BF16),
            pltpu.VMEM((2, 8, SLOTS), I32),
            pltpu.VMEM((D, SLOTS), F32),
            pltpu.VMEM((D, 2 * SLOTS), F32),
            pltpu.VMEM((D, SLOTS), BF16),
            pltpu.VMEM((EP, SLOTS), BF16),
            pltpu.VMEM((EP, SLOTS), BF16),
            pltpu.VMEM((WIDE, 4 * SLOTS), BF16),
            pltpu.VMEM((D, EP), BF16),
            pltpu.VMEM((8, EP), F32),
            pltpu.VMEM((D, EP), BF16),
            pltpu.VMEM((8, EP), F32),
            pltpu.VMEM((4, 4, ROWS, WIDE), BF16),
            pltpu.VMEM((2, 3, ROWS, WIDE), BF16),
            pltpu.VMEM((2, 3, 4, ROWS, LANE), BF16),
            pltpu.VMEM((2, 3, ROWS, LANE), BF16),
            pltpu.VMEM((2, 3, ROWS, LANE), BF16),
            pltpu.VMEM((4, ROWS, LANE), BF16),
            pltpu.VMEM((3, ROWS, LANE), BF16),
            pltpu.VMEM((4, ROWS, LANE), BF16),
            pltpu.VMEM((ROWS, WIDE), F32),
            pltpu.VMEM((2, 4, ROWS, LANE), BF16),
            pltpu.VMEM((2, ROWS, WIDE), BF16),
            pltpu.SemaphoreType.DMA((N_COPIES,)),
            pltpu.SemaphoreType.DMA((N_COPIES,)),
            pltpu.SemaphoreType.DMA((10,)),
            pltpu.SemaphoreType.DMA((6,)),
        ],
        compiler_params=pltpu.CompilerParams(
            collective_id=0, has_side_effects=True, vmem_limit_bytes=60 * 2**20
        ),
        name="train",
    )(
        lhs_table.T, lhs_state[None, :], rhs_table.T, rhs_state[None, :], relations, rel_state[None, :],
        src_index, dst_index, rel_index, neg_index, edge_count,
    )
    lhs, lhs_st, rhs, rhs_st, rel, rel_st = pl.pallas_call(
        hand_on,
        out_shape=out_shape,
        in_specs=[hbm] * 6,
        out_specs=(hbm,) * 6,
        scratch_shapes=[*[pltpu.VMEM(out.shape, out.dtype) for out in out_shape], pltpu.SemaphoreType.DMA((12,))],
        compiler_params=pltpu.CompilerParams(vmem_limit_bytes=60 * 2**20),
        name="hand_on",
    )(*outs)
    return (lhs.T, lhs_st[0], rhs.T, rhs_st[0], rel, rel_st[0])


def solution(mesh):
    return jax.shard_map(
        body,
        mesh=mesh,
        in_specs=(
            P(("grp", "dev"), None),
            P(("grp", "dev")),
            P(("grp", "dev"), None),
            P(("grp", "dev")),
            P("dev", None),
            P("dev"),
            P(("grp", "dev"), None, None),
            P(("grp", "dev"), None, None),
            P(("grp", "dev"), None, None),
            P(("grp", "dev"), None, None),
            P(("grp", "dev"), None),
        ),
        out_specs=(
            P(("grp", "dev"), None),
            P(("grp", "dev")),
            P(("grp", "dev"), None),
            P(("grp", "dev")),
            P("dev", None),
            P("dev"),
        ),
        check_vma=False,
    )
```

```python
import functools

import jax
import jax.numpy as jnp
from jax import lax
from jax.experimental import pallas as pl
from jax.experimental.pallas import tpu as pltpu
from jax.sharding import PartitionSpec as P

LEARN = 0.1
EPSILON = 1e-06
MESH = pl.DeviceIdType.MESH
F32, BF16, I32 = jnp.float32, jnp.bfloat16, jnp.int32

D = 400
HALF = 200
WIDE = 512
OWN = 65
ROWS = 64
MAIN = 384
EP = 128
SLOTS = 512
LANE = 128


def flip(value, k):
    if k == 1:
        return value + 1 - 2 * (value % 2)
    if k == 3:
        return 3 - value
    return (value + 2) % 4


def dot(a, b, ca, cb):
    return lax.dot_general(a, b, (((ca,), (cb,)), ((), ())), preferred_element_type=F32)


def hot(index, first, count):
    rows = lax.broadcasted_iota(I32, (count, index.shape[1]), 0) + first
    return jnp.where(rows == index, 1.0, 0.0).astype(BF16)


def split(value):
    high = value.astype(BF16)
    return high, (value - high.astype(F32)).astype(BF16)


def fold(tail):
    total = tail[0:8]
    for i in range(1, 8):
        total += pltpu.roll(tail[8 * i : 8 * i + 8], 16 * i, 1)
    return total


def unfold(folded, shards):
    flat = folded.reshape(shards * 8, LANE)
    groups = [flat if i == 0 else pltpu.roll(flat, LANE - 16 * i, 1) for i in range(8)]
    return jnp.stack([group.reshape(shards, 8, LANE) for group in groups], axis=1).reshape(shards, ROWS, LANE)


def place_of(kind):
    shard = (kind * 64528) >> 22
    return shard, kind - OWN * shard


def adagrad(rows, state, grad):
    new_state = state + jnp.sum(grad * grad, axis=0, keepdims=True) / D
    moved = rows.astype(F32) - LEARN * grad / (jnp.sqrt(new_state) + EPSILON)
    return moved.astype(BF16), new_state


def kernel(
    lhs_hbm, lst_hbm, rhs_hbm, rst_hbm, rel_hbm, relst_hbm, src_hbm, dst_hbm, kind_hbm, neg_hbm, count_ref,
    lhs_res, lst_res, rhs_res, rst_res, rel_res, relst_res,
    lhs_ref, lst_ref, rhs_ref, rst_ref, rel_ref, relst_ref, src_ref, dst_ref, kind_ref, neg_ref,
    lhs_out, lst_out, rhs_out, rst_out, rel_out, relst_out,
    table, left, spare, hot_all, hot_spare, hot_mine, hot_mine_spare, kinds, wide, a_buf, rr_buf, q_buf, m_hi, m_lo, edges,
    rhs_send, rst_send, rhs_in, rst_in, part, part_left, l_in, l_y, x_in, y_in, x2_in, y2_in, z_out, z_in, low, full, stage2x, stage2y,
    send_sem, recv_sem, in_sem, out_sem,
):
    grp, dev = lax.axis_index("grp"), lax.axis_index("dev")
    y, zl = grp // 4, grp % 4
    zh, x, c = dev // 8, (dev // 2) % 4, dev % 2

    def place(x_=None, y_=None, zh_=None, zl_=None, c_=None):
        x_ = x if x_ is None else x_
        y_ = y if y_ is None else y_
        zh_ = zh if zh_ is None else zh_
        zl_ = zl if zl_ is None else zl_
        c_ = c if c_ is None else c_
        return (y_ * 4 + zl_, zh_ * 8 + x_ * 2 + c_)

    sibling = place(c_=1 - c)
    after = (grp, (dev + 1) % 32)
    ks = (1, 3, 2)
    xs = {k: place(x_=flip(x, k)) for k in ks}
    ys = {k: place(y_=flip(y, k)) for k in ks}
    zhs = {k: place(zh_=flip(zh, k)) for k in ks}
    zls = {k: place(zl_=flip(zl, k)) for k in ks}

    barrier = pltpu.get_barrier_semaphore()
    greet = [sibling, *xs.values(), *ys.values(), zhs[1], zhs[3], *zls.values()]
    for other in greet:
        pl.semaphore_signal(barrier, inc=1, device_id=other, device_id_type=MESH)

    loads = [
        pltpu.make_async_copy(src, dst, in_sem.at[i])
        for i, (src, dst) in enumerate(
            (
                (rel_hbm, rel_ref), (kind_hbm, kind_ref), (lhs_hbm, lhs_ref), (src_hbm, src_ref), (rhs_hbm, rhs_ref),
                (dst_hbm, dst_ref), (neg_hbm, neg_ref), (lst_hbm, lst_ref), (rst_hbm, rst_ref), (relst_hbm, relst_ref),
            )
        )
    ]
    for copy in loads:
        copy.start()
    started, stores = [], []

    def give(src, dst):
        copy = pltpu.make_async_copy(src, dst, out_sem.at[len(stores)])
        copy.start()
        stores.append(copy)

    def send(src, dst, target):
        i = len(started)
        copy = pltpu.make_async_remote_copy(
            src_ref=src, dst_ref=dst, send_sem=send_sem.at[i], recv_sem=recv_sem.at[i],
            device_id=target, device_id_type=MESH,
        )
        copy.start()
        started.append(copy)
        return copy

    def arrived(copies):
        for copy in copies:
            copy.wait_recv()

    def rows(value):
        return pl.ds(pl.multiple_of(value * 16, 16), 16)

    own_slots = pl.ds(pl.multiple_of(c * 2 * SLOTS, 2 * SLOTS), 2 * SLOTS)
    edges[D:WIDE, own_slots] = jnp.zeros((WIDE - D, 2 * SLOTS), BF16)
    wide[...] = jnp.zeros(wide.shape, F32)
    for copy in loads[:2]:
        copy.wait()
    wide[0:OWN, 0:D] = rel_ref[...]
    table[zh, x, c] = wide[0:ROWS, :].astype(BF16)
    last_row = [wide[ROWS:OWN, LANE * i : LANE * i + LANE] for i in range(4)]
    left[zh, x, c] = jnp.concatenate(
        [fold(wide[0:ROWS, MAIN:WIDE]), *last_row, jnp.zeros((4, LANE), F32)], axis=0
    ).astype(BF16)
    kinds[c] = jnp.concatenate([kind_ref[0], jnp.zeros((6, SLOTS), I32)], axis=0)

    pl.semaphore_wait(barrier, len(greet))

    mine, mine_left = table.at[zh, x, c, :, 0:MAIN], left.at[zh, x, c]
    quarter = table.at[zh, x, c, rows(y), 0:MAIN]
    to_zh = {k: [send(quarter, quarter, zhs[k]), send(mine_left, mine_left, zhs[k])] for k in (1, 3)}
    own_x = [send(mine, mine, xs[k]) for k in ks] + [send(mine_left, mine_left, xs[k]) for k in ks]
    kinds_sib = send(kinds.at[c], kinds.at[c], sibling)

    both = jnp.concatenate([kind_ref[0, 0:1, :], kind_ref[0, 1:2, :]], axis=1)
    shard_of, row_of = place_of(both)
    spot = jnp.where(row_of < ROWS, ROWS * shard_of + row_of, -1)
    hot_spare[...] = hot(jnp.where(row_of == ROWS, shard_of, -1), 0, 32)

    def fill(i, _):
        hot_all[i // 8, pl.ds(pl.multiple_of((i % 8) * ROWS, ROWS), ROWS), :] = hot(spot, i * ROWS, ROWS)
        return 0

    lax.fori_loop(0, 32, fill, 0)
    for copy in loads[2:]:
        copy.wait()

    def piece_of(k, lo, hi):
        return table.at[flip(zh, k), x, c, rows(y), lo:hi]

    def y_second(k, lo, hi):
        piece = table.at[flip(zh, k), :, c, rows(y), lo:hi]
        return [send(piece, piece, ys[j]) for j in ks]

    def x_second(k, lo, hi):
        piece = table.at[flip(zh, k), x, c, :, lo:hi]
        return [send(piece, piece, xs[j]) for j in ks]

    def spread(piece, targets):
        return [send(piece, piece, targets[j]) for j in ks]

    def left_of(k):
        return left.at[flip(zh, k), x, c]

    def to_sibling(where):
        piece, piece_left = table.at[where, :, c, :, 0:MAIN], left.at[where, :, c]
        return [send(piece, piece, sibling), send(piece_left, piece_left, sibling)]

    def look_up(where, first):
        folded = left[where].astype(F32).reshape(8, 16, LANE)
        table[where, :, :, :, MAIN:WIDE] = unfold(folded[:, 0:8], 8).astype(BF16).reshape(4, 2, ROWS, LANE)
        for shard in range(8):
            for i in range(4):
                spare[where, shard : shard + 1, LANE * i : LANE * i + LANE] = folded[shard, 8 + i : 9 + i]
        got = dot(table[where].reshape(8 * ROWS, WIDE)[:, 0:D], hot_all[where], 0, 0)
        if first:
            rr_buf[...] = got
        else:
            rr_buf[...] += got

    cut = 256
    arrived(to_zh[1])
    one_a = spread(piece_of(1, 0, MAIN), ys)
    one_left = spread(left_of(1), xs)
    piece = piece_of(1, 0, cut)
    relay_x = [send(piece, piece, zhs[3])]
    arrived(to_zh[3])
    three_a = spread(piece_of(3, 0, MAIN), xs)
    three_left = spread(left_of(3), xs)
    piece = piece_of(3, cut, MAIN)
    relay_y = [send(piece, piece, zhs[1]), send(left_of(3), left_of(3), zhs[1])]
    arrived(own_x)
    sib_own = to_sibling(zh)
    arrived(relay_x)
    two_x = spread(piece_of(2, 0, cut), xs)
    arrived(relay_y)
    two_y = spread(piece_of(2, cut, MAIN), ys)
    two_left = spread(left_of(2), xs)
    arrived(one_a)
    one_b = x_second(1, 0, MAIN)
    arrived(three_a)
    three_b = y_second(3, 0, MAIN)
    arrived(sib_own)
    look_up(zh, True)
    arrived(two_x)
    two_xb = y_second(2, 0, cut)
    arrived(two_y)
    two_yb = x_second(2, cut, MAIN)
    arrived(one_left)
    arrived(one_b)
    sib_one = to_sibling(flip(zh, 1))
    arrived(three_left)
    arrived(three_b)
    sib_three = to_sibling(flip(zh, 3))
    arrived(sib_one)
    look_up(flip(zh, 1), False)
    arrived(two_left)
    arrived(two_xb)
    arrived(two_yb)
    sib_two = to_sibling(flip(zh, 2))
    arrived(sib_three)
    look_up(flip(zh, 3), False)
    arrived(sib_two)
    look_up(flip(zh, 2), False)
    rr_buf[...] += dot(spare[...].reshape(32, WIDE)[:, 0:D].astype(BF16), hot_spare[...], 0, 0)

    def front(turn, lhs):
        src = hot(src_ref[0, turn : turn + 1, :], 0, EP)
        a_buf[...] = dot(lhs, src, 1, 0)
        cols = slice(turn * SLOTS, (turn + 1) * SLOTS)
        a_re, a_im = a_buf[0:HALF, :], a_buf[HALF:D, :]
        r_re, r_im = rr_buf[0:HALF, cols], rr_buf[HALF:D, cols]
        q_buf[...] = jnp.concatenate([a_re * r_re - a_im * r_im, a_re * r_im + a_im * r_re], axis=0).astype(BF16)

    def weights(turn, rhs):
        score = dot(rhs, q_buf[...], 0, 0)
        dst = dst_ref[0, turn : turn + 1, :]
        is_dst = lax.broadcasted_iota(I32, (EP, SLOTS), 0) == dst
        drawn = hot(neg_ref[0, turn : turn + 1, :], 0, EP)
        times = jnp.sum(drawn.astype(F32), axis=1, keepdims=True)
        pos = jnp.sum(jnp.where(is_dst, score, 0.0), axis=0, keepdims=True)
        live = jnp.where(
            lax.broadcasted_iota(I32, (1, SLOTS), 1) < count_ref[0, turn], 1.0, 0.0
        )
        neg_exp = jnp.exp(score)
        pos_exp = jnp.exp(pos)
        total = pos_exp + jnp.sum(jnp.where(times > 0.0, times * neg_exp, 0.0), axis=0, keepdims=True)
        w_pos = live * (pos_exp / total - 1.0)
        w_neg = (live * neg_exp / total).astype(BF16).astype(F32)
        weight = jnp.where(times > 0.0, times * w_neg, 0.0) + jnp.where(is_dst, w_pos, 0.0)
        high, rest = split(weight)
        m_hi[...] = high
        m_lo[...] = rest

    def rhs_grad():
        q = q_buf[...]
        return dot(q, m_hi[...], 1, 1) + dot(q, m_lo[...], 1, 1)

    def back(turn, rhs):
        dq = dot(rhs, m_hi[...], 1, 0) + dot(rhs, m_lo[...], 1, 0)
        cols = slice(turn * SLOTS, (turn + 1) * SLOTS)
        d_re, d_im = dq[0:HALF, :], dq[HALF:D, :]
        a_re, a_im = a_buf[0:HALF, :], a_buf[HALF:D, :]
        r_re, r_im = rr_buf[0:HALF, cols], rr_buf[HALF:D, cols]
        grad_r = jnp.concatenate([d_re * a_re + d_im * a_im, d_im * a_re - d_re * a_im], axis=0)
        a_buf[...] = jnp.concatenate([d_re * r_re + d_im * r_im, d_im * r_re - d_re * r_im], axis=0)
        spot_ = pl.ds(pl.multiple_of((c * 2 + turn) * SLOTS, SLOTS), SLOTS)
        edges[0:D, spot_] = grad_r.astype(BF16)
        return send(edges.at[:, spot_], edges.at[:, spot_], sibling)

    def lhs_grad(turn):
        src = hot(src_ref[0, turn : turn + 1, :], 0, EP)
        high, rest = split(a_buf[...])
        return dot(high, src, 1, 1) + dot(rest, src, 1, 1)

    front(0, lhs_ref[...])
    weights(0, rhs_ref[...])
    new_rhs, new_rst = adagrad(rhs_ref[...], rst_ref[...], rhs_grad())
    rhs_send[...] = new_rhs
    rst_send[...] = jnp.broadcast_to(new_rst, (8, EP))
    passed = [send(rhs_send, rhs_in, after), send(rst_send, rst_in, after)]
    edges_sib = [back(0, rhs_ref[...])]
    new_lhs, new_lst = adagrad(lhs_ref[...], lst_ref[...], lhs_grad(0))
    lhs_out[...] = new_lhs
    lst_out[...] = new_lst

    front(1, lhs_out[...])

    arrived([kinds_sib])
    for core in range(2):
        for turn in range(2):
            kind = kinds[core, turn : turn + 1, :]
            shard, row = place_of(kind)
            half = shard >> 1
            ours = shard - 2 * half == c
            local = jnp.where(ours & (row < ROWS), ROWS * half + row, -1)
            at = (core * 2 + turn) * SLOTS

            hot_mine_spare[:, at : at + SLOTS] = hot(jnp.where(ours & (row == ROWS), half, -1), 0, 16)

            def fill_mine(i, _, local=local, at=at):
                hot_mine[i // 4, pl.ds(pl.multiple_of((i % 4) * ROWS, ROWS), ROWS), at : at + SLOTS] = hot(
                    local, i * ROWS, ROWS
                )
                return 0

            lax.fori_loop(0, 16, fill_mine, 0)

    arrived(passed)
    weights(1, rhs_in[...])
    edges_sib.append(back(1, rhs_in[...]))
    arrived(edges_sib)

    last_rows = dot(hot_mine_spare[...], edges[...], 1, 1)

    def chunk(i):
        got = dot(hot_mine[i], edges[...], 1, 1)
        part[i] = got[:, 0:MAIN].astype(BF16).reshape(4, ROWS, MAIN)
        for j in range(4):
            at = 4 * i + j
            spare_rows = [last_rows[at : at + 1, LANE * q : LANE * q + LANE] for q in range(4)]
            part_left[i, j] = jnp.concatenate(
                [fold(got[ROWS * j : ROWS * j + ROWS, MAIN:WIDE]), *spare_rows, jnp.zeros((4, LANE), F32)], axis=0
            ).astype(BF16)

    def x_first(i):
        chunk(i)
        return {k: send(part.at[i, flip(x, k)], x_in.at[i, k - 1], xs[k]) for k in ks}

    def y_first(i):
        chunk(i)
        return {k: send(part.at[i, :, rows(flip(y, k))], y_in.at[i - 2, k - 1], ys[k]) for k in ks}

    first = {0: x_first(0), 2: y_first(2), 1: x_first(1), 3: y_first(3)}
    first_left = {k: send(part_left.at[:, flip(x, k)], l_in.at[k - 1], xs[k]) for k in ks}

    new_rhs, new_rst = adagrad(rhs_in[...], rst_in[0:1, :], rhs_grad())
    rhs_out[...] = new_rhs
    rst_out[...] = new_rst
    new_lhs, new_lst = adagrad(lhs_out[...], lst_out[...], lhs_grad(1))
    lhs_out[...] = new_lhs
    lst_out[...] = new_lst
    for src, dst in ((lhs_out, lhs_res), (lst_out, lst_res), (rhs_out, rhs_res), (rst_out, rst_res)):
        give(src, dst)

    def x_then_y(i):
        arrived(first[i].values())
        total = part[i, x].astype(F32)
        for k in ks:
            total += x_in[i, k - 1].astype(F32)
        stage2y[i] = total.astype(BF16)
        return {k: send(stage2y.at[i, rows(flip(y, k))], y2_in.at[i, k - 1], ys[k]) for k in ks}

    def y_then_x(i):
        arrived(first[i].values())
        total = part[i, :, rows(y)].astype(F32)
        for k in ks:
            total += y_in[i - 2, k - 1].astype(F32)
        stage2x[i - 2] = total.astype(BF16)
        return {k: send(stage2x.at[i - 2, flip(x, k)], x2_in.at[i - 2, k - 1], xs[k]) for k in ks}

    second = {0: x_then_y(0), 2: y_then_x(2), 1: x_then_y(1), 3: y_then_x(3)}

    arrived(first_left.values())
    sum_left = part_left[:, x].astype(F32)
    for k in ks:
        sum_left += l_in[k - 1].astype(F32)
    l_y[y] = sum_left.astype(BF16)
    second_left = [send(l_y.at[y], l_y.at[y], ys[k]) for k in ks]

    for i in (0, 2, 1, 3):
        arrived(second[i].values())
        total = (stage2y[i, rows(y)] if i < 2 else stage2x[i - 2, x]).astype(F32)
        for k in ks:
            total += (y2_in[i, k - 1] if i < 2 else x2_in[i - 2, k - 1]).astype(F32)
        z_out[i, :, 0:MAIN] = total.astype(BF16)
    arrived(second_left)
    all_left = (l_y[0].astype(F32) + l_y[1].astype(F32)) + (l_y[2].astype(F32) + l_y[3].astype(F32))
    z_out[:, :, MAIN:WIDE] = all_left.astype(BF16)

    za = {k: send(z_out.at[flip(zh, k)], z_in.at[k - 1], zhs[k]) for k in ks}
    arrived(za.values())
    over_zh = z_out[zh].astype(F32)
    for k in ks:
        over_zh += z_in[k - 1].astype(F32)
    low[zl] = over_zh.astype(BF16)
    zb = [send(low.at[zl], low.at[zl], zls[k]) for k in ks]
    arrived(zb)
    both_z = (low[0].astype(F32) + low[1].astype(F32)) + (low[2].astype(F32) + low[3].astype(F32))
    full[rows(y), 0:MAIN] = both_z[:, 0:MAIN]
    last = [send(full.at[rows(y), 0:MAIN], full.at[rows(y), 0:MAIN], ys[k]) for k in ks]
    wide[0:ROWS, MAIN:WIDE] = unfold(both_z[0:8, MAIN:WIDE].reshape(1, 8, LANE), 1)[0]
    for i in range(4):
        wide[ROWS:OWN, LANE * i : LANE * i + LANE] = both_z[8 + i : 9 + i, MAIN:WIDE]
    arrived(last)
    wide[0:ROWS, 0:MAIN] = full[...]

    total = wide[0:OWN, 0:D]
    eye = lax.broadcasted_iota(I32, (OWN, OWN), 0) == lax.broadcasted_iota(I32, (OWN, OWN), 1)
    old = jnp.sum(jnp.where(eye, relst_ref[...], 0.0), axis=1, keepdims=True)
    new = old + jnp.sum(total * total, axis=1, keepdims=True) / D
    rel_out[...] = rel_ref[...] - LEARN * total / (jnp.sqrt(new) + EPSILON)
    relst_out[...] = jnp.sum(jnp.where(eye, new, 0.0), axis=0, keepdims=True)

    give(rel_out, rel_res)
    give(relst_out, relst_res)
    for copy in started:
        copy.wait_send()
    for copy in stores:
        copy.wait()


def hand_on(*refs):
    held, sem = refs[12:18], refs[18]
    loads = [pltpu.make_async_copy(refs[i], held[i], sem.at[i]) for i in range(6)]
    stores = [pltpu.make_async_copy(held[i], refs[6 + i], sem.at[6 + i]) for i in range(6)]
    for copy in loads:
        copy.start()
    for load, store in zip(loads, stores):
        load.wait()
        store.start()
    for copy in stores:
        copy.wait()


N_COPIES = 112


def body(
    lhs_table, lhs_state, rhs_table, rhs_state, relations, rel_state,
    src_index, dst_index, rel_index, neg_index, edge_count,
):
    hbm = pl.BlockSpec(memory_space=pltpu.HBM)
    smem = pl.BlockSpec(memory_space=pltpu.SMEM)
    shape = jax.ShapeDtypeStruct
    out_shape = (
        shape((D, EP), BF16), shape((1, EP), F32), shape((D, EP), BF16), shape((1, EP), F32),
        shape((OWN, D), F32), shape((1, OWN), F32),
    )
    outs = pl.pallas_call(
        kernel,
        out_shape=out_shape,
        in_specs=[hbm] * 10 + [smem],
        out_specs=(hbm,) * 6,
        scratch_shapes=[
            pltpu.VMEM((D, EP), BF16), pltpu.VMEM((1, EP), F32), pltpu.VMEM((D, EP), BF16), pltpu.VMEM((1, EP), F32),
            pltpu.VMEM((OWN, D), F32), pltpu.VMEM((1, OWN), F32),
            *[pltpu.VMEM((1, 2, SLOTS), I32) for _ in range(4)],
            *[pltpu.VMEM(out.shape, out.dtype) for out in out_shape],
            pltpu.VMEM((4, 4, 2, ROWS, WIDE), BF16),
            pltpu.VMEM((4, 4, 2, 16, LANE), BF16),
            pltpu.VMEM((4, 8, WIDE), F32),
            pltpu.VMEM((4, 8 * ROWS, 2 * SLOTS), BF16),
            pltpu.VMEM((32, 2 * SLOTS), BF16),
            pltpu.VMEM((4, 4 * ROWS, 4 * SLOTS), BF16),
            pltpu.VMEM((16, 4 * SLOTS), BF16),
            pltpu.VMEM((2, 8, SLOTS), I32),
            pltpu.VMEM((72, WIDE), F32),
            pltpu.VMEM((D, SLOTS), F32),
            pltpu.VMEM((D, 2 * SLOTS), F32),
            pltpu.VMEM((D, SLOTS), BF16),
            pltpu.VMEM((EP, SLOTS), BF16),
            pltpu.VMEM((EP, SLOTS), BF16),
            pltpu.VMEM((WIDE, 4 * SLOTS), BF16),
            pltpu.VMEM((D, EP), BF16),
            pltpu.VMEM((8, EP), F32),
            pltpu.VMEM((D, EP), BF16),
            pltpu.VMEM((8, EP), F32),
            pltpu.VMEM((4, 4, ROWS, MAIN), BF16),
            pltpu.VMEM((4, 4, 16, LANE), BF16),
            pltpu.VMEM((3, 4, 16, LANE), BF16),
            pltpu.VMEM((4, 4, 16, LANE), BF16),
            pltpu.VMEM((2, 3, ROWS, MAIN), BF16),
            pltpu.VMEM((2, 3, 4, 16, MAIN), BF16),
            pltpu.VMEM((2, 3, 16, MAIN), BF16),
            pltpu.VMEM((2, 3, 16, MAIN), BF16),
            pltpu.VMEM((4, 16, WIDE), BF16),
            pltpu.VMEM((3, 16, WIDE), BF16),
            pltpu.VMEM((4, 16, WIDE), BF16),
            pltpu.VMEM((ROWS, MAIN), F32),
            pltpu.VMEM((2, 4, 16, MAIN), BF16),
            pltpu.VMEM((2, ROWS, MAIN), BF16),
            pltpu.SemaphoreType.DMA((N_COPIES,)),
            pltpu.SemaphoreType.DMA((N_COPIES,)),
            pltpu.SemaphoreType.DMA((10,)),
            pltpu.SemaphoreType.DMA((6,)),
        ],
        compiler_params=pltpu.CompilerParams(
            collective_id=0, has_side_effects=True, vmem_limit_bytes=60 * 2**20
        ),
        name="train",
    )(
        lhs_table.T, lhs_state[None, :], rhs_table.T, rhs_state[None, :], relations, rel_state[None, :],
        src_index, dst_index, rel_index, neg_index, edge_count,
    )
    lhs, lhs_st, rhs, rhs_st, rel, rel_st = pl.pallas_call(
        hand_on,
        out_shape=out_shape,
        in_specs=[hbm] * 6,
        out_specs=(hbm,) * 6,
        scratch_shapes=[*[pltpu.VMEM(out.shape, out.dtype) for out in out_shape], pltpu.SemaphoreType.DMA((12,))],
        compiler_params=pltpu.CompilerParams(vmem_limit_bytes=60 * 2**20),
        name="hand_on",
    )(*outs)
    return (lhs.T, lhs_st[0], rhs.T, rhs_st[0], rel, rel_st[0])


def solution(mesh):
    return jax.shard_map(
        body,
        mesh=mesh,
        in_specs=(
            P(("grp", "dev"), None),
            P(("grp", "dev")),
            P(("grp", "dev"), None),
            P(("grp", "dev")),
            P("dev", None),
            P("dev"),
            P(("grp", "dev"), None, None),
            P(("grp", "dev"), None, None),
            P(("grp", "dev"), None, None),
            P(("grp", "dev"), None, None),
            P(("grp", "dev"), None),
        ),
        out_specs=(
            P(("grp", "dev"), None),
            P(("grp", "dev")),
            P(("grp", "dev"), None),
            P(("grp", "dev")),
            P("dev", None),
            P("dev"),
        ),
        check_vma=False,
    )
```

```python
import functools

import jax
import jax.numpy as jnp
from jax import lax
from jax.experimental import pallas as pl
from jax.experimental.pallas import tpu as pltpu
from jax.sharding import PartitionSpec as P

LEARN = 0.1
EPSILON = 1e-06
MESH = pl.DeviceIdType.MESH
F32, BF16, I32 = jnp.float32, jnp.bfloat16, jnp.int32

D = 400
HALF = 200
WIDE = 512
OWN = 65
ROWS = 64
MAIN = 384
EP = 128
SLOTS = 512
LANE = 128


def flip(value, k):
    if k == 1:
        return value + 1 - 2 * (value % 2)
    if k == 3:
        return 3 - value
    return (value + 2) % 4


def dot(a, b, ca, cb):
    return lax.dot_general(a, b, (((ca,), (cb,)), ((), ())), preferred_element_type=F32)


def hot(index, first, count):
    rows = lax.broadcasted_iota(I32, (count, index.shape[1]), 0) + first
    return jnp.where(rows == index, 1.0, 0.0).astype(BF16)


def split(value):
    high = value.astype(BF16)
    return high, (value - high.astype(F32)).astype(BF16)


def fold(tail):
    total = tail[0:8]
    for i in range(1, 8):
        total += pltpu.roll(tail[8 * i : 8 * i + 8], 16 * i, 1)
    return total


def unfold(folded, shards):
    flat = folded.reshape(shards * 8, LANE)
    groups = [flat if i == 0 else pltpu.roll(flat, LANE - 16 * i, 1) for i in range(8)]
    return jnp.stack([group.reshape(shards, 8, LANE) for group in groups], axis=1).reshape(shards, ROWS, LANE)


def place_of(kind):
    shard = (kind * 64528) >> 22
    return shard, kind - OWN * shard


def adagrad(rows, state, grad):
    new_state = state + jnp.sum(grad * grad, axis=0, keepdims=True) / D
    moved = rows.astype(F32) - LEARN * grad / (jnp.sqrt(new_state) + EPSILON)
    return moved.astype(BF16), new_state


def kernel(
    lhs_hbm, lst_hbm, rhs_hbm, rst_hbm, rel_hbm, relst_hbm, src_hbm, dst_hbm, kind_hbm, neg_hbm, count_ref,
    lhs_res, lst_res, rhs_res, rst_res, rel_res, relst_res,
    lhs_ref, lst_ref, rhs_ref, rst_ref, rel_ref, relst_ref, src_ref, dst_ref, kind_ref, neg_ref,
    lhs_out, lst_out, rhs_out, rst_out, rel_out, relst_out,
    times_buf, row_sums, table, left, spare, hot_all, hot_spare, hot_mine, hot_mine_spare, kinds, wide, a_buf, rr_buf, q_buf, m_hi, m_lo, edges,
    rhs_send, rst_send, rhs_in, rst_in, part, part_left, l_in, l_y, x_in, y_in, x2_in, y2_in, z_out, z_in, low, full, stage2x, stage2y,
    send_sem, recv_sem, in_sem, out_sem,
):
    grp, dev = lax.axis_index("grp"), lax.axis_index("dev")
    y, zl = grp // 4, grp % 4
    zh, x, c = dev // 8, (dev // 2) % 4, dev % 2

    def place(x_=None, y_=None, zh_=None, zl_=None, c_=None):
        x_ = x if x_ is None else x_
        y_ = y if y_ is None else y_
        zh_ = zh if zh_ is None else zh_
        zl_ = zl if zl_ is None else zl_
        c_ = c if c_ is None else c_
        return (y_ * 4 + zl_, zh_ * 8 + x_ * 2 + c_)

    sibling = place(c_=1 - c)
    after = (grp, (dev + 1) % 32)
    ks = (1, 3, 2)
    xs = {k: place(x_=flip(x, k)) for k in ks}
    ys = {k: place(y_=flip(y, k)) for k in ks}
    zhs = {k: place(zh_=flip(zh, k)) for k in ks}
    zls = {k: place(zl_=flip(zl, k)) for k in ks}

    barrier = pltpu.get_barrier_semaphore()
    greet = [sibling, *xs.values(), *ys.values(), zhs[1], zhs[3], *zls.values()]
    for other in greet:
        pl.semaphore_signal(barrier, inc=1, device_id=other, device_id_type=MESH)

    loads = [
        pltpu.make_async_copy(src, dst, in_sem.at[i])
        for i, (src, dst) in enumerate(
            (
                (rel_hbm, rel_ref), (kind_hbm, kind_ref), (lhs_hbm, lhs_ref), (src_hbm, src_ref), (rhs_hbm, rhs_ref),
                (dst_hbm, dst_ref), (neg_hbm, neg_ref), (lst_hbm, lst_ref), (rst_hbm, rst_ref), (relst_hbm, relst_ref),
            )
        )
    ]
    for copy in loads[:2]:
        copy.start()
    started, stores = [], []

    def give(src, dst):
        copy = pltpu.make_async_copy(src, dst, out_sem.at[len(stores)])
        copy.start()
        stores.append(copy)

    def send(src, dst, target):
        i = len(started)
        copy = pltpu.make_async_remote_copy(
            src_ref=src, dst_ref=dst, send_sem=send_sem.at[i], recv_sem=recv_sem.at[i],
            device_id=target, device_id_type=MESH,
        )
        copy.start()
        started.append(copy)
        return copy

    def arrived(copies):
        for copy in copies:
            copy.wait_recv()

    def rows(value):
        return pl.ds(pl.multiple_of(value * 16, 16), 16)

    def slot(turn):
        return pl.ds(pl.multiple_of((turn * 2 + c) * SLOTS, SLOTS), SLOTS)

    for turn in range(2):
        edges[D:WIDE, slot(turn)] = jnp.zeros((WIDE - D, SLOTS), BF16)
    wide[...] = jnp.zeros(wide.shape, F32)
    for copy in loads[:2]:
        copy.wait()
    wide[0:OWN, 0:D] = rel_ref[...]
    table[zh, x, c] = wide[0:ROWS, :].astype(BF16)
    last_row = [wide[ROWS:OWN, LANE * i : LANE * i + LANE] for i in range(4)]
    left[zh, x, c] = jnp.concatenate(
        [fold(wide[0:ROWS, MAIN:WIDE]), *last_row, jnp.zeros((4, LANE), F32)], axis=0
    ).astype(BF16)
    kinds[c] = jnp.concatenate([kind_ref[0], jnp.zeros((6, SLOTS), I32)], axis=0)

    pl.semaphore_wait(barrier, len(greet))

    mine, mine_left = table.at[zh, x, c, :, 0:MAIN], left.at[zh, x, c]
    quarter = table.at[zh, x, c, rows(y), 0:MAIN]
    to_zh = {k: [send(quarter, quarter, zhs[k]), send(mine_left, mine_left, zhs[k])] for k in (1, 3)}
    own_x = [send(mine, mine, xs[k]) for k in ks] + [send(mine_left, mine_left, xs[k]) for k in ks]
    kinds_sib = send(kinds.at[c], kinds.at[c], sibling)

    for copy in loads[2:]:
        copy.start()

    both = jnp.concatenate([kind_ref[0, 0:1, :], kind_ref[0, 1:2, :]], axis=1)
    shard_of, row_of = place_of(both)
    spot = jnp.where(row_of < ROWS, ROWS * shard_of + row_of, -1)
    hot_spare[...] = hot(jnp.where(row_of == ROWS, shard_of, -1), 0, 32)

    def fill(i, _):
        hot_all[i // 8, pl.ds(pl.multiple_of((i % 8) * ROWS, ROWS), ROWS), :] = hot(spot, i * ROWS, ROWS)
        return 0

    lax.fori_loop(0, 32, fill, 0)
    for copy in loads[2:]:
        copy.wait()

    def piece_of(k, lo, hi):
        return table.at[flip(zh, k), x, c, rows(y), lo:hi]

    def y_second(k, lo, hi):
        piece = table.at[flip(zh, k), :, c, rows(y), lo:hi]
        return [send(piece, piece, ys[j]) for j in ks]

    def x_second(k, lo, hi):
        piece = table.at[flip(zh, k), x, c, :, lo:hi]
        return [send(piece, piece, xs[j]) for j in ks]

    def spread(piece, targets):
        return [send(piece, piece, targets[j]) for j in ks]

    def left_of(k):
        return left.at[flip(zh, k), x, c]

    def to_sibling(where):
        piece, piece_left = table.at[where, :, c, :, 0:MAIN], left.at[where, :, c]
        return [send(piece, piece, sibling), send(piece_left, piece_left, sibling)]

    def look_up(where, first):
        folded = left[where].astype(F32).reshape(8, 16, LANE)
        table[where, :, :, :, MAIN:WIDE] = unfold(folded[:, 0:8], 8).astype(BF16).reshape(4, 2, ROWS, LANE)
        for shard in range(8):
            for i in range(4):
                spare[where, shard : shard + 1, LANE * i : LANE * i + LANE] = folded[shard, 8 + i : 9 + i]
        got = dot(table[where].reshape(8 * ROWS, WIDE)[:, 0:D], hot_all[where], 0, 0)
        if first:
            rr_buf[...] = got
        else:
            rr_buf[...] += got

    def source_rows(turn, lhs):
        a_buf[...] = dot(lhs, hot(src_ref[0, turn : turn + 1, :], 0, EP), 1, 0)

    cut = 256
    arrived(to_zh[1])
    piece = piece_of(1, 0, cut)
    relay_x = [send(piece, piece, zhs[3])]
    one_a = spread(piece_of(1, 0, MAIN), ys)
    arrived(to_zh[3])
    piece = piece_of(3, cut, MAIN)
    relay_y = [send(piece, piece, zhs[1]), send(left_of(3), left_of(3), zhs[1])]
    three_a = spread(piece_of(3, 0, MAIN), xs)
    one_left = spread(left_of(1), xs)
    three_left = spread(left_of(3), xs)
    arrived(own_x)
    sib_own = to_sibling(zh)
    arrived(one_a)
    one_b = x_second(1, 0, MAIN)
    arrived(three_a)
    three_b = y_second(3, 0, MAIN)
    arrived(relay_x)
    two_x = spread(piece_of(2, 0, cut), xs)
    arrived(relay_y)
    two_y = spread(piece_of(2, cut, MAIN), ys)
    two_left = spread(left_of(2), xs)
    source_rows(0, lhs_ref[...])
    for turn in range(2):
        drawn = hot(neg_ref[0, turn : turn + 1, :], 0, EP)
        times_buf[turn] = jnp.broadcast_to(jnp.sum(drawn.astype(F32), axis=1, keepdims=True), (EP, LANE))
    arrived(sib_own)
    look_up(zh, True)
    arrived(two_x)
    two_xb = y_second(2, 0, cut)
    arrived(two_y)
    two_yb = x_second(2, cut, MAIN)
    arrived(one_left)
    arrived(one_b)
    sib_one = to_sibling(flip(zh, 1))
    arrived(three_left)
    arrived(three_b)
    sib_three = to_sibling(flip(zh, 3))
    arrived(sib_one)
    look_up(flip(zh, 1), False)
    arrived(two_left)
    arrived(two_xb)
    arrived(two_yb)
    sib_two = to_sibling(flip(zh, 2))
    arrived(sib_three)
    look_up(flip(zh, 3), False)
    arrived(sib_two)
    look_up(flip(zh, 2), False)
    rr_buf[...] += dot(spare[...].reshape(32, WIDE)[:, 0:D].astype(BF16), hot_spare[...], 0, 0)

    def front(turn):
        cols = slice(turn * SLOTS, (turn + 1) * SLOTS)
        a_re, a_im = a_buf[0:HALF, :], a_buf[HALF:D, :]
        r_re, r_im = rr_buf[0:HALF, cols], rr_buf[HALF:D, cols]
        q_buf[...] = jnp.concatenate([a_re * r_re - a_im * r_im, a_re * r_im + a_im * r_re], axis=0).astype(BF16)

    def weights(turn, rhs):
        score = dot(rhs, q_buf[...], 0, 0)
        dst = dst_ref[0, turn : turn + 1, :]
        is_dst = lax.broadcasted_iota(I32, (EP, SLOTS), 0) == dst
        times = times_buf[turn, :, 0:1]
        pos = jnp.sum(jnp.where(is_dst, score, 0.0), axis=0, keepdims=True)
        live = jnp.where(
            lax.broadcasted_iota(I32, (1, SLOTS), 1) < count_ref[0, turn], 1.0, 0.0
        )
        neg_exp = jnp.exp(score)
        pos_exp = jnp.exp(pos)
        total = pos_exp + jnp.sum(jnp.where(times > 0.0, times * neg_exp, 0.0), axis=0, keepdims=True)
        w_pos = live * (pos_exp / total - 1.0)
        w_neg = (live * neg_exp / total).astype(BF16).astype(F32)
        weight = jnp.where(times > 0.0, times * w_neg, 0.0) + jnp.where(is_dst, w_pos, 0.0)
        high, rest = split(weight)
        m_hi[...] = high
        m_lo[...] = rest

    def rhs_grad():
        q = q_buf[...]
        return dot(q, m_hi[...], 1, 1) + dot(q, m_lo[...], 1, 1)

    def back(turn, rhs):
        dq = dot(rhs, m_hi[...], 1, 0) + dot(rhs, m_lo[...], 1, 0)
        cols = slice(turn * SLOTS, (turn + 1) * SLOTS)
        d_re, d_im = dq[0:HALF, :], dq[HALF:D, :]
        a_re, a_im = a_buf[0:HALF, :], a_buf[HALF:D, :]
        r_re, r_im = rr_buf[0:HALF, cols], rr_buf[HALF:D, cols]
        grad_r = jnp.concatenate([d_re * a_re + d_im * a_im, d_im * a_re - d_re * a_im], axis=0)
        edges[0:D, slot(turn)] = grad_r.astype(BF16)
        copy = send(edges.at[:, slot(turn)], edges.at[:, slot(turn)], sibling)
        a_buf[...] = jnp.concatenate([d_re * r_re + d_im * r_im, d_im * r_re - d_re * r_im], axis=0)
        return copy

    def lhs_grad(turn):
        src = hot(src_ref[0, turn : turn + 1, :], 0, EP)
        high, rest = split(a_buf[...])
        return dot(high, src, 1, 1) + dot(rest, src, 1, 1)

    front(0)
    weights(0, rhs_ref[...])
    new_rhs, new_rst = adagrad(rhs_ref[...], rst_ref[...], rhs_grad())
    rhs_send[...] = new_rhs
    rst_send[...] = jnp.broadcast_to(new_rst, (8, EP))
    passed = [send(rhs_send, rhs_in, after), send(rst_send, rst_in, after)]
    edges_sib = [back(0, rhs_ref[...])]
    new_lhs, new_lst = adagrad(lhs_ref[...], lst_ref[...], lhs_grad(0))
    lhs_out[...] = new_lhs
    lst_out[...] = new_lst

    source_rows(1, lhs_out[...])
    front(1)

    arrived([kinds_sib])
    for core in range(2):
        for turn in range(2):
            kind = kinds[core, turn : turn + 1, :]
            shard, row = place_of(kind)
            half = shard >> 1
            ours = shard - 2 * half == c
            local = jnp.where(ours & (row < ROWS), ROWS * half + row, -1)
            at = (turn * 2 + core) * SLOTS

            hot_mine_spare[:, at : at + SLOTS] = hot(jnp.where(ours & (row == ROWS), half, -1), 0, 16)

            def fill_mine(i, _, local=local, at=at):
                hot_mine[i // 4, pl.ds(pl.multiple_of((i % 4) * ROWS, ROWS), ROWS), at : at + SLOTS] = hot(
                    local, i * ROWS, ROWS
                )
                return 0

            lax.fori_loop(0, 16, fill_mine, 0)

    arrived(edges_sib)
    early, late = slice(0, 2 * SLOTS), slice(2 * SLOTS, 4 * SLOTS)
    for i in range(4):
        row_sums[i] = dot(hot_mine[i, :, early], edges[:, early], 1, 1)
    row_sums[4, 0:16] = dot(hot_mine_spare[:, early], edges[:, early], 1, 1)

    arrived(passed)
    weights(1, rhs_in[...])
    arrived([back(1, rhs_in[...])])

    last_rows = row_sums[4, 0:16] + dot(hot_mine_spare[:, late], edges[:, late], 1, 1)

    def chunk(i):
        got = row_sums[i] + dot(hot_mine[i, :, late], edges[:, late], 1, 1)
        part[i] = got[:, 0:MAIN].astype(BF16).reshape(4, ROWS, MAIN)
        for j in range(4):
            at = 4 * i + j
            spare_rows = [last_rows[at : at + 1, LANE * q : LANE * q + LANE] for q in range(4)]
            part_left[i, j] = jnp.concatenate(
                [fold(got[ROWS * j : ROWS * j + ROWS, MAIN:WIDE]), *spare_rows, jnp.zeros((4, LANE), F32)], axis=0
            ).astype(BF16)

    def x_first(i):
        chunk(i)
        return {k: send(part.at[i, flip(x, k)], x_in.at[i, k - 1], xs[k]) for k in ks}

    def y_first(i):
        chunk(i)
        return {k: send(part.at[i, :, rows(flip(y, k))], y_in.at[i - 2, k - 1], ys[k]) for k in ks}

    first = {0: x_first(0), 2: y_first(2), 1: x_first(1), 3: y_first(3)}
    first_left = {k: send(part_left.at[:, flip(x, k)], l_in.at[k - 1], xs[k]) for k in ks}

    new_rhs, new_rst = adagrad(rhs_in[...], rst_in[0:1, :], rhs_grad())
    rhs_out[...] = new_rhs
    rst_out[...] = new_rst
    new_lhs, new_lst = adagrad(lhs_out[...], lst_out[...], lhs_grad(1))
    lhs_out[...] = new_lhs
    lst_out[...] = new_lst
    for src, dst in ((lhs_out, lhs_res), (lst_out, lst_res), (rhs_out, rhs_res), (rst_out, rst_res)):
        give(src, dst)

    def x_then_y(i):
        arrived(first[i].values())
        total = part[i, x].astype(F32)
        for k in ks:
            total += x_in[i, k - 1].astype(F32)
        stage2y[i] = total.astype(BF16)
        return {k: send(stage2y.at[i, rows(flip(y, k))], y2_in.at[i, k - 1], ys[k]) for k in ks}

    def y_then_x(i):
        arrived(first[i].values())
        total = part[i, :, rows(y)].astype(F32)
        for k in ks:
            total += y_in[i - 2, k - 1].astype(F32)
        stage2x[i - 2] = total.astype(BF16)
        return {k: send(stage2x.at[i - 2, flip(x, k)], x2_in.at[i - 2, k - 1], xs[k]) for k in ks}

    second = {0: x_then_y(0), 2: y_then_x(2), 1: x_then_y(1), 3: y_then_x(3)}

    arrived(first_left.values())
    sum_left = part_left[:, x].astype(F32)
    for k in ks:
        sum_left += l_in[k - 1].astype(F32)
    l_y[y] = sum_left.astype(BF16)
    second_left = [send(l_y.at[y], l_y.at[y], ys[k]) for k in ks]

    for i in (0, 2, 1, 3):
        arrived(second[i].values())
        total = (stage2y[i, rows(y)] if i < 2 else stage2x[i - 2, x]).astype(F32)
        for k in ks:
            total += (y2_in[i, k - 1] if i < 2 else x2_in[i - 2, k - 1]).astype(F32)
        z_out[i, :, 0:MAIN] = total.astype(BF16)
    arrived(second_left)
    all_left = (l_y[0].astype(F32) + l_y[1].astype(F32)) + (l_y[2].astype(F32) + l_y[3].astype(F32))
    z_out[:, :, MAIN:WIDE] = all_left.astype(BF16)

    za = {k: send(z_out.at[flip(zh, k)], z_in.at[k - 1], zhs[k]) for k in ks}
    arrived(za.values())
    over_zh = z_out[zh].astype(F32)
    for k in ks:
        over_zh += z_in[k - 1].astype(F32)
    low[zl] = over_zh.astype(BF16)
    zb = [send(low.at[zl], low.at[zl], zls[k]) for k in ks]
    arrived(zb)
    both_z = (low[0].astype(F32) + low[1].astype(F32)) + (low[2].astype(F32) + low[3].astype(F32))
    full[rows(y), 0:MAIN] = both_z[:, 0:MAIN]
    last = [send(full.at[rows(y), 0:MAIN], full.at[rows(y), 0:MAIN], ys[k]) for k in ks]
    wide[0:ROWS, MAIN:WIDE] = unfold(both_z[0:8, MAIN:WIDE].reshape(1, 8, LANE), 1)[0]
    for i in range(4):
        wide[ROWS:OWN, LANE * i : LANE * i + LANE] = both_z[8 + i : 9 + i, MAIN:WIDE]
    arrived(last)
    wide[0:ROWS, 0:MAIN] = full[...]

    total = wide[0:OWN, 0:D]
    eye = lax.broadcasted_iota(I32, (OWN, OWN), 0) == lax.broadcasted_iota(I32, (OWN, OWN), 1)
    old = jnp.sum(jnp.where(eye, relst_ref[...], 0.0), axis=1, keepdims=True)
    new = old + jnp.sum(total * total, axis=1, keepdims=True) / D
    rel_out[...] = rel_ref[...] - LEARN * total / (jnp.sqrt(new) + EPSILON)
    relst_out[...] = jnp.sum(jnp.where(eye, new, 0.0), axis=0, keepdims=True)

    give(rel_out, rel_res)
    give(relst_out, relst_res)
    for copy in started:
        copy.wait_send()
    for copy in stores:
        copy.wait()


def hand_on(*refs):
    held, sem = refs[12:18], refs[18]
    loads = [pltpu.make_async_copy(refs[i], held[i], sem.at[i]) for i in range(6)]
    stores = [pltpu.make_async_copy(held[i], refs[6 + i], sem.at[6 + i]) for i in range(6)]
    for copy in loads:
        copy.start()
    for load, store in zip(loads, stores):
        load.wait()
        store.start()
    for copy in stores:
        copy.wait()


N_COPIES = 112


def body(
    lhs_table, lhs_state, rhs_table, rhs_state, relations, rel_state,
    src_index, dst_index, rel_index, neg_index, edge_count,
):
    hbm = pl.BlockSpec(memory_space=pltpu.HBM)
    smem = pl.BlockSpec(memory_space=pltpu.SMEM)
    shape = jax.ShapeDtypeStruct
    out_shape = (
        shape((D, EP), BF16), shape((1, EP), F32), shape((D, EP), BF16), shape((1, EP), F32),
        shape((OWN, D), F32), shape((1, OWN), F32),
    )
    outs = pl.pallas_call(
        kernel,
        out_shape=out_shape,
        in_specs=[hbm] * 10 + [smem],
        out_specs=(hbm,) * 6,
        scratch_shapes=[
            pltpu.VMEM((D, EP), BF16), pltpu.VMEM((1, EP), F32), pltpu.VMEM((D, EP), BF16), pltpu.VMEM((1, EP), F32),
            pltpu.VMEM((OWN, D), F32), pltpu.VMEM((1, OWN), F32),
            *[pltpu.VMEM((1, 2, SLOTS), I32) for _ in range(4)],
            *[pltpu.VMEM(out.shape, out.dtype) for out in out_shape],
            pltpu.VMEM((2, EP, LANE), F32),
            pltpu.VMEM((5, 4 * ROWS, WIDE), F32),
            pltpu.VMEM((4, 4, 2, ROWS, WIDE), BF16),
            pltpu.VMEM((4, 4, 2, 16, LANE), BF16),
            pltpu.VMEM((4, 8, WIDE), F32),
            pltpu.VMEM((4, 8 * ROWS, 2 * SLOTS), BF16),
            pltpu.VMEM((32, 2 * SLOTS), BF16),
            pltpu.VMEM((4, 4 * ROWS, 4 * SLOTS), BF16),
            pltpu.VMEM((16, 4 * SLOTS), BF16),
            pltpu.VMEM((2, 8, SLOTS), I32),
            pltpu.VMEM((72, WIDE), F32),
            pltpu.VMEM((D, SLOTS), F32),
            pltpu.VMEM((D, 2 * SLOTS), F32),
            pltpu.VMEM((D, SLOTS), BF16),
            pltpu.VMEM((EP, SLOTS), BF16),
            pltpu.VMEM((EP, SLOTS), BF16),
            pltpu.VMEM((WIDE, 4 * SLOTS), BF16),
            pltpu.VMEM((D, EP), BF16),
            pltpu.VMEM((8, EP), F32),
            pltpu.VMEM((D, EP), BF16),
            pltpu.VMEM((8, EP), F32),
            pltpu.VMEM((4, 4, ROWS, MAIN), BF16),
            pltpu.VMEM((4, 4, 16, LANE), BF16),
            pltpu.VMEM((3, 4, 16, LANE), BF16),
            pltpu.VMEM((4, 4, 16, LANE), BF16),
            pltpu.VMEM((2, 3, ROWS, MAIN), BF16),
            pltpu.VMEM((2, 3, 4, 16, MAIN), BF16),
            pltpu.VMEM((2, 3, 16, MAIN), BF16),
            pltpu.VMEM((2, 3, 16, MAIN), BF16),
            pltpu.VMEM((4, 16, WIDE), BF16),
            pltpu.VMEM((3, 16, WIDE), BF16),
            pltpu.VMEM((4, 16, WIDE), BF16),
            pltpu.VMEM((ROWS, MAIN), F32),
            pltpu.VMEM((2, 4, 16, MAIN), BF16),
            pltpu.VMEM((2, ROWS, MAIN), BF16),
            pltpu.SemaphoreType.DMA((N_COPIES,)),
            pltpu.SemaphoreType.DMA((N_COPIES,)),
            pltpu.SemaphoreType.DMA((10,)),
            pltpu.SemaphoreType.DMA((6,)),
        ],
        compiler_params=pltpu.CompilerParams(
            collective_id=0, has_side_effects=True, vmem_limit_bytes=60 * 2**20
        ),
        name="train",
    )(
        lhs_table.T, lhs_state[None, :], rhs_table.T, rhs_state[None, :], relations, rel_state[None, :],
        src_index, dst_index, rel_index, neg_index, edge_count,
    )
    lhs, lhs_st, rhs, rhs_st, rel, rel_st = pl.pallas_call(
        hand_on,
        out_shape=out_shape,
        in_specs=[hbm] * 6,
        out_specs=(hbm,) * 6,
        scratch_shapes=[*[pltpu.VMEM(out.shape, out.dtype) for out in out_shape], pltpu.SemaphoreType.DMA((12,))],
        compiler_params=pltpu.CompilerParams(vmem_limit_bytes=60 * 2**20),
        name="hand_on",
    )(*outs)
    return (lhs.T, lhs_st[0], rhs.T, rhs_st[0], rel, rel_st[0])


def solution(mesh):
    return jax.shard_map(
        body,
        mesh=mesh,
        in_specs=(
            P(("grp", "dev"), None),
            P(("grp", "dev")),
            P(("grp", "dev"), None),
            P(("grp", "dev")),
            P("dev", None),
            P("dev"),
            P(("grp", "dev"), None, None),
            P(("grp", "dev"), None, None),
            P(("grp", "dev"), None, None),
            P(("grp", "dev"), None, None),
            P(("grp", "dev"), None),
        ),
        out_specs=(
            P(("grp", "dev"), None),
            P(("grp", "dev")),
            P(("grp", "dev"), None),
            P(("grp", "dev")),
            P("dev", None),
            P("dev"),
        ),
        check_vma=False,
    )
```

```python
import functools

import jax
import jax.numpy as jnp
from jax import lax
from jax.experimental import pallas as pl
from jax.experimental.pallas import tpu as pltpu
from jax.sharding import PartitionSpec as P

LEARN = 0.1
EPSILON = 1e-06
MESH = pl.DeviceIdType.MESH
F32, BF16, I32 = jnp.float32, jnp.bfloat16, jnp.int32

D = 400
HALF = 200
WIDE = 512
OWN = 65
ROWS = 64
MAIN = 384
EP = 128
SLOTS = 512
LANE = 128


def flip(value, k):
    if k == 1:
        return value + 1 - 2 * (value % 2)
    if k == 3:
        return 3 - value
    return (value + 2) % 4


def dot(a, b, ca, cb):
    return lax.dot_general(a, b, (((ca,), (cb,)), ((), ())), preferred_element_type=F32)


def hot(index, first, count):
    rows = lax.broadcasted_iota(I32, (count, index.shape[1]), 0) + first
    return jnp.where(rows == index, 1.0, 0.0).astype(BF16)


def split(value):
    high = value.astype(BF16)
    return high, (value - high.astype(F32)).astype(BF16)


def fold(tail):
    total = tail[0:8]
    for i in range(1, 8):
        total += pltpu.roll(tail[8 * i : 8 * i + 8], 16 * i, 1)
    return total


def unfold(folded, shards):
    flat = folded.reshape(shards * 8, LANE)
    groups = [flat if i == 0 else pltpu.roll(flat, LANE - 16 * i, 1) for i in range(8)]
    return jnp.stack([group.reshape(shards, 8, LANE) for group in groups], axis=1).reshape(shards, ROWS, LANE)


def place_of(kind):
    shard = (kind * 64528) >> 22
    return shard, kind - OWN * shard


def adagrad(rows, state, grad):
    new_state = state + jnp.sum(grad * grad, axis=0, keepdims=True) / D
    moved = rows.astype(F32) - LEARN * grad / (jnp.sqrt(new_state) + EPSILON)
    return moved.astype(BF16), new_state


def kernel(
    lhs_hbm, lst_hbm, rhs_hbm, rst_hbm, rel_hbm, relst_hbm, src_hbm, dst_hbm, kind_hbm, neg_hbm, count_hbm,
    lhs_res, lst_res, rhs_res, rst_res, rel_res, relst_res,
    lhs_ref, lst_ref, rhs_ref, rst_ref, rel_ref, relst_ref, src_ref, dst_ref, kind_ref, neg_ref, count_ref,
    lhs_out, lst_out, rhs_out, rst_out, rel_out, relst_out,
    times_buf, row_sums, table, left, spare, hot_all, hot_spare, hot_mine, hot_mine_spare, kinds, wide, a_buf, rr_buf, q_buf, m_hi, m_lo, edges,
    rhs_send, rst_send, rhs_in, rst_in, part, part_left, l_in, l_y, x_in, y_in, x2_in, y2_in, z_out, z_in, low, stage2x, stage2y,
    send_sem, recv_sem, in_sem, out_sem,
):
    grp, dev = lax.axis_index("grp"), lax.axis_index("dev")
    y, zl = grp // 4, grp % 4
    zh, x, c = dev // 8, (dev // 2) % 4, dev % 2

    def place(x_=None, y_=None, zh_=None, zl_=None, c_=None):
        x_ = x if x_ is None else x_
        y_ = y if y_ is None else y_
        zh_ = zh if zh_ is None else zh_
        zl_ = zl if zl_ is None else zl_
        c_ = c if c_ is None else c_
        return (y_ * 4 + zl_, zh_ * 8 + x_ * 2 + c_)

    sibling = place(c_=1 - c)
    after = (grp, (dev + 1) % 32)
    ks = (1, 3, 2)
    xs = {k: place(x_=flip(x, k)) for k in ks}
    ys = {k: place(y_=flip(y, k)) for k in ks}
    zhs = {k: place(zh_=flip(zh, k)) for k in ks}
    zls = {k: place(zl_=flip(zl, k)) for k in ks}

    barrier = pltpu.get_barrier_semaphore()
    greet = [sibling, *xs.values(), *ys.values(), zhs[1], zhs[3], *zls.values()]
    for other in greet:
        pl.semaphore_signal(barrier, inc=1, device_id=other, device_id_type=MESH)

    loads = [
        pltpu.make_async_copy(src, dst, in_sem.at[i])
        for i, (src, dst) in enumerate(
            (
                (rel_hbm, rel_ref), (kind_hbm, kind_ref), (lhs_hbm, lhs_ref), (src_hbm, src_ref), (rhs_hbm, rhs_ref),
                (dst_hbm, dst_ref), (neg_hbm, neg_ref), (lst_hbm, lst_ref), (rst_hbm, rst_ref), (relst_hbm, relst_ref),
                (count_hbm, count_ref),
            )
        )
    ]
    for copy in loads[:2]:
        copy.start()
    started, stores = [], []

    def give(src, dst):
        copy = pltpu.make_async_copy(src, dst, out_sem.at[len(stores)])
        copy.start()
        stores.append(copy)

    def send(src, dst, target):
        i = len(started)
        copy = pltpu.make_async_remote_copy(
            src_ref=src, dst_ref=dst, send_sem=send_sem.at[i], recv_sem=recv_sem.at[i],
            device_id=target, device_id_type=MESH,
        )
        copy.start()
        started.append(copy)
        return copy

    def arrived(copies):
        for copy in copies:
            copy.wait_recv()

    def rows(value):
        return pl.ds(pl.multiple_of(value * 16, 16), 16)

    def slot(turn):
        return pl.ds(pl.multiple_of((turn * 2 + c) * SLOTS, SLOTS), SLOTS)

    edges[D:WIDE, :] = jnp.zeros((WIDE - D, 4 * SLOTS), BF16)
    wide[...] = jnp.zeros(wide.shape, F32)
    for copy in loads[:2]:
        copy.wait()
    wide[0:OWN, 0:D] = rel_ref[...]
    table[zh, x, c] = wide[0:ROWS, :].astype(BF16)
    last_row = [wide[ROWS:OWN, LANE * i : LANE * i + LANE] for i in range(4)]
    left[zh, x, c] = jnp.concatenate(
        [fold(wide[0:ROWS, MAIN:WIDE]), *last_row, jnp.zeros((4, LANE), F32)], axis=0
    ).astype(BF16)
    kinds[c] = jnp.concatenate([kind_ref[0], jnp.zeros((6, SLOTS), I32)], axis=0)

    pl.semaphore_wait(barrier, len(greet))

    mine, mine_left = table.at[zh, x, c, :, 0:MAIN], left.at[zh, x, c]
    quarter = table.at[zh, x, c, rows(y), 0:MAIN]
    to_zh = {k: [send(quarter, quarter, zhs[k]), send(mine_left, mine_left, zhs[k])] for k in (1, 3)}
    own_x = [send(mine, mine, xs[k]) for k in ks] + [send(mine_left, mine_left, xs[k]) for k in ks]
    kinds_sib = send(kinds.at[c], kinds.at[c], sibling)

    for copy in loads[2:]:
        copy.start()

    both = jnp.concatenate([kind_ref[0, 0:1, :], kind_ref[0, 1:2, :]], axis=1)
    shard_of, row_of = place_of(both)
    spot = jnp.where(row_of < ROWS, ROWS * shard_of + row_of, -1)
    hot_spare[...] = hot(jnp.where(row_of == ROWS, shard_of, -1), 0, 32)

    def fill(i, _):
        hot_all[i // 8, pl.ds(pl.multiple_of((i % 8) * ROWS, ROWS), ROWS), :] = hot(spot, i * ROWS, ROWS)
        return 0

    lax.fori_loop(0, 32, fill, 0)
    for copy in loads[2:]:
        copy.wait()

    def piece_of(k, lo, hi):
        return table.at[flip(zh, k), x, c, rows(y), lo:hi]

    def y_second(k, lo, hi):
        piece = table.at[flip(zh, k), :, c, rows(y), lo:hi]
        return [send(piece, piece, ys[j]) for j in ks]

    def x_second(k, lo, hi):
        piece = table.at[flip(zh, k), x, c, :, lo:hi]
        return [send(piece, piece, xs[j]) for j in ks]

    def spread(piece, targets):
        return [send(piece, piece, targets[j]) for j in ks]

    def left_of(k):
        return left.at[flip(zh, k), x, c]

    def to_sibling(where):
        piece, piece_left = table.at[where, :, c, :, 0:MAIN], left.at[where, :, c]
        return [send(piece, piece, sibling), send(piece_left, piece_left, sibling)]

    def look_up(where, first):
        folded = left[where].astype(F32).reshape(8, 16, LANE)
        table[where, :, :, :, MAIN:WIDE] = unfold(folded[:, 0:8], 8).astype(BF16).reshape(4, 2, ROWS, LANE)
        for shard in range(8):
            for i in range(4):
                spare[where, shard : shard + 1, LANE * i : LANE * i + LANE] = folded[shard, 8 + i : 9 + i]
        got = dot(table[where].reshape(8 * ROWS, WIDE)[:, 0:D], hot_all[where], 0, 0)
        if first:
            rr_buf[...] = got
        else:
            rr_buf[...] += got

    def source_rows(turn, lhs):
        a_buf[...] = dot(lhs, hot(src_ref[0, turn : turn + 1, :], 0, EP), 1, 0)

    cut = 256
    arrived(to_zh[1])
    piece = piece_of(1, 0, cut)
    relay_x = [send(piece, piece, zhs[3])]
    one_a = spread(piece_of(1, 0, MAIN), ys)
    arrived(to_zh[3])
    piece = piece_of(3, cut, MAIN)
    relay_y = [send(piece, piece, zhs[1]), send(left_of(3), left_of(3), zhs[1])]
    three_a = spread(piece_of(3, 0, MAIN), xs)
    one_left = spread(left_of(1), xs)
    three_left = spread(left_of(3), xs)
    arrived(own_x)
    sib_own = to_sibling(zh)
    arrived(one_a)
    one_b = x_second(1, 0, MAIN)
    arrived(three_a)
    three_b = y_second(3, 0, MAIN)
    arrived(relay_x)
    arrived(relay_y)
    piece = piece_of(2, 0, MAIN)
    two = [send(piece, piece, place(x_=flip(x, i), y_=flip(y, j))) for i in ks for j in ks]
    two += spread(piece, xs) + spread(piece, ys) + spread(left_of(2), xs)
    source_rows(0, lhs_ref[...])
    for turn in range(2):
        drawn = hot(neg_ref[0, turn : turn + 1, :], 0, EP)
        times_buf[turn] = jnp.broadcast_to(jnp.sum(drawn.astype(F32), axis=1, keepdims=True), (EP, LANE))
    arrived(sib_own)
    look_up(zh, True)
    arrived(one_left)
    arrived(one_b)
    sib_one = to_sibling(flip(zh, 1))
    arrived(three_left)
    arrived(three_b)
    sib_three = to_sibling(flip(zh, 3))
    arrived(sib_one)
    look_up(flip(zh, 1), False)
    arrived(two)
    sib_two = to_sibling(flip(zh, 2))
    arrived(sib_three)
    look_up(flip(zh, 3), False)
    arrived(sib_two)
    look_up(flip(zh, 2), False)
    rr_buf[...] += dot(spare[...].reshape(32, WIDE)[:, 0:D].astype(BF16), hot_spare[...], 0, 0)

    def front(turn):
        cols = slice(turn * SLOTS, (turn + 1) * SLOTS)
        a_re, a_im = a_buf[0:HALF, :], a_buf[HALF:D, :]
        r_re, r_im = rr_buf[0:HALF, cols], rr_buf[HALF:D, cols]
        q_buf[...] = jnp.concatenate([a_re * r_re - a_im * r_im, a_re * r_im + a_im * r_re], axis=0).astype(BF16)

    def weights(turn, rhs):
        score = dot(rhs, q_buf[...], 0, 0)
        dst = dst_ref[0, turn : turn + 1, :]
        is_dst = lax.broadcasted_iota(I32, (EP, SLOTS), 0) == dst
        times = times_buf[turn, :, 0:1]
        pos = jnp.sum(jnp.where(is_dst, score, 0.0), axis=0, keepdims=True)
        live = jnp.where(
            lax.broadcasted_iota(I32, (1, SLOTS), 1) < count_ref[0:1, turn : turn + 1], 1.0, 0.0
        )
        neg_exp = jnp.exp(score)
        pos_exp = jnp.exp(pos)
        total = pos_exp + jnp.sum(jnp.where(times > 0.0, times * neg_exp, 0.0), axis=0, keepdims=True)
        w_pos = live * (pos_exp / total - 1.0)
        w_neg = (live * neg_exp / total).astype(BF16).astype(F32)
        weight = jnp.where(times > 0.0, times * w_neg, 0.0) + jnp.where(is_dst, w_pos, 0.0)
        high, rest = split(weight)
        m_hi[...] = high
        m_lo[...] = rest

    def rhs_grad():
        q = q_buf[...]
        return dot(q, m_hi[...], 1, 1) + dot(q, m_lo[...], 1, 1)

    def back(turn, rhs):
        dq = dot(rhs, m_hi[...], 1, 0) + dot(rhs, m_lo[...], 1, 0)
        cols = slice(turn * SLOTS, (turn + 1) * SLOTS)
        d_re, d_im = dq[0:HALF, :], dq[HALF:D, :]
        a_re, a_im = a_buf[0:HALF, :], a_buf[HALF:D, :]
        r_re, r_im = rr_buf[0:HALF, cols], rr_buf[HALF:D, cols]
        grad_r = jnp.concatenate([d_re * a_re + d_im * a_im, d_im * a_re - d_re * a_im], axis=0)
        edges[0:D, slot(turn)] = grad_r.astype(BF16)
        copy = send(edges.at[0:D, slot(turn)], edges.at[0:D, slot(turn)], sibling)
        a_buf[...] = jnp.concatenate([d_re * r_re + d_im * r_im, d_im * r_re - d_re * r_im], axis=0)
        return copy

    def lhs_grad(turn):
        src = hot(src_ref[0, turn : turn + 1, :], 0, EP)
        high, rest = split(a_buf[...])
        return dot(high, src, 1, 1) + dot(rest, src, 1, 1)

    front(0)
    weights(0, rhs_ref[...])
    new_rhs, new_rst = adagrad(rhs_ref[...], rst_ref[...], rhs_grad())
    rhs_send[...] = new_rhs
    rst_send[...] = jnp.broadcast_to(new_rst, (8, EP))
    passed = [send(rhs_send, rhs_in, after), send(rst_send, rst_in, after)]
    edges_sib = [back(0, rhs_ref[...])]
    new_lhs, new_lst = adagrad(lhs_ref[...], lst_ref[...], lhs_grad(0))
    lhs_out[...] = new_lhs
    lst_out[...] = new_lst

    source_rows(1, lhs_out[...])
    front(1)

    arrived([kinds_sib])
    for core in range(2):
        for turn in range(2):
            kind = kinds[core, turn : turn + 1, :]
            shard, row = place_of(kind)
            half = shard >> 1
            ours = shard - 2 * half == c
            local = jnp.where(ours & (row < ROWS), ROWS * half + row, -1)
            at = (turn * 2 + core) * SLOTS

            hot_mine_spare[:, at : at + SLOTS] = hot(jnp.where(ours & (row == ROWS), half, -1), 0, 16)

            def fill_mine(i, _, local=local, at=at):
                hot_mine[i // 4, pl.ds(pl.multiple_of((i % 4) * ROWS, ROWS), ROWS), at : at + SLOTS] = hot(
                    local, i * ROWS, ROWS
                )
                return 0

            lax.fori_loop(0, 16, fill_mine, 0)

    arrived(edges_sib)
    early, late = slice(0, 2 * SLOTS), slice(2 * SLOTS, 4 * SLOTS)
    for i in range(4):
        row_sums[i] = dot(hot_mine[i, :, early], edges[:, early], 1, 1)
    row_sums[4, 0:16] = dot(hot_mine_spare[:, early], edges[:, early], 1, 1)

    arrived(passed)
    weights(1, rhs_in[...])
    arrived([back(1, rhs_in[...])])

    last_rows = row_sums[4, 0:16] + dot(hot_mine_spare[:, late], edges[:, late], 1, 1)

    def chunk(i):
        got = row_sums[i] + dot(hot_mine[i, :, late], edges[:, late], 1, 1)
        part[i] = got[:, 0:MAIN].astype(BF16).reshape(4, ROWS, MAIN)
        return got[:, MAIN:WIDE]

    def fold_chunk(i, tails):
        for j in range(4):
            at = 4 * i + j
            spare_rows = [last_rows[at : at + 1, LANE * q : LANE * q + LANE] for q in range(4)]
            part_left[i, j] = jnp.concatenate(
                [fold(tails[ROWS * j : ROWS * j + ROWS]), *spare_rows, jnp.zeros((4, LANE), F32)], axis=0
            ).astype(BF16)

    def x_first(i):
        tails = chunk(i)
        copies = {k: send(part.at[i, flip(x, k)], x_in.at[i, k - 1], xs[k]) for k in ks}
        fold_chunk(i, tails)
        return copies

    def y_first(i):
        tails = chunk(i)
        copies = {k: send(part.at[i, :, rows(flip(y, k))], y_in.at[i - 2, k - 1], ys[k]) for k in ks}
        fold_chunk(i, tails)
        return copies

    first = {0: x_first(0), 2: y_first(2), 1: x_first(1), 3: y_first(3)}
    first_left = {k: send(part_left.at[:, flip(x, k)], l_in.at[k - 1], xs[k]) for k in ks}

    new_rhs, new_rst = adagrad(rhs_in[...], rst_in[0:1, :], rhs_grad())
    rhs_out[...] = new_rhs
    rst_out[...] = new_rst
    new_lhs, new_lst = adagrad(lhs_out[...], lst_out[...], lhs_grad(1))
    lhs_out[...] = new_lhs
    lst_out[...] = new_lst
    for src, dst in ((lhs_out, lhs_res), (lst_out, lst_res), (rhs_out, rhs_res), (rst_out, rst_res)):
        give(src, dst)

    def x_then_y(i):
        arrived(first[i].values())
        total = part[i, x].astype(F32)
        for k in ks:
            total += x_in[i, k - 1].astype(F32)
        stage2y[i] = total.astype(BF16)
        return {k: send(stage2y.at[i, rows(flip(y, k))], y2_in.at[i, k - 1], ys[k]) for k in ks}

    def y_then_x(i):
        arrived(first[i].values())
        total = part[i, :, rows(y)].astype(F32)
        for k in ks:
            total += y_in[i - 2, k - 1].astype(F32)
        stage2x[i - 2] = total.astype(BF16)
        return {k: send(stage2x.at[i - 2, flip(x, k)], x2_in.at[i - 2, k - 1], xs[k]) for k in ks}

    second = {0: x_then_y(0), 2: y_then_x(2), 1: x_then_y(1), 3: y_then_x(3)}

    arrived(first_left.values())
    sum_left = part_left[:, x].astype(F32)
    for k in ks:
        sum_left += l_in[k - 1].astype(F32)
    l_y[y] = sum_left.astype(BF16)
    second_left = [send(l_y.at[y], l_y.at[y], ys[k]) for k in ks]

    for i in (0, 2, 1, 3):
        arrived(second[i].values())
        total = (stage2y[i, rows(y)] if i < 2 else stage2x[i - 2, x]).astype(F32)
        for k in ks:
            total += (y2_in[i, k - 1] if i < 2 else x2_in[i - 2, k - 1]).astype(F32)
        z_out[i, :, 0:MAIN] = total.astype(BF16)
    arrived(second_left)
    all_left = (l_y[0].astype(F32) + l_y[1].astype(F32)) + (l_y[2].astype(F32) + l_y[3].astype(F32))
    z_out[:, :, MAIN:WIDE] = all_left.astype(BF16)

    za = {k: send(z_out.at[flip(zh, k)], z_in.at[k - 1], zhs[k]) for k in ks}
    arrived(za.values())
    over_zh = z_out[zh].astype(F32)
    for k in ks:
        over_zh += z_in[k - 1].astype(F32)
    low[zl] = over_zh.astype(BF16)
    zb = [send(low.at[zl], low.at[zl], zls[k]) for k in ks]
    arrived(zb)
    both_z = (low[0].astype(F32) + low[1].astype(F32)) + (low[2].astype(F32) + low[3].astype(F32))
    own_rows = wide.at[rows(y), 0:MAIN]
    own_rows[...] = both_z[:, 0:MAIN]
    last = [send(own_rows, own_rows, ys[k]) for k in ks]
    wide[0:ROWS, MAIN:WIDE] = unfold(both_z[0:8, MAIN:WIDE].reshape(1, 8, LANE), 1)[0]
    for i in range(4):
        wide[ROWS:OWN, LANE * i : LANE * i + LANE] = both_z[8 + i : 9 + i, MAIN:WIDE]
    arrived(last)

    total = wide[0:OWN, 0:D]
    eye = lax.broadcasted_iota(I32, (OWN, OWN), 0) == lax.broadcasted_iota(I32, (OWN, OWN), 1)
    old = jnp.sum(jnp.where(eye, relst_ref[...], 0.0), axis=1, keepdims=True)
    new = old + jnp.sum(total * total, axis=1, keepdims=True) / D
    rel_out[...] = rel_ref[...] - LEARN * total / (jnp.sqrt(new) + EPSILON)
    relst_out[...] = jnp.sum(jnp.where(eye, new, 0.0), axis=0, keepdims=True)

    give(rel_out, rel_res)
    give(relst_out, relst_res)
    for copy in started:
        copy.wait_send()
    for copy in stores:
        copy.wait()


def hand_on(*refs):
    held, sem = refs[12:18], refs[18]
    loads = [pltpu.make_async_copy(refs[i], held[i], sem.at[i]) for i in range(6)]
    stores = [pltpu.make_async_copy(held[i], refs[6 + i], sem.at[6 + i]) for i in range(6)]
    for copy in loads:
        copy.start()
    for load, store in zip(loads, stores):
        load.wait()
        store.start()
    for copy in stores:
        copy.wait()


N_COPIES = 112


def body(
    lhs_table, lhs_state, rhs_table, rhs_state, relations, rel_state,
    src_index, dst_index, rel_index, neg_index, edge_count,
):
    hbm = pl.BlockSpec(memory_space=pltpu.HBM)
    shape = jax.ShapeDtypeStruct
    out_shape = (
        shape((D, EP), BF16), shape((1, EP), F32), shape((D, EP), BF16), shape((1, EP), F32),
        shape((OWN, D), F32), shape((1, OWN), F32),
    )
    outs = pl.pallas_call(
        kernel,
        out_shape=out_shape,
        in_specs=[hbm] * 11,
        out_specs=(hbm,) * 6,
        scratch_shapes=[
            pltpu.VMEM((D, EP), BF16), pltpu.VMEM((1, EP), F32), pltpu.VMEM((D, EP), BF16), pltpu.VMEM((1, EP), F32),
            pltpu.VMEM((OWN, D), F32), pltpu.VMEM((1, OWN), F32),
            *[pltpu.VMEM((1, 2, SLOTS), I32) for _ in range(4)],
            pltpu.VMEM((1, 2), I32),
            *[pltpu.VMEM(out.shape, out.dtype) for out in out_shape],
            pltpu.VMEM((2, EP, LANE), F32),
            pltpu.VMEM((5, 4 * ROWS, WIDE), F32),
            pltpu.VMEM((4, 4, 2, ROWS, WIDE), BF16),
            pltpu.VMEM((4, 4, 2, 16, LANE), BF16),
            pltpu.VMEM((4, 8, WIDE), F32),
            pltpu.VMEM((4, 8 * ROWS, 2 * SLOTS), BF16),
            pltpu.VMEM((32, 2 * SLOTS), BF16),
            pltpu.VMEM((4, 4 * ROWS, 4 * SLOTS), BF16),
            pltpu.VMEM((16, 4 * SLOTS), BF16),
            pltpu.VMEM((2, 8, SLOTS), I32),
            pltpu.VMEM((72, WIDE), F32),
            pltpu.VMEM((D, SLOTS), F32),
            pltpu.VMEM((D, 2 * SLOTS), F32),
            pltpu.VMEM((D, SLOTS), BF16),
            pltpu.VMEM((EP, SLOTS), BF16),
            pltpu.VMEM((EP, SLOTS), BF16),
            pltpu.VMEM((WIDE, 4 * SLOTS), BF16),
            pltpu.VMEM((D, EP), BF16),
            pltpu.VMEM((8, EP), F32),
            pltpu.VMEM((D, EP), BF16),
            pltpu.VMEM((8, EP), F32),
            pltpu.VMEM((4, 4, ROWS, MAIN), BF16),
            pltpu.VMEM((4, 4, 16, LANE), BF16),
            pltpu.VMEM((3, 4, 16, LANE), BF16),
            pltpu.VMEM((4, 4, 16, LANE), BF16),
            pltpu.VMEM((2, 3, ROWS, MAIN), BF16),
            pltpu.VMEM((2, 3, 4, 16, MAIN), BF16),
            pltpu.VMEM((2, 3, 16, MAIN), BF16),
            pltpu.VMEM((2, 3, 16, MAIN), BF16),
            pltpu.VMEM((4, 16, WIDE), BF16),
            pltpu.VMEM((3, 16, WIDE), BF16),
            pltpu.VMEM((4, 16, WIDE), BF16),
            pltpu.VMEM((2, 4, 16, MAIN), BF16),
            pltpu.VMEM((2, ROWS, MAIN), BF16),
            pltpu.SemaphoreType.DMA((N_COPIES,)),
            pltpu.SemaphoreType.DMA((N_COPIES,)),
            pltpu.SemaphoreType.DMA((11,)),
            pltpu.SemaphoreType.DMA((6,)),
        ],
        compiler_params=pltpu.CompilerParams(
            collective_id=0, has_side_effects=True, vmem_limit_bytes=60 * 2**20
        ),
        name="train",
    )(
        lhs_table.T, lhs_state[None, :], rhs_table.T, rhs_state[None, :], relations, rel_state[None, :],
        src_index, dst_index, rel_index, neg_index, edge_count,
    )
    lhs, lhs_st, rhs, rhs_st, rel, rel_st = pl.pallas_call(
        hand_on,
        out_shape=out_shape,
        in_specs=[hbm] * 6,
        out_specs=(hbm,) * 6,
        scratch_shapes=[*[pltpu.VMEM(out.shape, out.dtype) for out in out_shape], pltpu.SemaphoreType.DMA((12,))],
        compiler_params=pltpu.CompilerParams(vmem_limit_bytes=60 * 2**20),
        name="hand_on",
    )(*outs)
    return (lhs.T, lhs_st[0], rhs.T, rhs_st[0], rel, rel_st[0])


def solution(mesh):
    return jax.shard_map(
        body,
        mesh=mesh,
        in_specs=(
            P(("grp", "dev"), None),
            P(("grp", "dev")),
            P(("grp", "dev"), None),
            P(("grp", "dev")),
            P("dev", None),
            P("dev"),
            P(("grp", "dev"), None, None),
            P(("grp", "dev"), None, None),
            P(("grp", "dev"), None, None),
            P(("grp", "dev"), None, None),
            P(("grp", "dev"), None),
        ),
        out_specs=(
            P(("grp", "dev"), None),
            P(("grp", "dev")),
            P(("grp", "dev"), None),
            P(("grp", "dev")),
            P("dev", None),
            P("dev"),
        ),
        check_vma=False,
    )
```

```python
import functools

import jax
import jax.numpy as jnp
from jax import lax
from jax.experimental import pallas as pl
from jax.experimental.pallas import tpu as pltpu
from jax.sharding import PartitionSpec as P

LEARN = 0.1
EPSILON = 1e-06
MESH = pl.DeviceIdType.MESH
F32, BF16, I32 = jnp.float32, jnp.bfloat16, jnp.int32

D = 400
HALF = 200
WIDE = 512
OWN = 65
ROWS = 64
MAIN = 384
EP = 128
SLOTS = 512
LANE = 128


def flip(value, k):
    if k == 1:
        return value + 1 - 2 * (value % 2)
    if k == 3:
        return 3 - value
    return (value + 2) % 4


def dot(a, b, ca, cb):
    return lax.dot_general(a, b, (((ca,), (cb,)), ((), ())), preferred_element_type=F32)


def hot(index, first, count):
    rows = lax.broadcasted_iota(I32, (count, index.shape[1]), 0) + first
    return jnp.where(rows == index, 1.0, 0.0).astype(BF16)


def split(value):
    high = value.astype(BF16)
    return high, (value - high.astype(F32)).astype(BF16)


def fold(tail):
    total = tail[0:8]
    for i in range(1, 8):
        total += pltpu.roll(tail[8 * i : 8 * i + 8], 16 * i, 1)
    return total


def unfold(folded, shards):
    flat = folded.reshape(shards * 8, LANE)
    groups = [flat if i == 0 else pltpu.roll(flat, LANE - 16 * i, 1) for i in range(8)]
    return jnp.stack([group.reshape(shards, 8, LANE) for group in groups], axis=1).reshape(shards, ROWS, LANE)


def place_of(kind):
    shard = (kind * 64528) >> 22
    return shard, kind - OWN * shard


def adagrad(rows, state, grad):
    new_state = state + jnp.sum(grad * grad, axis=0, keepdims=True) / D
    moved = rows.astype(F32) - LEARN * grad / (jnp.sqrt(new_state) + EPSILON)
    return moved.astype(BF16), new_state


def kernel(
    lhs_hbm, lst_hbm, rhs_hbm, rst_hbm, rel_hbm, relst_hbm, src_hbm, dst_hbm, kind_hbm, neg_hbm, count_hbm,
    lhs_res, lst_res, rhs_res, rst_res, rel_res, relst_res,
    lhs_ref, lst_ref, rhs_ref, rst_ref, rel_ref, relst_ref, src_ref, dst_ref, kind_ref, neg_ref, count_ref,
    lhs_out, lst_out, rhs_out, rst_out, rel_out, relst_out,
    times_buf, row_sums, table, left, spare, hot_all, hot_spare, hot_mine, hot_mine_spare, kinds, wide, a_buf, rr_buf, q_buf, m_hi, m_lo, edges,
    rhs_send, rst_send, rhs_in, rst_in, part, part_left, l_in, l_y, x_in, y_in, x2_in, y2_in, z_out, z_in, low, stage2x, stage2y,
    send_sem, recv_sem, in_sem, out_sem,
):
    grp, dev = lax.axis_index("grp"), lax.axis_index("dev")
    y, zl = grp // 4, grp % 4
    zh, x, c = dev // 8, (dev // 2) % 4, dev % 2

    def place(x_=None, y_=None, zh_=None, zl_=None, c_=None):
        x_ = x if x_ is None else x_
        y_ = y if y_ is None else y_
        zh_ = zh if zh_ is None else zh_
        zl_ = zl if zl_ is None else zl_
        c_ = c if c_ is None else c_
        return (y_ * 4 + zl_, zh_ * 8 + x_ * 2 + c_)

    sibling = place(c_=1 - c)
    after = (grp, (dev + 1) % 32)
    ks = (2, 1, 3)
    xs = {k: place(x_=flip(x, k)) for k in ks}
    ys = {k: place(y_=flip(y, k)) for k in ks}
    zhs = {k: place(zh_=flip(zh, k)) for k in ks}
    zls = {k: place(zl_=flip(zl, k)) for k in ks}

    barrier = pltpu.get_barrier_semaphore()
    greet = [sibling, *xs.values(), *ys.values(), zhs[1], zhs[3], *zls.values()]
    for other in greet:
        pl.semaphore_signal(barrier, inc=1, device_id=other, device_id_type=MESH)

    loads = [
        pltpu.make_async_copy(src, dst, in_sem.at[i])
        for i, (src, dst) in enumerate(
            (
                (rel_hbm, rel_ref), (kind_hbm, kind_ref), (lhs_hbm, lhs_ref), (src_hbm, src_ref), (rhs_hbm, rhs_ref),
                (dst_hbm, dst_ref), (neg_hbm, neg_ref), (lst_hbm, lst_ref), (rst_hbm, rst_ref), (relst_hbm, relst_ref),
                (count_hbm, count_ref),
            )
        )
    ]
    for copy in loads[:2]:
        copy.start()
    started, stores = [], []

    def give(src, dst):
        copy = pltpu.make_async_copy(src, dst, out_sem.at[len(stores)])
        copy.start()
        stores.append(copy)

    def send(src, dst, target):
        i = len(started)
        copy = pltpu.make_async_remote_copy(
            src_ref=src, dst_ref=dst, send_sem=send_sem.at[i], recv_sem=recv_sem.at[i],
            device_id=target, device_id_type=MESH,
        )
        copy.start()
        started.append(copy)
        return copy

    def arrived(copies):
        for copy in copies:
            copy.wait_recv()

    def rows(value):
        return pl.ds(pl.multiple_of(value * 16, 16), 16)

    def slot(turn):
        return pl.ds(pl.multiple_of((turn * 2 + c) * SLOTS, SLOTS), SLOTS)

    edges[D:WIDE, :] = jnp.zeros((WIDE - D, 4 * SLOTS), BF16)
    wide[...] = jnp.zeros(wide.shape, F32)
    for copy in loads[:2]:
        copy.wait()
    wide[0:OWN, 0:D] = rel_ref[...]
    table[zh, x, c] = wide[0:ROWS, :].astype(BF16)
    last_row = [wide[ROWS:OWN, LANE * i : LANE * i + LANE] for i in range(4)]
    left[zh, x, c] = jnp.concatenate(
        [fold(wide[0:ROWS, MAIN:WIDE]), *last_row, jnp.zeros((4, LANE), F32)], axis=0
    ).astype(BF16)
    kinds[c] = jnp.concatenate([kind_ref[0], jnp.zeros((6, SLOTS), I32)], axis=0)

    pl.semaphore_wait(barrier, len(greet))

    mine, mine_left = table.at[zh, x, c, :, 0:MAIN], left.at[zh, x, c]
    quarter = table.at[zh, x, c, rows(y), 0:MAIN]
    to_zh = {k: [send(quarter, quarter, zhs[k]), send(mine_left, mine_left, zhs[k])] for k in (1, 3)}
    own_x = [send(mine, mine, xs[k]) for k in ks] + [send(mine_left, mine_left, xs[k]) for k in ks]
    kinds_sib = send(kinds.at[c], kinds.at[c], sibling)

    for copy in loads[2:]:
        copy.start()

    both = jnp.concatenate([kind_ref[0, 0:1, :], kind_ref[0, 1:2, :]], axis=1)
    shard_of, row_of = place_of(both)
    spot = jnp.where(row_of < ROWS, ROWS * shard_of + row_of, -1)
    hot_spare[...] = hot(jnp.where(row_of == ROWS, shard_of, -1), 0, 32)

    def fill(i, _):
        hot_all[i // 8, pl.ds(pl.multiple_of((i % 8) * ROWS, ROWS), ROWS), :] = hot(spot, i * ROWS, ROWS)
        return 0

    lax.fori_loop(0, 32, fill, 0)
    for copy in loads[2:]:
        copy.wait()

    def piece_of(k, lo, hi):
        return table.at[flip(zh, k), x, c, rows(y), lo:hi]

    def y_second(k, lo, hi):
        piece = table.at[flip(zh, k), :, c, rows(y), lo:hi]
        return [send(piece, piece, ys[j]) for j in ks]

    def x_second(k, lo, hi):
        piece = table.at[flip(zh, k), x, c, :, lo:hi]
        return [send(piece, piece, xs[j]) for j in ks]

    def spread(piece, targets):
        return [send(piece, piece, targets[j]) for j in ks]

    def left_of(k):
        return left.at[flip(zh, k), x, c]

    def to_sibling(where):
        piece, piece_left = table.at[where, :, c, :, 0:MAIN], left.at[where, :, c]
        return [send(piece, piece, sibling), send(piece_left, piece_left, sibling)]

    def look_up(where, first):
        folded = left[where].astype(F32).reshape(8, 16, LANE)
        table[where, :, :, :, MAIN:WIDE] = unfold(folded[:, 0:8], 8).astype(BF16).reshape(4, 2, ROWS, LANE)
        for shard in range(8):
            for i in range(4):
                spare[where, shard : shard + 1, LANE * i : LANE * i + LANE] = folded[shard, 8 + i : 9 + i]
        got = dot(table[where].reshape(8 * ROWS, WIDE)[:, 0:D], hot_all[where], 0, 0)
        if first:
            rr_buf[...] = got
        else:
            rr_buf[...] += got

    def source_rows(turn, lhs):
        a_buf[...] = dot(lhs, hot(src_ref[0, turn : turn + 1, :], 0, EP), 1, 0)

    cut = 256
    arrived(to_zh[1])
    piece = piece_of(1, 0, cut)
    relay_x = [send(piece, piece, zhs[3])]
    one_a = spread(piece_of(1, 0, MAIN), ys)
    arrived(to_zh[3])
    piece = piece_of(3, cut, MAIN)
    relay_y = [send(piece, piece, zhs[1]), send(left_of(3), left_of(3), zhs[1])]
    three_a = spread(piece_of(3, 0, MAIN), xs)
    one_left = spread(left_of(1), xs)
    three_left = spread(left_of(3), xs)
    arrived(own_x)
    sib_own = to_sibling(zh)
    arrived(one_a)
    one_b = x_second(1, 0, MAIN)
    arrived(three_a)
    three_b = y_second(3, 0, MAIN)
    arrived(relay_x)
    arrived(relay_y)
    piece = piece_of(2, 0, MAIN)
    two = [send(piece, piece, place(x_=flip(x, i), y_=flip(y, j))) for i in ks for j in ks]
    two += spread(piece, xs) + spread(piece, ys) + spread(left_of(2), xs)
    source_rows(0, lhs_ref[...])
    for turn in range(2):
        drawn = hot(neg_ref[0, turn : turn + 1, :], 0, EP)
        times_buf[turn] = jnp.broadcast_to(jnp.sum(drawn.astype(F32), axis=1, keepdims=True), (EP, LANE))
    arrived(sib_own)
    look_up(zh, True)
    arrived(one_left)
    arrived(one_b)
    sib_one = to_sibling(flip(zh, 1))
    arrived(three_left)
    arrived(three_b)
    sib_three = to_sibling(flip(zh, 3))
    arrived(sib_one)
    look_up(flip(zh, 1), False)
    arrived(two)
    sib_two = to_sibling(flip(zh, 2))
    arrived(sib_three)
    look_up(flip(zh, 3), False)
    arrived(sib_two)
    look_up(flip(zh, 2), False)
    rr_buf[...] += dot(spare[...].reshape(32, WIDE)[:, 0:D].astype(BF16), hot_spare[...], 0, 0)

    def front(turn):
        cols = slice(turn * SLOTS, (turn + 1) * SLOTS)
        a_re, a_im = a_buf[0:HALF, :], a_buf[HALF:D, :]
        r_re, r_im = rr_buf[0:HALF, cols], rr_buf[HALF:D, cols]
        q_buf[...] = jnp.concatenate([a_re * r_re - a_im * r_im, a_re * r_im + a_im * r_re], axis=0).astype(BF16)

    def weights(turn, rhs):
        score = dot(rhs, q_buf[...], 0, 0)
        dst = dst_ref[0, turn : turn + 1, :]
        is_dst = lax.broadcasted_iota(I32, (EP, SLOTS), 0) == dst
        times = times_buf[turn, :, 0:1]
        pos = jnp.sum(jnp.where(is_dst, score, 0.0), axis=0, keepdims=True)
        live = jnp.where(
            lax.broadcasted_iota(I32, (1, SLOTS), 1) < count_ref[0:1, turn : turn + 1], 1.0, 0.0
        )
        neg_exp = jnp.exp(score)
        pos_exp = jnp.exp(pos)
        total = pos_exp + jnp.sum(jnp.where(times > 0.0, times * neg_exp, 0.0), axis=0, keepdims=True)
        w_pos = live * (pos_exp / total - 1.0)
        w_neg = (live * neg_exp / total).astype(BF16).astype(F32)
        weight = jnp.where(times > 0.0, times * w_neg, 0.0) + jnp.where(is_dst, w_pos, 0.0)
        high, rest = split(weight)
        m_hi[...] = high
        m_lo[...] = rest

    def rhs_grad():
        q = q_buf[...]
        return dot(q, m_hi[...], 1, 1) + dot(q, m_lo[...], 1, 1)

    def back(turn, rhs):
        dq = dot(rhs, m_hi[...], 1, 0) + dot(rhs, m_lo[...], 1, 0)
        cols = slice(turn * SLOTS, (turn + 1) * SLOTS)
        d_re, d_im = dq[0:HALF, :], dq[HALF:D, :]
        a_re, a_im = a_buf[0:HALF, :], a_buf[HALF:D, :]
        r_re, r_im = rr_buf[0:HALF, cols], rr_buf[HALF:D, cols]
        grad_r = jnp.concatenate([d_re * a_re + d_im * a_im, d_im * a_re - d_re * a_im], axis=0)
        edges[0:D, slot(turn)] = grad_r.astype(BF16)
        copy = send(edges.at[0:D, slot(turn)], edges.at[0:D, slot(turn)], sibling)
        a_buf[...] = jnp.concatenate([d_re * r_re + d_im * r_im, d_im * r_re - d_re * r_im], axis=0)
        return copy

    def lhs_grad(turn):
        src = hot(src_ref[0, turn : turn + 1, :], 0, EP)
        high, rest = split(a_buf[...])
        return dot(high, src, 1, 1) + dot(rest, src, 1, 1)

    front(0)
    weights(0, rhs_ref[...])
    new_rhs, new_rst = adagrad(rhs_ref[...], rst_ref[...], rhs_grad())
    rhs_send[...] = new_rhs
    rst_send[...] = jnp.broadcast_to(new_rst, (8, EP))
    passed = [send(rhs_send, rhs_in, after), send(rst_send, rst_in, after)]
    edges_sib = [back(0, rhs_ref[...])]
    new_lhs, new_lst = adagrad(lhs_ref[...], lst_ref[...], lhs_grad(0))
    lhs_out[...] = new_lhs
    lst_out[...] = new_lst

    source_rows(1, lhs_out[...])
    front(1)

    arrived([kinds_sib])
    for core in range(2):
        for turn in range(2):
            kind = kinds[core, turn : turn + 1, :]
            shard, row = place_of(kind)
            half = shard >> 1
            ours = shard - 2 * half == c
            local = jnp.where(ours & (row < ROWS), ROWS * half + row, -1)
            at = (turn * 2 + core) * SLOTS

            hot_mine_spare[:, at : at + SLOTS] = hot(jnp.where(ours & (row == ROWS), half, -1), 0, 16)

            def fill_mine(i, _, local=local, at=at):
                hot_mine[i // 4, pl.ds(pl.multiple_of((i % 4) * ROWS, ROWS), ROWS), at : at + SLOTS] = hot(
                    local, i * ROWS, ROWS
                )
                return 0

            lax.fori_loop(0, 16, fill_mine, 0)

    arrived(edges_sib)
    early, late = slice(0, 2 * SLOTS), slice(2 * SLOTS, 4 * SLOTS)
    for i in range(4):
        row_sums[i] = dot(hot_mine[i, :, early], edges[:, early], 1, 1)
    row_sums[4, 0:16] = dot(hot_mine_spare[:, early], edges[:, early], 1, 1)

    arrived(passed)
    weights(1, rhs_in[...])
    arrived([back(1, rhs_in[...])])

    last_rows = row_sums[4, 0:16] + dot(hot_mine_spare[:, late], edges[:, late], 1, 1)

    def chunk(i):
        got = row_sums[i] + dot(hot_mine[i, :, late], edges[:, late], 1, 1)
        part[i] = got[:, 0:MAIN].astype(BF16).reshape(4, ROWS, MAIN)
        return got[:, MAIN:WIDE]

    def fold_chunk(i, tails):
        for j in range(4):
            at = 4 * i + j
            spare_rows = [last_rows[at : at + 1, LANE * q : LANE * q + LANE] for q in range(4)]
            part_left[i, j] = jnp.concatenate(
                [fold(tails[ROWS * j : ROWS * j + ROWS]), *spare_rows, jnp.zeros((4, LANE), F32)], axis=0
            ).astype(BF16)

    def x_first(i):
        tails = chunk(i)
        copies = {k: send(part.at[i, flip(x, k)], x_in.at[i, k - 1], xs[k]) for k in ks}
        fold_chunk(i, tails)
        return copies

    def y_first(i):
        tails = chunk(i)
        copies = {k: send(part.at[i, :, rows(flip(y, k))], y_in.at[i - 2, k - 1], ys[k]) for k in ks}
        fold_chunk(i, tails)
        return copies

    first = {0: x_first(0), 2: y_first(2), 1: x_first(1), 3: y_first(3)}
    first_left = {k: send(part_left.at[:, flip(x, k)], l_in.at[k - 1], xs[k]) for k in ks}

    new_rhs, new_rst = adagrad(rhs_in[...], rst_in[0:1, :], rhs_grad())
    rhs_out[...] = new_rhs
    rst_out[...] = new_rst
    new_lhs, new_lst = adagrad(lhs_out[...], lst_out[...], lhs_grad(1))
    lhs_out[...] = new_lhs
    lst_out[...] = new_lst
    for src, dst in ((lhs_out, lhs_res), (lst_out, lst_res), (rhs_out, rhs_res), (rst_out, rst_res)):
        give(src, dst)

    def x_then_y(i):
        arrived(first[i].values())
        total = part[i, x].astype(F32)
        for k in ks:
            total += x_in[i, k - 1].astype(F32)
        stage2y[i] = total.astype(BF16)
        return {k: send(stage2y.at[i, rows(flip(y, k))], y2_in.at[i, k - 1], ys[k]) for k in ks}

    def y_then_x(i):
        arrived(first[i].values())
        total = part[i, :, rows(y)].astype(F32)
        for k in ks:
            total += y_in[i - 2, k - 1].astype(F32)
        stage2x[i - 2] = total.astype(BF16)
        return {k: send(stage2x.at[i - 2, flip(x, k)], x2_in.at[i - 2, k - 1], xs[k]) for k in ks}

    second = {0: x_then_y(0), 2: y_then_x(2), 1: x_then_y(1), 3: y_then_x(3)}

    arrived(first_left.values())
    sum_left = part_left[:, x].astype(F32)
    for k in ks:
        sum_left += l_in[k - 1].astype(F32)
    l_y[y] = sum_left.astype(BF16)
    second_left = [send(l_y.at[y], l_y.at[y], ys[k]) for k in ks]

    for i in (0, 2, 1, 3):
        arrived(second[i].values())
        total = (stage2y[i, rows(y)] if i < 2 else stage2x[i - 2, x]).astype(F32)
        for k in ks:
            total += (y2_in[i, k - 1] if i < 2 else x2_in[i - 2, k - 1]).astype(F32)
        z_out[i, :, 0:MAIN] = total.astype(BF16)
    arrived(second_left)
    all_left = (l_y[0].astype(F32) + l_y[1].astype(F32)) + (l_y[2].astype(F32) + l_y[3].astype(F32))
    z_out[:, :, MAIN:WIDE] = all_left.astype(BF16)

    za = {k: send(z_out.at[flip(zh, k)], z_in.at[k - 1], zhs[k]) for k in ks}
    arrived(za.values())
    over_zh = z_out[zh].astype(F32)
    for k in ks:
        over_zh += z_in[k - 1].astype(F32)
    low[zl] = over_zh.astype(BF16)
    zb = [send(low.at[zl], low.at[zl], zls[k]) for k in ks]
    arrived(zb)
    both_z = (low[0].astype(F32) + low[1].astype(F32)) + (low[2].astype(F32) + low[3].astype(F32))
    own_rows = wide.at[rows(y), 0:MAIN]
    own_rows[...] = both_z[:, 0:MAIN]
    last = [send(own_rows, own_rows, ys[k]) for k in ks]
    wide[0:ROWS, MAIN:WIDE] = unfold(both_z[0:8, MAIN:WIDE].reshape(1, 8, LANE), 1)[0]
    for i in range(4):
        wide[ROWS:OWN, LANE * i : LANE * i + LANE] = both_z[8 + i : 9 + i, MAIN:WIDE]
    arrived(last)

    total = wide[0:OWN, 0:D]
    eye = lax.broadcasted_iota(I32, (OWN, OWN), 0) == lax.broadcasted_iota(I32, (OWN, OWN), 1)
    old = jnp.sum(jnp.where(eye, relst_ref[...], 0.0), axis=1, keepdims=True)
    new = old + jnp.sum(total * total, axis=1, keepdims=True) / D
    rel_out[...] = rel_ref[...] - LEARN * total / (jnp.sqrt(new) + EPSILON)
    relst_out[...] = jnp.sum(jnp.where(eye, new, 0.0), axis=0, keepdims=True)

    give(rel_out, rel_res)
    give(relst_out, relst_res)
    for copy in started:
        copy.wait_send()
    for copy in stores:
        copy.wait()


def hand_on(*refs):
    held, sem = refs[12:18], refs[18]
    loads = [pltpu.make_async_copy(refs[i], held[i], sem.at[i]) for i in range(6)]
    stores = [pltpu.make_async_copy(held[i], refs[6 + i], sem.at[6 + i]) for i in range(6)]
    for copy in loads:
        copy.start()
    for load, store in zip(loads, stores):
        load.wait()
        store.start()
    for copy in stores:
        copy.wait()


N_COPIES = 112


def body(
    lhs_table, lhs_state, rhs_table, rhs_state, relations, rel_state,
    src_index, dst_index, rel_index, neg_index, edge_count,
):
    hbm = pl.BlockSpec(memory_space=pltpu.HBM)
    shape = jax.ShapeDtypeStruct
    out_shape = (
        shape((D, EP), BF16), shape((1, EP), F32), shape((D, EP), BF16), shape((1, EP), F32),
        shape((OWN, D), F32), shape((1, OWN), F32),
    )
    outs = pl.pallas_call(
        kernel,
        out_shape=out_shape,
        in_specs=[hbm] * 11,
        out_specs=(hbm,) * 6,
        scratch_shapes=[
            pltpu.VMEM((D, EP), BF16), pltpu.VMEM((1, EP), F32), pltpu.VMEM((D, EP), BF16), pltpu.VMEM((1, EP), F32),
            pltpu.VMEM((OWN, D), F32), pltpu.VMEM((1, OWN), F32),
            *[pltpu.VMEM((1, 2, SLOTS), I32) for _ in range(4)],
            pltpu.VMEM((1, 2), I32),
            *[pltpu.VMEM(out.shape, out.dtype) for out in out_shape],
            pltpu.VMEM((2, EP, LANE), F32),
            pltpu.VMEM((5, 4 * ROWS, WIDE), F32),
            pltpu.VMEM((4, 4, 2, ROWS, WIDE), BF16),
            pltpu.VMEM((4, 4, 2, 16, LANE), BF16),
            pltpu.VMEM((4, 8, WIDE), F32),
            pltpu.VMEM((4, 8 * ROWS, 2 * SLOTS), BF16),
            pltpu.VMEM((32, 2 * SLOTS), BF16),
            pltpu.VMEM((4, 4 * ROWS, 4 * SLOTS), BF16),
            pltpu.VMEM((16, 4 * SLOTS), BF16),
            pltpu.VMEM((2, 8, SLOTS), I32),
            pltpu.VMEM((72, WIDE), F32),
            pltpu.VMEM((D, SLOTS), F32),
            pltpu.VMEM((D, 2 * SLOTS), F32),
            pltpu.VMEM((D, SLOTS), BF16),
            pltpu.VMEM((EP, SLOTS), BF16),
            pltpu.VMEM((EP, SLOTS), BF16),
            pltpu.VMEM((WIDE, 4 * SLOTS), BF16),
            pltpu.VMEM((D, EP), BF16),
            pltpu.VMEM((8, EP), F32),
            pltpu.VMEM((D, EP), BF16),
            pltpu.VMEM((8, EP), F32),
            pltpu.VMEM((4, 4, ROWS, MAIN), BF16),
            pltpu.VMEM((4, 4, 16, LANE), BF16),
            pltpu.VMEM((3, 4, 16, LANE), BF16),
            pltpu.VMEM((4, 4, 16, LANE), BF16),
            pltpu.VMEM((2, 3, ROWS, MAIN), BF16),
            pltpu.VMEM((2, 3, 4, 16, MAIN), BF16),
            pltpu.VMEM((2, 3, 16, MAIN), BF16),
            pltpu.VMEM((2, 3, 16, MAIN), BF16),
            pltpu.VMEM((4, 16, WIDE), BF16),
            pltpu.VMEM((3, 16, WIDE), BF16),
            pltpu.VMEM((4, 16, WIDE), BF16),
            pltpu.VMEM((2, 4, 16, MAIN), BF16),
            pltpu.VMEM((2, ROWS, MAIN), BF16),
            pltpu.SemaphoreType.DMA((N_COPIES,)),
            pltpu.SemaphoreType.DMA((N_COPIES,)),
            pltpu.SemaphoreType.DMA((11,)),
            pltpu.SemaphoreType.DMA((6,)),
        ],
        compiler_params=pltpu.CompilerParams(
            collective_id=0, has_side_effects=True, vmem_limit_bytes=60 * 2**20
        ),
        name="train",
    )(
        lhs_table.T, lhs_state[None, :], rhs_table.T, rhs_state[None, :], relations, rel_state[None, :],
        src_index, dst_index, rel_index, neg_index, edge_count,
    )
    lhs, lhs_st, rhs, rhs_st, rel, rel_st = pl.pallas_call(
        hand_on,
        out_shape=out_shape,
        in_specs=[hbm] * 6,
        out_specs=(hbm,) * 6,
        scratch_shapes=[*[pltpu.VMEM(out.shape, out.dtype) for out in out_shape], pltpu.SemaphoreType.DMA((12,))],
        compiler_params=pltpu.CompilerParams(vmem_limit_bytes=60 * 2**20),
        name="hand_on",
    )(*outs)
    return (lhs.T, lhs_st[0], rhs.T, rhs_st[0], rel, rel_st[0])


def solution(mesh):
    return jax.shard_map(
        body,
        mesh=mesh,
        in_specs=(
            P(("grp", "dev"), None),
            P(("grp", "dev")),
            P(("grp", "dev"), None),
            P(("grp", "dev")),
            P("dev", None),
            P("dev"),
            P(("grp", "dev"), None, None),
            P(("grp", "dev"), None, None),
            P(("grp", "dev"), None, None),
            P(("grp", "dev"), None, None),
            P(("grp", "dev"), None),
        ),
        out_specs=(
            P(("grp", "dev"), None),
            P(("grp", "dev")),
            P(("grp", "dev"), None),
            P(("grp", "dev")),
            P("dev", None),
            P("dev"),
        ),
        check_vma=False,
    )
```

```python
import functools

import jax
import jax.numpy as jnp
from jax import lax
from jax.experimental import pallas as pl
from jax.experimental.pallas import tpu as pltpu
from jax.sharding import PartitionSpec as P

LEARN = 0.1
EPSILON = 1e-06
MESH = pl.DeviceIdType.MESH
F32, BF16, I32 = jnp.float32, jnp.bfloat16, jnp.int32

D = 400
HALF = 200
WIDE = 512
OWN = 65
ROWS = 64
MAIN = 384
EP = 128
SLOTS = 512
LANE = 128


def flip(value, k):
    if k == 1:
        return value + 1 - 2 * (value % 2)
    if k == 3:
        return 3 - value
    return (value + 2) % 4


def dot(a, b, ca, cb):
    return lax.dot_general(a, b, (((ca,), (cb,)), ((), ())), preferred_element_type=F32)


def hot(index, first, count):
    rows = lax.broadcasted_iota(I32, (count, index.shape[1]), 0) + first
    return jnp.where(rows == index, 1.0, 0.0).astype(BF16)


def split(value):
    high = value.astype(BF16)
    return high, (value - high.astype(F32)).astype(BF16)


def fold(tail):
    total = tail[0:8]
    for i in range(1, 8):
        total += pltpu.roll(tail[8 * i : 8 * i + 8], 16 * i, 1)
    return total


def unfold(folded, shards):
    flat = folded.reshape(shards * 8, LANE)
    groups = [flat if i == 0 else pltpu.roll(flat, LANE - 16 * i, 1) for i in range(8)]
    return jnp.stack([group.reshape(shards, 8, LANE) for group in groups], axis=1).reshape(shards, ROWS, LANE)


def place_of(kind):
    shard = (kind * 64528) >> 22
    return shard, kind - OWN * shard


def adagrad(rows, state, grad):
    new_state = state + jnp.sum(grad * grad, axis=0, keepdims=True) / D
    moved = rows.astype(F32) - LEARN * grad / (jnp.sqrt(new_state) + EPSILON)
    return moved.astype(BF16), new_state


def kernel(
    lhs_hbm, lst_hbm, rhs_hbm, rst_hbm, rel_hbm, relst_hbm, src_hbm, dst_hbm, kind_hbm, neg_hbm, count_hbm,
    lhs_res, lst_res, rhs_res, rst_res, rel_res, relst_res,
    lhs_ref, lst_ref, rhs_ref, rst_ref, rel_ref, relst_ref, src_ref, dst_ref, kind_ref, neg_ref, count_ref,
    lhs_out, lst_out, rhs_out, rst_out, rel_out, relst_out,
    times_buf, row_sums, table, left, spare, hot_all, hot_spare, hot_mine, hot_mine_spare, kinds, wide, a_buf, rr_buf, q_buf, m_hi, m_lo, edges,
    rhs_send, rst_send, rhs_in, rst_in, part, part_left, l_in, l_y, x_in, y_in, x2_in, y2_in, z_out, z_in, low, whole, stage2x, stage2y,
    send_sem, recv_sem, in_sem, out_sem,
):
    grp, dev = lax.axis_index("grp"), lax.axis_index("dev")
    y, zl = grp // 4, grp % 4
    zh, x, c = dev // 8, (dev // 2) % 4, dev % 2

    def place(x_=None, y_=None, zh_=None, zl_=None, c_=None):
        x_ = x if x_ is None else x_
        y_ = y if y_ is None else y_
        zh_ = zh if zh_ is None else zh_
        zl_ = zl if zl_ is None else zl_
        c_ = c if c_ is None else c_
        return (y_ * 4 + zl_, zh_ * 8 + x_ * 2 + c_)

    sibling = place(c_=1 - c)
    after = (grp, (dev + 1) % 32)
    ks = (2, 1, 3)
    xs = {k: place(x_=flip(x, k)) for k in ks}
    ys = {k: place(y_=flip(y, k)) for k in ks}
    zhs = {k: place(zh_=flip(zh, k)) for k in ks}
    zls = {k: place(zl_=flip(zl, k)) for k in ks}

    loads = [
        pltpu.make_async_copy(src, dst, in_sem.at[i])
        for i, (src, dst) in enumerate(
            (
                (rel_hbm, rel_ref), (kind_hbm, kind_ref), (lhs_hbm, lhs_ref), (src_hbm, src_ref), (rhs_hbm, rhs_ref),
                (dst_hbm, dst_ref), (neg_hbm, neg_ref), (lst_hbm, lst_ref), (rst_hbm, rst_ref), (relst_hbm, relst_ref),
                (count_hbm, count_ref),
            )
        )
    ]
    for copy in loads[:2]:
        copy.start()
    barrier = pltpu.get_barrier_semaphore()
    greet = [sibling, *xs.values(), *ys.values(), zhs[1], zhs[3], *zls.values()]
    for other in greet:
        pl.semaphore_signal(barrier, inc=1, device_id=other, device_id_type=MESH)

    started, stores = [], []

    def give(src, dst):
        copy = pltpu.make_async_copy(src, dst, out_sem.at[len(stores)])
        copy.start()
        stores.append(copy)

    def send(src, dst, target):
        i = len(started)
        copy = pltpu.make_async_remote_copy(
            src_ref=src, dst_ref=dst, send_sem=send_sem.at[i], recv_sem=recv_sem.at[i],
            device_id=target, device_id_type=MESH,
        )
        copy.start()
        started.append(copy)
        return copy

    def arrived(copies):
        for copy in copies:
            copy.wait_recv()

    def rows(value):
        return pl.ds(pl.multiple_of(value * 16, 16), 16)

    def slot(turn):
        return pl.ds(pl.multiple_of((turn * 2 + c) * SLOTS, SLOTS), SLOTS)

    edges[D:WIDE, :] = jnp.zeros((WIDE - D, 4 * SLOTS), BF16)
    wide[...] = jnp.zeros(wide.shape, F32)
    loads[0].wait()
    wide[0:OWN, 0:D] = rel_ref[...]
    table[zh, x, c] = wide[0:ROWS, :].astype(BF16)
    last_row = [wide[ROWS:OWN, LANE * i : LANE * i + LANE] for i in range(4)]
    left[zh, x, c] = jnp.concatenate(
        [fold(wide[0:ROWS, MAIN:WIDE]), *last_row, jnp.zeros((4, LANE), F32)], axis=0
    ).astype(BF16)

    pl.semaphore_wait(barrier, len(greet))

    mine, mine_left = table.at[zh, x, c, :, 0:MAIN], left.at[zh, x, c]
    quarter = table.at[zh, x, c, rows(y), 0:MAIN]
    to_zh = {k: [send(quarter, quarter, zhs[k]), send(mine_left, mine_left, zhs[k])] for k in (1, 3)}
    own_x = [send(mine, mine, xs[k]) for k in ks] + [send(mine_left, mine_left, xs[k]) for k in ks]
    loads[1].wait()
    kinds[c] = jnp.concatenate([kind_ref[0], jnp.zeros((6, SLOTS), I32)], axis=0)
    kinds_sib = send(kinds.at[c], kinds.at[c], sibling)

    for copy in loads[2:]:
        copy.start()

    both = jnp.concatenate([kind_ref[0, 0:1, :], kind_ref[0, 1:2, :]], axis=1)
    shard_of, row_of = place_of(both)
    spot = jnp.where(row_of < ROWS, ROWS * shard_of + row_of, -1)
    hot_spare[...] = hot(jnp.where(row_of == ROWS, shard_of, -1), 0, 32)

    def fill(i, _):
        hot_all[i // 8, pl.ds(pl.multiple_of((i % 8) * ROWS, ROWS), ROWS), :] = hot(spot, i * ROWS, ROWS)
        return 0

    lax.fori_loop(0, 32, fill, 0)
    for copy in loads[2:]:
        copy.wait()

    def piece_of(k, lo, hi):
        return table.at[flip(zh, k), x, c, rows(y), lo:hi]

    def y_second(k, lo, hi):
        piece = table.at[flip(zh, k), :, c, rows(y), lo:hi]
        return [send(piece, piece, ys[j]) for j in ks]

    def x_second(k, lo, hi):
        piece = table.at[flip(zh, k), x, c, :, lo:hi]
        return [send(piece, piece, xs[j]) for j in ks]

    def spread(piece, targets):
        return [send(piece, piece, targets[j]) for j in ks]

    def left_of(k):
        return left.at[flip(zh, k), x, c]

    def to_sibling(where):
        piece, piece_left = table.at[where, :, c, :, 0:MAIN], left.at[where, :, c]
        return [send(piece, piece, sibling), send(piece_left, piece_left, sibling)]

    def look_up(where, first):
        folded = left[where].astype(F32).reshape(8, 16, LANE)
        table[where, :, :, :, MAIN:WIDE] = unfold(folded[:, 0:8], 8).astype(BF16).reshape(4, 2, ROWS, LANE)
        for shard in range(8):
            for i in range(4):
                spare[where, shard : shard + 1, LANE * i : LANE * i + LANE] = folded[shard, 8 + i : 9 + i]
        got = dot(table[where].reshape(8 * ROWS, WIDE)[:, 0:D], hot_all[where], 0, 0)
        if first:
            rr_buf[...] = got
        else:
            rr_buf[...] += got

    def source_rows(turn, lhs):
        a_buf[...] = dot(lhs, hot(src_ref[0, turn : turn + 1, :], 0, EP), 1, 0)

    cut = 256
    arrived(to_zh[1])
    piece = piece_of(1, 0, cut)
    relay_x = [send(piece, piece, zhs[3])]
    one_a = spread(piece_of(1, 0, MAIN), ys)
    arrived(to_zh[3])
    piece = piece_of(3, cut, MAIN)
    relay_y = [send(piece, piece, zhs[1]), send(left_of(3), left_of(3), zhs[1])]
    three_a = spread(piece_of(3, 0, MAIN), xs)
    one_left = spread(left_of(1), xs)
    three_left = spread(left_of(3), xs)
    arrived(own_x)
    sib_own = to_sibling(zh)
    arrived(one_a)
    one_b = x_second(1, 0, MAIN)
    arrived(three_a)
    three_b = y_second(3, 0, MAIN)
    arrived(relay_x)
    arrived(relay_y)
    piece = piece_of(2, 0, MAIN)
    two = [send(piece, piece, place(x_=flip(x, i), y_=flip(y, j))) for i in ks for j in ks]
    two += spread(piece, xs) + spread(piece, ys) + spread(left_of(2), xs)
    source_rows(0, lhs_ref[...])
    for turn in range(2):
        drawn = hot(neg_ref[0, turn : turn + 1, :], 0, EP)
        times_buf[turn] = jnp.broadcast_to(jnp.sum(drawn.astype(F32), axis=1, keepdims=True), (EP, LANE))
    arrived(sib_own)
    look_up(zh, True)
    arrived(one_left)
    arrived(one_b)
    sib_one = to_sibling(flip(zh, 1))
    arrived(three_left)
    arrived(three_b)
    sib_three = to_sibling(flip(zh, 3))
    arrived(sib_one)
    look_up(flip(zh, 1), False)
    arrived(two)
    sib_two = to_sibling(flip(zh, 2))
    arrived(sib_three)
    look_up(flip(zh, 3), False)
    arrived(sib_two)
    look_up(flip(zh, 2), False)
    rr_buf[...] += dot(spare[...].reshape(32, WIDE)[:, 0:D].astype(BF16), hot_spare[...], 0, 0)

    def front(turn):
        cols = slice(turn * SLOTS, (turn + 1) * SLOTS)
        a_re, a_im = a_buf[0:HALF, :], a_buf[HALF:D, :]
        r_re, r_im = rr_buf[0:HALF, cols], rr_buf[HALF:D, cols]
        q_buf[...] = jnp.concatenate([a_re * r_re - a_im * r_im, a_re * r_im + a_im * r_re], axis=0).astype(BF16)

    def weights(turn, rhs):
        score = dot(rhs, q_buf[...], 0, 0)
        dst = dst_ref[0, turn : turn + 1, :]
        is_dst = lax.broadcasted_iota(I32, (EP, SLOTS), 0) == dst
        times = times_buf[turn, :, 0:1]
        pos = jnp.sum(jnp.where(is_dst, score, 0.0), axis=0, keepdims=True)
        live = jnp.where(
            lax.broadcasted_iota(I32, (1, SLOTS), 1) < count_ref[0:1, turn : turn + 1], 1.0, 0.0
        )
        neg_exp = jnp.exp(score)
        pos_exp = jnp.exp(pos)
        total = pos_exp + jnp.sum(jnp.where(times > 0.0, times * neg_exp, 0.0), axis=0, keepdims=True)
        w_pos = live * (pos_exp / total - 1.0)
        w_neg = (live * neg_exp / total).astype(BF16).astype(F32)
        weight = jnp.where(times > 0.0, times * w_neg, 0.0) + jnp.where(is_dst, w_pos, 0.0)
        high, rest = split(weight)
        m_hi[...] = high
        m_lo[...] = rest

    def rhs_grad():
        q = q_buf[...]
        return dot(q, m_hi[...], 1, 1) + dot(q, m_lo[...], 1, 1)

    def back(turn, rhs):
        dq = dot(rhs, m_hi[...], 1, 0) + dot(rhs, m_lo[...], 1, 0)
        cols = slice(turn * SLOTS, (turn + 1) * SLOTS)
        d_re, d_im = dq[0:HALF, :], dq[HALF:D, :]
        a_re, a_im = a_buf[0:HALF, :], a_buf[HALF:D, :]
        r_re, r_im = rr_buf[0:HALF, cols], rr_buf[HALF:D, cols]
        grad_r = jnp.concatenate([d_re * a_re + d_im * a_im, d_im * a_re - d_re * a_im], axis=0)
        edges[0:D, slot(turn)] = grad_r.astype(BF16)
        copy = send(edges.at[0:D, slot(turn)], edges.at[0:D, slot(turn)], sibling)
        a_buf[...] = jnp.concatenate([d_re * r_re + d_im * r_im, d_im * r_re - d_re * r_im], axis=0)
        return copy

    def lhs_grad(turn):
        src = hot(src_ref[0, turn : turn + 1, :], 0, EP)
        high, rest = split(a_buf[...])
        return dot(high, src, 1, 1) + dot(rest, src, 1, 1)

    front(0)
    weights(0, rhs_ref[...])
    new_rhs, new_rst = adagrad(rhs_ref[...], rst_ref[...], rhs_grad())
    rhs_send[...] = new_rhs
    rst_send[...] = jnp.broadcast_to(new_rst, (8, EP))
    passed = [send(rhs_send, rhs_in, after), send(rst_send, rst_in, after)]
    edges_sib = [back(0, rhs_ref[...])]
    new_lhs, new_lst = adagrad(lhs_ref[...], lst_ref[...], lhs_grad(0))
    lhs_out[...] = new_lhs
    lst_out[...] = new_lst

    source_rows(1, lhs_out[...])
    front(1)

    arrived([kinds_sib])
    for core in range(2):
        for turn in range(2):
            kind = kinds[core, turn : turn + 1, :]
            shard, row = place_of(kind)
            half = shard >> 1
            ours = shard - 2 * half == c
            local = jnp.where(ours & (row < ROWS), ROWS * half + row, -1)
            at = (turn * 2 + core) * SLOTS

            hot_mine_spare[:, at : at + SLOTS] = hot(jnp.where(ours & (row == ROWS), half, -1), 0, 16)

            def fill_mine(i, _, local=local, at=at):
                hot_mine[i // 4, pl.ds(pl.multiple_of((i % 4) * ROWS, ROWS), ROWS), at : at + SLOTS] = hot(
                    local, i * ROWS, ROWS
                )
                return 0

            lax.fori_loop(0, 16, fill_mine, 0)

    arrived(edges_sib)
    early, late = slice(0, 2 * SLOTS), slice(2 * SLOTS, 4 * SLOTS)
    for i in range(4):
        row_sums[i] = dot(hot_mine[i, :, early], edges[:, early], 1, 1)
    row_sums[4, 0:16] = dot(hot_mine_spare[:, early], edges[:, early], 1, 1)

    arrived(passed)
    weights(1, rhs_in[...])
    arrived([back(1, rhs_in[...])])

    last_rows = row_sums[4, 0:16] + dot(hot_mine_spare[:, late], edges[:, late], 1, 1)

    def chunk(i):
        got = row_sums[i] + dot(hot_mine[i, :, late], edges[:, late], 1, 1)
        part[i] = got[:, 0:MAIN].astype(BF16).reshape(4, ROWS, MAIN)
        return got[:, MAIN:WIDE]

    def fold_chunk(i, tails):
        for j in range(4):
            at = 4 * i + j
            spare_rows = [last_rows[at : at + 1, LANE * q : LANE * q + LANE] for q in range(4)]
            part_left[i, j] = jnp.concatenate(
                [fold(tails[ROWS * j : ROWS * j + ROWS]), *spare_rows, jnp.zeros((4, LANE), F32)], axis=0
            ).astype(BF16)

    def x_first(i):
        tails = chunk(i)
        copies = {k: send(part.at[i, flip(x, k)], x_in.at[i, k - 1], xs[k]) for k in ks}
        fold_chunk(i, tails)
        return copies

    def y_first(i):
        tails = chunk(i)
        copies = {k: send(part.at[i, :, rows(flip(y, k))], y_in.at[i - 2, k - 1], ys[k]) for k in ks}
        fold_chunk(i, tails)
        return copies

    first = {0: x_first(0), 2: y_first(2), 1: x_first(1), 3: y_first(3)}
    first_left = {k: send(part_left.at[:, flip(x, k)], l_in.at[k - 1], xs[k]) for k in ks}

    new_rhs, new_rst = adagrad(rhs_in[...], rst_in[0:1, :], rhs_grad())
    rhs_out[...] = new_rhs
    rst_out[...] = new_rst
    new_lhs, new_lst = adagrad(lhs_out[...], lst_out[...], lhs_grad(1))
    lhs_out[...] = new_lhs
    lst_out[...] = new_lst
    for src, dst in ((lhs_out, lhs_res), (lst_out, lst_res), (rhs_out, rhs_res), (rst_out, rst_res)):
        give(src, dst)

    def x_then_y(i):
        arrived(first[i].values())
        total = part[i, x].astype(F32)
        for k in ks:
            total += x_in[i, k - 1].astype(F32)
        stage2y[i] = total.astype(BF16)
        return {k: send(stage2y.at[i, rows(flip(y, k))], y2_in.at[i, k - 1], ys[k]) for k in ks}

    def y_then_x(i):
        arrived(first[i].values())
        total = part[i, :, rows(y)].astype(F32)
        for k in ks:
            total += y_in[i - 2, k - 1].astype(F32)
        stage2x[i - 2] = total.astype(BF16)
        return {k: send(stage2x.at[i - 2, flip(x, k)], x2_in.at[i - 2, k - 1], xs[k]) for k in ks}

    second = {0: x_then_y(0), 2: y_then_x(2), 1: x_then_y(1), 3: y_then_x(3)}

    arrived(first_left.values())
    sum_left = part_left[:, x].astype(F32)
    for k in ks:
        sum_left += l_in[k - 1].astype(F32)
    l_y[y] = sum_left.astype(BF16)
    second_left = [send(l_y.at[y], l_y.at[y], ys[k]) for k in ks]

    for i in (0, 2, 1, 3):
        arrived(second[i].values())
        total = (stage2y[i, rows(y)] if i < 2 else stage2x[i - 2, x]).astype(F32)
        for k in ks:
            total += (y2_in[i, k - 1] if i < 2 else x2_in[i - 2, k - 1]).astype(F32)
        z_out[i, :, 0:MAIN] = total.astype(BF16)
    arrived(second_left)
    all_left = (l_y[0].astype(F32) + l_y[1].astype(F32)) + (l_y[2].astype(F32) + l_y[3].astype(F32))
    z_out[:, :, MAIN:WIDE] = all_left.astype(BF16)

    za = {k: send(z_out.at[flip(zh, k)], z_in.at[k - 1], zhs[k]) for k in ks}
    arrived(za.values())
    over_zh = z_out[zh].astype(F32)
    for k in ks:
        over_zh += z_in[k - 1].astype(F32)
    low[zl] = over_zh.astype(BF16)
    zb = [send(low.at[zl], low.at[zl], zls[k]) for k in ks]
    arrived(zb)
    both_z = (low[0].astype(F32) + low[1].astype(F32)) + (low[2].astype(F32) + low[3].astype(F32))
    own_rows = whole.at[rows(y)]
    own_rows[...] = both_z[:, 0:MAIN].astype(BF16)
    last = [send(own_rows, own_rows, ys[k]) for k in ks]
    wide[0:ROWS, MAIN:WIDE] = unfold(both_z[0:8, MAIN:WIDE].reshape(1, 8, LANE), 1)[0]
    for i in range(4):
        wide[ROWS:OWN, LANE * i : LANE * i + LANE] = both_z[8 + i : 9 + i, MAIN:WIDE]
    arrived(last)
    wide[0:ROWS, 0:MAIN] = whole[...].astype(F32)

    total = wide[0:OWN, 0:D]
    eye = lax.broadcasted_iota(I32, (OWN, OWN), 0) == lax.broadcasted_iota(I32, (OWN, OWN), 1)
    old = jnp.sum(jnp.where(eye, relst_ref[...], 0.0), axis=1, keepdims=True)
    new = old + jnp.sum(total * total, axis=1, keepdims=True) / D
    rel_out[...] = rel_ref[...] - LEARN * total / (jnp.sqrt(new) + EPSILON)
    relst_out[...] = jnp.sum(jnp.where(eye, new, 0.0), axis=0, keepdims=True)

    give(rel_out, rel_res)
    give(relst_out, relst_res)
    for copy in started:
        copy.wait_send()
    for copy in stores:
        copy.wait()


def hand_on(*refs):
    held, sem = refs[12:18], refs[18]
    loads = [pltpu.make_async_copy(refs[i], held[i], sem.at[i]) for i in range(6)]
    stores = [pltpu.make_async_copy(held[i], refs[6 + i], sem.at[6 + i]) for i in range(6)]
    for copy in loads:
        copy.start()
    for load, store in zip(loads, stores):
        load.wait()
        store.start()
    for copy in stores:
        copy.wait()


N_COPIES = 112


def body(
    lhs_table, lhs_state, rhs_table, rhs_state, relations, rel_state,
    src_index, dst_index, rel_index, neg_index, edge_count,
):
    hbm = pl.BlockSpec(memory_space=pltpu.HBM)
    shape = jax.ShapeDtypeStruct
    out_shape = (
        shape((D, EP), BF16), shape((1, EP), F32), shape((D, EP), BF16), shape((1, EP), F32),
        shape((OWN, D), F32), shape((1, OWN), F32),
    )
    outs = pl.pallas_call(
        kernel,
        out_shape=out_shape,
        in_specs=[hbm] * 11,
        out_specs=(hbm,) * 6,
        scratch_shapes=[
            pltpu.VMEM((D, EP), BF16), pltpu.VMEM((1, EP), F32), pltpu.VMEM((D, EP), BF16), pltpu.VMEM((1, EP), F32),
            pltpu.VMEM((OWN, D), F32), pltpu.VMEM((1, OWN), F32),
            *[pltpu.VMEM((1, 2, SLOTS), I32) for _ in range(4)],
            pltpu.VMEM((1, 2), I32),
            *[pltpu.VMEM(out.shape, out.dtype) for out in out_shape],
            pltpu.VMEM((2, EP, LANE), F32),
            pltpu.VMEM((5, 4 * ROWS, WIDE), F32),
            pltpu.VMEM((4, 4, 2, ROWS, WIDE), BF16),
            pltpu.VMEM((4, 4, 2, 16, LANE), BF16),
            pltpu.VMEM((4, 8, WIDE), F32),
            pltpu.VMEM((4, 8 * ROWS, 2 * SLOTS), BF16),
            pltpu.VMEM((32, 2 * SLOTS), BF16),
            pltpu.VMEM((4, 4 * ROWS, 4 * SLOTS), BF16),
            pltpu.VMEM((16, 4 * SLOTS), BF16),
            pltpu.VMEM((2, 8, SLOTS), I32),
            pltpu.VMEM((72, WIDE), F32),
            pltpu.VMEM((D, SLOTS), F32),
            pltpu.VMEM((D, 2 * SLOTS), F32),
            pltpu.VMEM((D, SLOTS), BF16),
            pltpu.VMEM((EP, SLOTS), BF16),
            pltpu.VMEM((EP, SLOTS), BF16),
            pltpu.VMEM((WIDE, 4 * SLOTS), BF16),
            pltpu.VMEM((D, EP), BF16),
            pltpu.VMEM((8, EP), F32),
            pltpu.VMEM((D, EP), BF16),
            pltpu.VMEM((8, EP), F32),
            pltpu.VMEM((4, 4, ROWS, MAIN), BF16),
            pltpu.VMEM((4, 4, 16, LANE), BF16),
            pltpu.VMEM((3, 4, 16, LANE), BF16),
            pltpu.VMEM((4, 4, 16, LANE), BF16),
            pltpu.VMEM((2, 3, ROWS, MAIN), BF16),
            pltpu.VMEM((2, 3, 4, 16, MAIN), BF16),
            pltpu.VMEM((2, 3, 16, MAIN), BF16),
            pltpu.VMEM((2, 3, 16, MAIN), BF16),
            pltpu.VMEM((4, 16, WIDE), BF16),
            pltpu.VMEM((3, 16, WIDE), BF16),
            pltpu.VMEM((4, 16, WIDE), BF16),
            pltpu.VMEM((ROWS, MAIN), BF16),
            pltpu.VMEM((2, 4, 16, MAIN), BF16),
            pltpu.VMEM((2, ROWS, MAIN), BF16),
            pltpu.SemaphoreType.DMA((N_COPIES,)),
            pltpu.SemaphoreType.DMA((N_COPIES,)),
            pltpu.SemaphoreType.DMA((11,)),
            pltpu.SemaphoreType.DMA((6,)),
        ],
        compiler_params=pltpu.CompilerParams(
            collective_id=0, has_side_effects=True, vmem_limit_bytes=60 * 2**20
        ),
        name="train",
    )(
        lhs_table.T, lhs_state[None, :], rhs_table.T, rhs_state[None, :], relations, rel_state[None, :],
        src_index, dst_index, rel_index, neg_index, edge_count,
    )
    lhs, lhs_st, rhs, rhs_st, rel, rel_st = pl.pallas_call(
        hand_on,
        out_shape=out_shape,
        in_specs=[hbm] * 6,
        out_specs=(hbm,) * 6,
        scratch_shapes=[*[pltpu.VMEM(out.shape, out.dtype) for out in out_shape], pltpu.SemaphoreType.DMA((12,))],
        compiler_params=pltpu.CompilerParams(vmem_limit_bytes=60 * 2**20),
        name="hand_on",
    )(*outs)
    return (lhs.T, lhs_st[0], rhs.T, rhs_st[0], rel, rel_st[0])


def solution(mesh):
    return jax.shard_map(
        body,
        mesh=mesh,
        in_specs=(
            P(("grp", "dev"), None),
            P(("grp", "dev")),
            P(("grp", "dev"), None),
            P(("grp", "dev")),
            P("dev", None),
            P("dev"),
            P(("grp", "dev"), None, None),
            P(("grp", "dev"), None, None),
            P(("grp", "dev"), None, None),
            P(("grp", "dev"), None, None),
            P(("grp", "dev"), None),
        ),
        out_specs=(
            P(("grp", "dev"), None),
            P(("grp", "dev")),
            P(("grp", "dev"), None),
            P(("grp", "dev")),
            P("dev", None),
            P("dev"),
        ),
        check_vma=False,
    )
```
